32 devices in a mesh: dp: 2 (over x), expert: 16 (over z, y, core).
Axes of the slice: x: 2, y: 2, z: 4, core: 2. Of those that a mesh axis runs over, the one named last changes fastest.
Arguments:
- tokens: bfloat16 [8192, 1536], P(('dp', 'expert')), may hold values from -6 to 6
- cotangent: bfloat16 [8192, 1536], P(('dp', 'expert')), may hold values from -6 to 6
- lengths: int32 [32], P(('dp', 'expert')), may hold values from 64 to 256, as said below
- routes: int32 [8192, 8], P(('dp', 'expert')), may hold values from 0 to 15, all different within a row; in each aligned block of 256 rows (0 to 255, 256 to 511, ...) at most 160 rows name the same one
- norm1_gain: bfloat16 [1536], P('expert'), may hold values from 0.5 to 1.5
- w_query: bfloat16 [1536, 1536], P('expert'), may hold values from -0.15625 to 0.15625
- w_kv: bfloat16 [1536, 1024], P('expert'), may hold values from -0.15625 to 0.15625
- w_out: bfloat16 [1536, 1536], P('expert'), may hold values from -0.625 to 0.625
- norm2_gain: bfloat16 [1536], P('expert'), may hold values from 0.5 to 1.5
- w_router: bfloat16 [1536, 16], P('expert'), may hold values from -0.078125 to 0.078125
- expert_gate: bfloat16 [16, 1536, 512], P('expert'), may hold values from -0.15625 to 0.15625
- expert_up: bfloat16 [16, 1536, 512], P('expert'), may hold values from -0.15625 to 0.15625
- expert_down: bfloat16 [16, 512, 1536], P('expert'), may hold values from -1 to 1
Outputs:
- output: bfloat16 [8192, 1536], P(('dp', 'expert'))
- input_grad: bfloat16 [8192, 1536], P(('dp', 'expert'))
- grad_norm1_gain: float32 [1536], P('expert')
- grad_w_query: float32 [1536, 1536], P('expert')
- grad_w_kv: float32 [1536, 1024], P('expert')
- grad_w_out: float32 [1536, 1536], P('expert')
- grad_norm2_gain: float32 [1536], P('expert')
- grad_w_router: float32 [1536, 16], P('expert')
- grad_expert_gate: float32 [16, 1536, 512], P('expert')
- grad_expert_up: float32 [16, 1536, 512], P('expert')
- grad_expert_down: float32 [16, 512, 1536], P('expert')
The draws below stay inside these ranges and needn't reach their ends.
Inputs may be any that keep to these rules, and one draw needn't show every extreme that they name: `routes`: each row names 8 different experts; among the rows of one device no expert is named more than 160 times. `lengths`: one sequence a device, holding that device's 256 rows of tokens; slots at or past its length are padding.
All inputs are finite; a program needn't handle non-finite values.
Results may differ from the reference program's by a relative error of at most 0.024.
Values may be sent and summed in bfloat16 or wider, within the bound.
A program may use at most 192 MiB of HBM per device.

```python
import math
import jax
import jax.numpy as jnp
import numpy as np
from jax import lax

D = 1536
H = 24
KVH = 8
HD = 64
FF = 512
TOP = 8
TOK_DEV = 256
EXPERTS = 16
SEQS = 32
TOKENS = 8192
CAP = 160


def draw_lengths(key, part):
    key = jax.random.fold_in(key, 11)
    key_values, key_first, key_other = jax.random.split(key, 3)
    drawn = jax.random.randint(key_values, (SEQS,), TOK_DEV // 4, TOK_DEV + 1)
    first = jax.random.randint(key_first, (), 0, SEQS)
    other = (first + 1 + jax.random.randint(key_other, (), 0, SEQS - 1)) % SEQS
    drawn = drawn.at[first].set(TOK_DEV).at[other].set(TOK_DEV // 4)
    return drawn.astype(jnp.int32)


def block_scale(stream_key, extent, cuts, low, high):
    level, own = 1.0, jax.random.fold_in(stream_key, 6)
    for axis_at, parts in cuts:
        steps = jnp.exp(jax.random.uniform(jax.random.fold_in(own, axis_at), (parts,), jnp.float32, low / len(cuts), high / len(cuts)))
        level = level * jnp.repeat(steps, extent[axis_at] // parts).reshape([-1 if axis == axis_at else 1 for axis in range(len(extent))])
    return level


def routed_block(own_key, own, number, rows, count, top, most, lean):
    order = jax.random.permutation(own_key, count)
    crowded, ordinary = load_shares(count, rows * top, most, lean, True), load_shares(count, rows * top, most, lean, False)
    places = jnp.arange(count)

    def named(tallies, offset_by):
        used = int((tallies > 0).sum())
        fixed = max(1, used // 4)
        passed = fixed + (places - fixed + offset_by * (used - fixed)) % max(1, count - fixed)
        return jnp.zeros((count,), jnp.int32).at[order[jnp.where(places < fixed, places, passed)]].set(jnp.asarray(tallies, jnp.int32))

    tallies = jnp.where(number % 4 == 0, named(crowded, number // 4), named(ordinary, number - number // 4 - 1))
    mixed = jax.random.permutation(jax.random.fold_in(own, 3), count)
    source_of, receiver = mixed[0:count // 2 * 2:2], mixed[1:count // 2 * 2:2]
    room = jnp.minimum(tallies[source_of] - 1, most - tallies[receiver]) // 2
    room = jnp.where((source_of == order[0]) | (receiver == order[0]) | (tallies[receiver] == 0), 0, jnp.maximum(room, 0))
    passed = jax.random.randint(jax.random.fold_in(own, 4), (count // 2,), 0, 1 << 20) % (room + 1)
    tallies = tallies.at[source_of].add(-passed).at[receiver].add(passed)
    labels = jnp.searchsorted(jnp.cumsum(tallies), jnp.arange(rows * top), side="right").astype(jnp.int32)
    grid = labels.reshape(top, rows).T
    grid = grid[jax.random.permutation(jax.random.fold_in(own, 1), rows)]
    offset_by = jax.random.randint(jax.random.fold_in(own, 2), (rows, 1), 0, top)
    return jnp.take_along_axis(grid, (jnp.arange(top)[None, :] + offset_by) % top, axis=1)


def load_shares(count, total, limit, slope, full):
    loads = [(1 << 20) // math.isqrt(standing ** slope) + 1 for standing in range(1, count + 1)]
    largest = limit if full else min(limit, max(-(-total // count), total * loads[0] // sum(loads)))
    least = 1 if total - largest >= count - 1 else 0
    counts, spare = [largest] + [least] * (count - 1), total - largest - least * (count - 1)
    while spare > 0:
        free = [i for i in range(1, count) if counts[i] < largest] or [i for i in range(1, count) if counts[i] < limit]
        pool, left = sum([loads[i] for i in free]), spare
        for i in free:
            more = min(limit - counts[i], max(1, left * loads[i] // pool), spare)
            counts[i] = counts[i] + more
            spare = spare - more
    return np.array(counts)


def normal_values(stream_key, dims, deviation, limit, cuts=(), dtype=jnp.bfloat16):
    values = jax.random.normal(stream_key, dims, jnp.float32) * deviation
    if len(cuts) > 0:
        values = block_scale(stream_key, dims, cuts, -0.22, 0.18) * values
    return jnp.clip(values, min=-limit, max=limit).astype(dtype)


def setup_inputs(seed: int = 0) -> dict:
    seeds = jax.random.split(jax.random.key(seed), 14)
    tokens = normal_values(seeds[0], (TOKENS, D), 1.0, 6.0, ((0, 32),))
    cotangent = normal_values(seeds[1], (TOKENS, D), 1.0, 6.0, ((0, 32),))
    lengths = draw_lengths(jax.random.fold_in(seeds[13], 71), 0)
    routes_keys = jax.random.split(jax.random.fold_in(seeds[3], 1), TOKENS // TOK_DEV)
    routes_turns = jax.random.permutation(jax.random.fold_in(seeds[3], 3), TOKENS // TOK_DEV)
    routes = jax.vmap(lambda own, number: routed_block(jax.random.fold_in(seeds[3], 2), own, number, TOK_DEV, EXPERTS, TOP, CAP, 1))(routes_keys, routes_turns).reshape((TOKENS, TOP))
    norm1_gain = jnp.clip(1.0 + 0.1 * jax.random.normal(seeds[4], (D,), jnp.float32), 0.5, 1.5).astype(jnp.bfloat16)
    w_query = normal_values(seeds[5], (D, H * HD), D ** -0.5, 0.15625, ((0, 16),))
    w_kv = normal_values(seeds[6], (D, 2 * KVH * HD), D ** -0.5, 0.15625, ((0, 16),))
    w_out = normal_values(seeds[7], (H * HD, D), ((H * HD) // 16) ** -0.5, 0.625, ((0, 16),))
    norm2_gain = jnp.clip(1.0 + 0.1 * jax.random.normal(seeds[8], (D,), jnp.float32), 0.5, 1.5).astype(jnp.bfloat16)
    w_router = normal_values(seeds[9], (D, EXPERTS), (4 * D) ** -0.5, 0.078125, ((0, 16),))
    expert_gate = normal_values(seeds[10], (EXPERTS, D, FF), D ** -0.5, 0.15625, ((0, 16),))
    expert_up = normal_values(seeds[11], (EXPERTS, D, FF), D ** -0.5, 0.15625, ((0, 16),))
    expert_down = normal_values(seeds[12], (EXPERTS, FF, D), (FF // 16) ** -0.5, 1.0, ((0, 16),))
    return dict(tokens=tokens, cotangent=cotangent, lengths=lengths, routes=routes, norm1_gain=norm1_gain, w_query=w_query, w_kv=w_kv, w_out=w_out, norm2_gain=norm2_gain, w_router=w_router, expert_gate=expert_gate, expert_up=expert_up, expert_down=expert_down)


EPSILON = 1e-05
PRECISE = lax.Precision.HIGHEST

@jax.custom_vjp
def low(v):
    return lax.optimization_barrier(v.astype(jnp.bfloat16)).astype(jnp.float32)

@jax.custom_vjp
def low_back(v):
    return v

def low_keep(v):
    return (low(v), None)

def low_pass(kept, grad):
    return (grad,)

def back_keep(v):
    return (v, None)

def back_low(kept, grad):
    return (low(grad),)
low.defvjp(low_keep, low_pass)
low_back.defvjp(back_keep, back_low)

def rotate(values, cosine, sines):
    half_dim = values.shape[-1] // 2
    first_half = values[..., :half_dim]
    second_half = values[..., half_dim:]
    return jnp.concatenate([first_half * cosine - second_half * sines, second_half * cosine + first_half * sines], -1)

def rope_tables(length):
    half_dim = HD // 2
    positions = jnp.arange(length).astype(jnp.float32)
    inverse = jnp.power(jnp.float32(10000.0), -jnp.arange(half_dim).astype(jnp.float32) / half_dim)
    angles = positions[:, None] * inverse[None, :]
    return (jnp.cos(angles)[:, None, :], jnp.sin(angles)[:, None, :])

def normalize(values, gain):
    return values * lax.rsqrt(lax.optimization_barrier(jnp.mean(values * values, axis=-1, keepdims=True)) + EPSILON) * gain

def attend(pieces):
    query_proj, kv_proj = pieces
    length = query_proj.shape[0]
    cosine, sines = rope_tables(length)
    queries = low(rotate(query_proj.reshape(length, H, HD), cosine, sines)).reshape(length, KVH, H // KVH, HD)
    keys = low(rotate(kv_proj[:, :KVH * HD].reshape(length, KVH, HD), cosine, sines))
    values = low(kv_proj[:, KVH * HD:].reshape(length, KVH, HD))
    scores = low_back(jnp.einsum('tgjd,ugd->gjtu', queries, keys, precision=PRECISE) * HD ** (-0.5))
    causal = jnp.arange(length)[:, None] >= jnp.arange(length)[None, :]
    probs = low(jax.nn.softmax(jnp.where(causal[None, None], scores, -1e+30), axis=-1))
    return jnp.einsum('gjtu,ugd->tgjd', probs, values, precision=PRECISE).reshape(length, H * HD)

def layer(inputs, route_rows, weights):
    gain_one, gain_two, query_w, kv_w, out_w, router_w, gate_w, up_w, down_w = weights
    group_count = inputs.shape[0] // TOK_DEV
    normed = low(normalize(inputs, gain_one))
    query_proj = low_back(jnp.dot(normed, query_w, precision=PRECISE))
    kv_proj = low_back(jnp.dot(normed, kv_w, precision=PRECISE))
    attended = lax.map(jax.checkpoint(attend), (query_proj.reshape(group_count, TOK_DEV, H * HD), kv_proj.reshape(group_count, TOK_DEV, 2 * KVH * HD)))
    attended = low(low_back(attended.reshape(-1, H * HD)))
    middle = inputs + low_back(jnp.dot(attended, out_w, precision=PRECISE))
    mixed_in = low(normalize(middle, gain_two))
    logits = low_back(jnp.dot(mixed_in, router_w, precision=PRECISE))
    chosen = (route_rows[:, :, None] == jnp.arange(EXPERTS).astype(jnp.int32)[None, None, :]).astype(jnp.float32)
    selected = lax.optimization_barrier(jnp.sum(chosen * logits[:, None, :], axis=-1))
    gates = jax.nn.softmax(selected, axis=-1)
    combine = jnp.einsum('tk,tke->et', gates, chosen, precision=PRECISE)

    def expert_step(running, pieces):
        gate_mat, up_mat, down_mat, weight_row = pieces
        entering = low_back(mixed_in)
        gate_pre = low_back(jnp.dot(entering, gate_mat, precision=PRECISE))
        up_pre = low_back(jnp.dot(entering, up_mat, precision=PRECISE))
        hidden = low(jax.nn.silu(gate_pre) * up_pre)
        result = low(low_back(jnp.dot(hidden, down_mat, precision=PRECISE)))
        return (running + weight_row[:, None] * result, None)
    mixture = lax.scan(jax.checkpoint(expert_step), jnp.zeros_like(middle), (gate_w, up_w, down_w, combine))[0]
    return middle + mixture

def reference(tokens, cotangent, lengths, routes, norm1_gain, w_query, w_kv, w_out, norm2_gain, w_router, expert_gate, expert_up, expert_down):
    weights = tuple((item.astype(jnp.float32) for item in (norm1_gain, norm2_gain, w_query, w_kv, w_out, w_router, expert_gate, expert_up, expert_down)))
    group_count = math.gcd(SEQS, max(1, 4096 // TOK_DEV))
    block_count = SEQS // group_count
    block_rows = group_count * TOK_DEV
    positions = jnp.arange(TOK_DEV).astype(jnp.int32)

    def reorder(params):
        gain_one, gain_two, query_w, kv_w, out_w, router_w, gate_w, up_w, down_w = params
        return (gain_one, gain_two, query_w, kv_w, out_w, router_w, gate_w, up_w, down_w)

    def block_step(totals, pieces):
        inputs, upstream, route_rows, seq_lengths = pieces
        live = (positions[None, :] < seq_lengths[:, None]).astype(jnp.float32).reshape(-1, 1)
        outputs, pull = jax.vjp(lambda values, params: layer(values, route_rows, reorder(params)), inputs.astype(jnp.float32), weights)
        input_grads, weight_grads = pull(upstream.astype(jnp.float32) * live)
        totals = jax.tree.map(lambda running, update: running + update, totals, weight_grads)
        return (totals, (outputs.astype(jnp.bfloat16), input_grads.astype(jnp.bfloat16)))
    zeros = jax.tree.map(jnp.zeros_like, weights)
    totals, (outputs, input_grads) = lax.scan(block_step, zeros, (tokens.reshape(block_count, block_rows, D), cotangent.reshape(block_count, block_rows, D), routes.reshape(block_count, block_rows, TOP), lengths.reshape(block_count, group_count)))
    return (outputs.reshape(TOKENS, D), input_grads.reshape(TOKENS, D), totals[0], totals[2], totals[3], totals[4], totals[1], totals[5], totals[6], totals[7], totals[8])
```

```python
import functools

import jax
import jax.numpy as jnp
from jax import lax
from jax.experimental import pallas as pl
from jax.experimental.pallas import tpu as pltpu
from jax.sharding import PartitionSpec as P

HD = 64
EPSILON = 1e-05
MESH = pl.DeviceIdType.MESH
ANY = pl.BlockSpec(memory_space=pl.ANY)
VMEM = pl.BlockSpec(memory_space=pltpu.VMEM)
DMA = pltpu.SemaphoreType.DMA
MB = 2**20
f32 = jnp.float32
bf16 = jnp.bfloat16


def mul(a, b, ca, cb):
    return lax.dot_general(a, b, (((ca,), (cb,)), ((), ())), preferred_element_type=f32)


class Place:
    def __init__(self, n):
        self.n, self.mid, self.ring = n, n // 8, n // 2
        self.half = self.ring // 2
        self.me = lax.axis_index("expert")
        self.chip, self.core = lax.div(self.me, 2), lax.rem(self.me, 2)
        outer, inner = lax.div(self.chip, self.mid), lax.rem(self.chip, self.mid)
        row = 3 - outer
        step = jnp.where(lax.rem(row, 2) == 0, inner - 1, self.mid - 1 - inner)
        self.at = jnp.where(inner == 0, outer, 4 + row * (self.mid - 1) + step)
        self.sibling = self.chip * 2 + 1 - self.core
        self.right, self.left = self.device(1), self.device(-1)

    def chip_at(self, distance):
        p = lax.rem(self.at + distance + self.ring, self.ring)
        wide = max(self.mid - 1, 1)
        row, k = lax.div(lax.max(p - 4, 0), wide), lax.rem(lax.max(p - 4, 0), wide)
        inner = jnp.where(lax.rem(row, 2) == 0, 1 + k, self.mid - 1 - k)
        return jnp.where(p < 4, p * self.mid, (3 - row) * self.mid + inner)

    def device(self, distance):
        return self.chip_at(distance) * 2 + self.core


def remote(src, dst, send, recv, device):
    return pltpu.make_async_remote_copy(
        src_ref=src, dst_ref=dst, send_sem=send, recv_sem=recv, device_id={"expert": device}, device_id_type=MESH
    )


def meet(targets):
    barrier = pltpu.get_barrier_semaphore()
    for target in targets:
        pl.semaphore_signal(barrier, inc=1, device_id={"expert": target}, device_id_type=MESH)
    pl.semaphore_wait(barrier, len(targets))


def meet_all(place):
    barrier = pltpu.get_barrier_semaphore()

    @pl.loop(1, place.n)
    def _(d):
        other = lax.rem(place.me + d, place.n)
        pl.semaphore_signal(barrier, inc=1, device_id={"expert": other}, device_id_type=MESH)

    pl.semaphore_wait(barrier, place.n - 1)


def column_cuts(width, parts):
    tiles = width // 128
    edges = [128 * (tiles * i // parts) for i in range(parts + 1)]
    return [(edges[i], edges[i + 1] - edges[i]) for i in range(parts)]


def gather_kernel(n, cuts, count, *refs):
    xs, outs, (own_sem, ss, rs, css, crs) = refs[:count], refs[count : 2 * count], refs[2 * count :]
    place = Place(n)
    half = place.half
    meet((place.right, place.left, place.sibling))
    started = []

    def begin(copy):
        copy.start()
        started.append(copy)

    def has(d, k, q, parts):
        return k < half or ((q < parts // 2) == (d == 0))

    for a in range(count):
        x_ref, o_ref = xs[a], outs[a]
        parts = len(cuts[a])
        own = pltpu.make_async_copy(x_ref, o_ref.at[place.me], own_sem.at[a])
        own.start()

        def part(ref, q, a=a):
            return ref.at[:, pl.ds(*cuts[a][q])]

        def along(d, k, q, a=a, x_ref=x_ref, o_ref=o_ref):
            b = place.device(1 - k) if d == 0 else place.device(k - 1)
            src = part(x_ref, q) if k == 1 else part(o_ref.at[b], q)
            return remote(
                src,
                part(o_ref.at[b], q),
                ss.at[a, d, k - 1, q],
                rs.at[a, d, k - 1, q],
                place.right if d == 0 else place.left,
            )

        def across(d, k, q, a=a, x_ref=x_ref, o_ref=o_ref):
            b = place.me if k == 0 else (place.device(-k) if d == 0 else place.device(k))
            src = part(x_ref, q) if k == 0 else part(o_ref.at[b], q)
            return remote(src, part(o_ref.at[b], q), css.at[a, d, k, q], crs.at[a, d, k, q], place.sibling)

        for k in range(1, half + 2):
            for i in range(parts):
                for d in (0, 1):
                    q = i if d == 0 else parts - 1 - i
                    if k > 1 and has(d, k - 1, q, parts):
                        along(d, k - 1, q).wait_recv()
                    if k <= half and has(d, k, q, parts):
                        begin(along(d, k, q))
                    if k == 1 and d == 0:
                        begin(across(0, 0, q))
                    if k > 1 and has(d, k - 1, q, parts):
                        begin(across(d, k - 1, q))
        for k in range(half + 1):
            for q in range(parts):
                for d in (0, 1):
                    if (k == 0 and d == 0) or (k > 0 and has(d, k, q, parts)):
                        across(d, k, q).wait_recv()
        own.wait()
    for copy in started:
        copy.wait_send()


def gather(n, arrays, collective_id):
    half, count = n // 4, len(arrays)
    cuts = [column_cuts(x.shape[1], 2) for x in arrays]
    return pl.pallas_call(
        functools.partial(gather_kernel, n, cuts, count),
        out_shape=[jax.ShapeDtypeStruct((n,) + x.shape, x.dtype) for x in arrays],
        in_specs=[ANY] * count,
        out_specs=[ANY] * count,
        scratch_shapes=[
            DMA((count,)),
            DMA((count, 2, half, 2)),
            DMA((count, 2, half, 2)),
            DMA((count, 2, half + 1, 2)),
            DMA((count, 2, half + 1, 2)),
        ],
        compiler_params=pltpu.CompilerParams(
            collective_id=collective_id, has_side_effects=True, vmem_limit_bytes=16 * MB
        ),
    )(*arrays)


SLOTS = 4


def ring_work(half, parts):
    work = []
    for k in range(half, 0, -1):
        for i in range(parts):
            for d in (0, 1):
                q = i if d == 0 else parts - 1 - i
                if goes(d, k, q, half, parts):
                    work.append((d, k, q))
    return work + [(None, 0, q) for q in range(parts)]


def goes(d, k, q, half, parts):
    return k < half or ((q < parts // 2) == (d == 0))


def widest(width, parts):
    return max(w for _, w in column_cuts(width, parts))


def reduce_scratch(rows, width, half, parts):
    return [
        pltpu.VMEM((2, half, rows, width), bf16),
        pltpu.VMEM((SLOTS, rows, widest(width, parts)), bf16),
        pltpu.VMEM((SLOTS, rows, widest(width, parts)), bf16),
        DMA((SLOTS,)),
        DMA((SLOTS,)),
        DMA((SLOTS,)),
        DMA((2, half, parts)),
    ]


def ring_reduce(place, own_at, other_at, other_wait, width, write, scratch):
    arrived, mine, theirs, mine_sem, theirs_sem, send_sem, recv_sem = scratch
    half = place.half
    parts = recv_sem.shape[2]
    cuts = column_cuts(width, parts)
    rows = arrived.shape[2]
    tile = 16
    work = ring_work(half, parts)

    def chip_of(d, k):
        return place.chip_at(k if d != 1 else -k)

    def loads(i):
        d, k, q = work[i]
        slot, chip, (start, size) = i % SLOTS, chip_of(d, k), cuts[q]
        return (
            pltpu.make_async_copy(
                own_at(chip).at[:, pl.ds(start, size)], mine.at[slot, :, pl.ds(0, size)], mine_sem.at[slot]
            ),
            pltpu.make_async_copy(
                other_at(chip).at[:, pl.ds(start, size)], theirs.at[slot, :, pl.ds(0, size)], theirs_sem.at[slot]
            ),
        )

    def send(i):
        d, k, q = work[i]
        start, size = cuts[q]
        return remote(
            mine.at[i % SLOTS, :, pl.ds(0, size)],
            arrived.at[d, k - 1, :, pl.ds(start, size)],
            send_sem.at[i % SLOTS],
            recv_sem.at[d, k - 1, q],
            place.right if d == 0 else place.left,
        )

    waited = set()

    def fetch(i):
        if i >= len(work):
            return
        d, k, q = work[i]
        if i >= SLOTS:
            send(i - SLOTS).wait_send()
        key = (0 if k in (0, half) else d, k)
        if key not in waited:
            waited.add(key)
            other_wait(chip_of(d, k))
        for copy in loads(i):
            copy.start()

    ahead = SLOTS // 2
    for i in range(ahead):
        fetch(i)
    for i, (d, k, q) in enumerate(work):
        fetch(i + ahead)
        for copy in loads(i):
            copy.wait()
        start, size = cuts[q]
        slot = i % SLOTS
        come = []
        for dd in (0, 1) if d is None else (d,):
            if k + 1 <= half and goes(dd, k + 1, q, half, parts):
                piece = arrived.at[dd, k, :, pl.ds(start, size)]
                remote(piece, piece, send_sem.at[slot], recv_sem.at[dd, k, q], place.sibling).wait_recv()
                come.append(dd)

        @pl.loop(0, rows // tile)
        def _(r):
            at = pl.ds(pl.multiple_of(r * tile, tile), tile)
            total = mine[slot, at, pl.ds(0, size)].astype(f32) + theirs[slot, at, pl.ds(0, size)].astype(f32)
            for dd in come:
                total += arrived[dd, k, at, pl.ds(start, size)].astype(f32)
            if d is None:
                write(at, pl.ds(start, size), total)
            else:
                mine[slot, at, pl.ds(0, size)] = total.astype(bf16)

        if d is not None:
            send(i).start()
        yield
    sends = len(work) - parts
    for i in range(max(0, len(work) - SLOTS), sends):
        send(i).wait_send()


DENSE_PARTS = 4


def swap_halves(values, lane):
    width = values.shape[1]
    return jnp.where(lane % HD < HD // 2, pltpu.roll(values, width - HD // 2, 1), pltpu.roll(values, HD // 2, 1))


def head_halves(block, lane, low):
    turned = pltpu.roll(block, HD, 1)
    lower, upper = (block, turned) if low == 0 else (turned, block)
    zero = jnp.zeros_like(block)
    return jnp.where(lane < HD, lower, zero).astype(bf16), jnp.where(lane < HD, zero, upper).astype(bf16)


def softmax_rows(q, k, causal):
    scores = jnp.where(causal, mul(q, k, 1, 1) * HD**-0.5, -1e30)
    e = jnp.exp(scores - jnp.max(scores, axis=1, keepdims=True))
    return e * (1.0 / jnp.sum(e, axis=1, keepdims=True))


def backward_kernel(
    n,
    dp,
    od_ref,
    sd_ref,
    wall_ref,
    dmix_ref,
    dgate_ref,
    gates_ref,
    middle_ref,
    mixed_ref,
    dout_ref,
    tokens_ref,
    normed_t_ref,
    attended_t_ref,
    q_ref,
    k_ref,
    v_ref,
    cos_ref,
    sin_ref,
    gains_ref,
    output_ref,
    input_grad_ref,
    dense_ref,
    weights,
    extra_w,
    d_middle,
    d_middle_low,
    d_att,
    d_qkv,
    d_normed,
    extra,
    logits_low,
    own_f,
    stage_f,
    other_f,
    come_f,
    copies_f,
    weight_sem,
    stage_sem,
    other_sem,
    send_f,
    recv_f,
    copy_s,
    copy_r,
    *scratch_d,
):
    place = Place(n)
    half, ring = place.half, place.ring
    rank = lax.axis_index("dp")
    rows, width = middle_ref.shape
    q_width, kv_width = q_ref.shape[1], 2 * k_ref.shape[1]
    qkv_width = q_width + kv_width
    shard = own_f.shape[1]
    full_width = own_f.shape[2]
    barrier = pltpu.get_barrier_semaphore()
    for target in (place.right, place.left, place.sibling):
        pl.semaphore_signal(barrier, inc=1, device_id={"expert": target}, device_id_type=MESH)
    for turn in range(1, dp):
        pl.semaphore_signal(barrier, inc=1, device_id={"dp": lax.rem(rank + turn, dp)}, device_id_type=MESH)
    out_w = pltpu.make_async_copy(
        wall_ref.at[:, pl.ds(qkv_width, width)], weights.at[:, pl.ds(0, width)], weight_sem.at[0]
    )
    extra_copy = pltpu.make_async_copy(wall_ref.at[:, pl.ds(qkv_width + width, 128)], extra_w, weight_sem.at[1])
    qkv_w = pltpu.make_async_copy(wall_ref.at[:, pl.ds(0, qkv_width)], weights, weight_sem.at[2])
    out_w.start()
    extra_copy.start()
    pl.semaphore_wait(barrier, 3 + dp - 1)

    def write_output(at, columns, total):
        output_ref[at, columns] = (middle_ref[at, columns] + total).astype(bf16)

    background = ring_reduce(
        place, lambda chip: od_ref.at[chip], lambda chip: sd_ref.at[chip], lambda chip: None, width, write_output, scratch_d
    )
    items = len(ring_work(half, scratch_d[6].shape[2]))
    done = [0]

    def pump(share):
        while done[0] < min(items, int(items * share + 0.5)):
            next(background)
            done[0] += 1

    pump(0.07)
    d_rows = jnp.concatenate([dgate_ref[:, 0, :], jnp.zeros((128 - n, rows), f32)], axis=0)
    d_gates = jnp.transpose(d_rows)
    gates = gates_ref[...]
    d_sel = gates * (d_gates - jnp.sum(gates * d_gates, axis=1, keepdims=True))
    logits_low[...] = d_sel.astype(bf16)
    extra_copy.wait()
    d_normed[...] = mul(logits_low[...], extra_w[...], 1, 1)
    gain_one, gain_two = gains_ref[0:1], gains_ref[1:2]
    tile = 32

    @pl.loop(0, rows // tile)
    def _(r):
        at = pl.ds(pl.multiple_of(r * tile, tile), tile)
        middle = middle_ref[at]
        d_mixed = dmix_ref[at] + d_normed[at]
        inv = lax.rsqrt(jnp.mean(middle * middle, axis=1, keepdims=True) + EPSILON)
        scaled = d_mixed * gain_two
        back = jnp.mean(scaled * middle, axis=1, keepdims=True)
        total = dout_ref[at].astype(f32) + inv * scaled - middle * (inv * inv * inv * back)
        d_middle[at] = total
        d_middle_low[at] = total.astype(bf16)
        d_att[at] = (d_mixed * middle * inv).astype(bf16)

    lane = lax.broadcasted_iota(jnp.int32, (rows, 128), 1)
    extra[...] = mul(mixed_ref[...], logits_low[...], 0, 0) + mul(
        d_att[...], (lane == n + 1).astype(bf16), 0, 0
    )
    pump(0.14)
    out_w.wait()
    d_att[...] = mul(d_middle_low[...], weights[:, pl.ds(0, width)], 1, 1).astype(bf16)
    qkv_w.start()
    pump(0.21)

    t_at = lax.broadcasted_iota(jnp.int32, (rows, rows), 0)
    u_at = lax.broadcasted_iota(jnp.int32, (rows, rows), 1)
    causal = t_at >= u_at
    cosine, sine = cos_ref[...], sin_ref[...]
    sine_back = jnp.where(lane % HD < HD // 2, sine, -sine)
    kv_count = k_ref.shape[1] // HD
    per_group = q_width // HD // kv_count
    d_normed[...] = jnp.zeros_like(d_normed)
    pair_k, pair_v = None, None
    for g in range(kv_count):
        pair = pl.ds(128 * (g // 2), 128)
        k_parts = head_halves(k_ref[:, pair].astype(f32), lane, g % 2)
        v_parts = head_halves(v_ref[:, pair].astype(f32), lane, g % 2)
        d_k, d_v = [None, None], [None, None]
        for h in range(per_group * g, per_group * (g + 1)):
            at = pl.ds(128 * (h // 2), 128)
            low = h % 2
            query, d_a = q_ref[:, at], d_att[:, at]
            probs = softmax_rows(query, k_parts[low], causal)
            probs_low = probs.astype(bf16)
            d_probs = mul(d_a, v_parts[low], 1, 1)
            weighted = probs * d_probs
            d_scores = (weighted - probs * jnp.sum(weighted, axis=1, keepdims=True)).astype(bf16)
            d_normed[:, at] += mul(d_scores, k_parts[low], 1, 0)
            step_k, step_v = mul(d_scores, query, 0, 0), mul(probs_low, d_a, 0, 0)
            d_k[low] = step_k if d_k[low] is None else d_k[low] + step_k
            d_v[low] = step_v if d_v[low] is None else d_v[low] + step_v

        def gathered(parts):
            stay, turn = parts[g % 2], parts[1 - g % 2]
            return stay if turn is None else (pltpu.roll(turn, HD, 1) if stay is None else stay + pltpu.roll(turn, HD, 1))

        if g % 2 == 0:
            pair_k, pair_v = gathered(d_k), gathered(d_v)
        if g % 2 == 1 or g + 1 == kv_count:
            total_k = jnp.where(lane < HD, pair_k, gathered(d_k)) * HD**-0.5
            total_v = jnp.where(lane < HD, pair_v, gathered(d_v))
            turned = total_k * cosine + swap_halves(total_k, lane) * sine_back
            d_qkv[:, pl.ds(q_width + 128 * (g // 2), 128)] = turned.astype(bf16)
            d_qkv[:, pl.ds(q_width + kv_width // 2 + 128 * (g // 2), 128)] = total_v.astype(bf16)
        pump(0.21 + 0.6 * (g + 1) / kv_count)
    for b in range(q_width // 128):
        at = pl.ds(128 * b, 128)
        total = d_normed[:, at] * HD**-0.5
        d_qkv[:, at] = (total * cosine + swap_halves(total, lane) * sine_back).astype(bf16)
    pump(0.85)
    qkv_w.wait()
    d_normed[...] = mul(d_qkv[...], weights[...], 1, 1)

    @pl.loop(0, rows // tile)
    def _(r):
        at = pl.ds(pl.multiple_of(r * tile, tile), tile)
        inputs = tokens_ref[at].astype(f32)
        d = d_normed[at]
        inv = lax.rsqrt(jnp.mean(inputs * inputs, axis=1, keepdims=True) + EPSILON)
        scaled = d * gain_one
        back = jnp.mean(scaled * inputs, axis=1, keepdims=True)
        total = d_middle[at] + inv * scaled - inputs * (inv * inv * inv * back)
        input_grad_ref[at] = total.astype(bf16)
        d_att[at] = (d * inputs * inv).astype(bf16)

    extra[...] += mul(d_att[...], (lane == n).astype(bf16), 0, 0)
    pump(1.0)
    for _ in background:
        pass

    def cross(chip, slot):
        return remote(stage_f.at[slot], other_f.at[chip], stage_sem.at[slot], other_sem.at[chip], place.sibling)

    def fill(ref, device):
        at = pl.ds(pl.multiple_of(device * shard, 16), shard)
        ref[:, pl.ds(0, qkv_width)] = mul(normed_t_ref[at], d_qkv[...], 1, 0).astype(bf16)
        ref[:, pl.ds(qkv_width, width)] = mul(attended_t_ref[at], d_middle_low[...], 1, 0).astype(bf16)
        ref[:, pl.ds(qkv_width + width, 128)] = extra[at].astype(bf16)

    @pl.loop(0, ring)
    def _(i):
        away = half - lax.div(i + 1, 2)
        chip = place.chip_at(jnp.where(lax.rem(i, 2) == 0, away, -away))
        slot = lax.rem(i, 2)

        @pl.when(i >= 2)
        def _():
            cross(chip, slot).wait_send()

        fill(stage_f.at[slot], chip * 2 + 1 - place.core)
        cross(chip, slot).start()
        fill(own_f.at[chip], chip * 2 + place.core)

    for slot in range(2):
        cross(place.chip, slot).wait_send()
    cuts = column_cuts(full_width, DENSE_PARTS)
    work = ring_work(half, DENSE_PARTS)

    def send(d, k, q):
        chip = place.chip_at(k if d == 0 else -k)
        at = pl.ds(*cuts[q])
        return remote(
            own_f.at[chip, :, at],
            come_f.at[d, k - 1, :, at],
            send_f.at[d, k - 1, q],
            recv_f.at[d, k - 1, q],
            place.right if d == 0 else place.left,
        )

    def spread(turn, q):
        at = pl.ds(*cuts[q])
        return pltpu.make_async_remote_copy(
            src_ref=copies_f.at[rank, :, at],
            dst_ref=copies_f.at[rank, :, at],
            send_sem=copy_s.at[turn, q],
            recv_sem=copy_r.at[turn, q],
            device_id={"dp": lax.rem(rank + turn, dp)},
            device_id_type=MESH,
        )

    met = set()
    for d, k, q in work:
        chip = place.chip_at(0 if d is None else (k if d == 0 else -k))
        key = (0 if k in (0, half) else d, k)
        if key not in met:
            met.add(key)
            remote(other_f.at[chip], other_f.at[chip], stage_sem.at[0], other_sem.at[chip], place.sibling).wait_recv()
        at = pl.ds(*cuts[q])
        total = own_f[chip, :, at].astype(f32) + other_f[chip, :, at].astype(f32)
        for dd in (0, 1) if d is None else (d,):
            if k + 1 <= half and goes(dd, k + 1, q, half, DENSE_PARTS):
                piece = come_f.at[dd, k, :, at]
                remote(piece, piece, send_f.at[dd, k, q], recv_f.at[dd, k, q], place.sibling).wait_recv()
                total += piece[...].astype(f32)
        if d is not None:
            own_f[chip, :, at] = total.astype(bf16)
            send(d, k, q).start()
        else:
            copies_f[rank, :, at] = total.astype(bf16)
            for turn in range(1, dp):
                spread(turn, q).start()
    for q in range(DENSE_PARTS):
        for turn in range(1, dp):
            spread(turn, q).wait()
        at = pl.ds(*cuts[q])
        total = copies_f[0, :, at].astype(f32)
        for r in range(1, dp):
            total += copies_f[r, :, at].astype(f32)
        dense_ref[:, at] = total
    for d, k, q in work:
        if d is not None:
            send(d, k, q).wait_send()


def backward(n, dp, own_d, other_d, wall, others, collective_id):
    half, ring = n // 4, n // 2
    rows, width = own_d.shape[1:]
    full_width = wall.shape[1]
    qkv_width = full_width - width - 128
    shard = wall.shape[0] // n
    q_width = others[9].shape[1]
    return pl.pallas_call(
        functools.partial(backward_kernel, n, dp),
        out_shape=[
            jax.ShapeDtypeStruct((rows, width), bf16),
            jax.ShapeDtypeStruct((rows, width), bf16),
            jax.ShapeDtypeStruct((shard, full_width), f32),
        ],
        in_specs=[ANY] * 3 + [VMEM] * len(others),
        out_specs=[VMEM] * 3,
        scratch_shapes=[
            pltpu.VMEM((width, qkv_width), bf16),
            pltpu.VMEM((width, 128), bf16),
            pltpu.VMEM((rows, width), f32),
            pltpu.VMEM((rows, width), bf16),
            pltpu.VMEM((rows, q_width), bf16),
            pltpu.VMEM((rows, qkv_width), bf16),
            pltpu.VMEM((rows, width), f32),
            pltpu.VMEM((width, 128), f32),
            pltpu.VMEM((rows, 128), bf16),
            pltpu.VMEM((ring, shard, full_width), bf16),
            pltpu.VMEM((2, shard, full_width), bf16),
            pltpu.VMEM((ring, shard, full_width), bf16),
            pltpu.VMEM((2, half, shard, full_width), bf16),
            pltpu.VMEM((dp, shard, full_width), bf16),
            DMA((3,)),
            DMA((2,)),
            DMA((ring,)),
            DMA((2, half, DENSE_PARTS)),
            DMA((2, half, DENSE_PARTS)),
            DMA((dp, DENSE_PARTS)),
            DMA((dp, DENSE_PARTS)),
        ]
        + reduce_scratch(rows, width, half, 4),
        compiler_params=pltpu.CompilerParams(
            collective_id=collective_id, has_side_effects=True, vmem_limit_bytes=63 * MB
        ),
    )(own_d, other_d, wall, *others)


QUARTERS = 4


def expert_kernel(
    n,
    x_ref,
    dog_ref,
    gates_ref,
    wgu_ref,
    wd_ref,
    de_ref,
    dgates_ref,
    ggu_ref,
    gd_ref,
    od_ref,
    sd_ref,
    oe_ref,
    se_ref,
    xg_ref,
    acc_gu,
    acc_d,
    gate_in,
    dgate_out,
    xbuf,
    dobuf,
    pd,
    pe,
    own_sem,
    ring_s,
    ring_r,
    cross_s,
    cross_r,
    load_sem,
    put_sem,
    sib_r,
    gate_s,
    gate_r,
    dgate_s,
    dgate_r,
    *reduce_refs,
):
    place = Place(n)
    half, ring, me = place.half, place.ring, place.me
    rows, width = x_ref.shape
    hidden_width = wd_ref.shape[0]
    piece = rows // QUARTERS
    meet_all(place)

    own = pltpu.make_async_copy(x_ref, xg_ref.at[me], own_sem.at[0])
    own.start()

    def at(q):
        return pl.ds(pl.multiple_of(q * piece, piece), piece)

    def block_of(d, k):
        return jnp.where(d == 0, place.device(-k), place.device(k))

    def along(d, k, q):
        b = block_of(d, k - 1)
        return remote(
            xg_ref.at[b, at(q)],
            xg_ref.at[b, at(q)],
            ring_s.at[d, k - 1, q],
            ring_r.at[d, k - 1, q],
            jnp.where(d == 0, place.right, place.left),
        )

    def across(d, k, q):
        b = block_of(d, k)
        return remote(xg_ref.at[b, at(q)], xg_ref.at[b, at(q)], cross_s.at[d, k, q], cross_r.at[d, k, q], place.sibling)

    def gate_copy(d):
        to = lax.rem(me + d, n)
        return remote(gates_ref.at[to], gate_in.at[me], gate_s.at[d], gate_r.at[d], to)

    @pl.loop(1, n)
    def _(d):
        gate_copy(d).start()

    own.wait()
    for q in range(QUARTERS):
        for d in (0, 1):
            along(d, 1, q).start()
    for q in range(QUARTERS):
        across(0, 0, q).start()
    gate_in[me] = gates_ref[me]
    acc_gu[...] = jnp.zeros_like(acc_gu)
    acc_d[...] = jnp.zeros_like(acc_d)

    def step_of(i):
        k = jnp.where(i < 2, 0, lax.div(i + 2, 4))
        j = jnp.where(i < 2, i, lax.rem(i + 2, 4))
        edge = jnp.logical_or(k == 0, k == half)
        d = jnp.where(edge, 0, lax.rem(j, 2))
        other = jnp.where(edge, j, lax.div(j, 2))
        chip = jnp.where(d == 0, place.chip_at(-k), place.chip_at(k))
        core = jnp.where(other == 0, place.core, 1 - place.core)
        return k, j, d, other, chip, chip * 2 + core

    def pump(d, k, q, last=False):
        along(d, k, q).wait_recv()
        if not last:
            near = jnp.where(q < QUARTERS // 2, 0, 1) == d

            @pl.when(jnp.logical_or(k + 1 < half, near))
            def _():
                along(d, k + 1, q).start()

        across(d, k, q).start()

    def load(block, slot):
        return (
            pltpu.make_async_copy(xg_ref.at[block], xbuf.at[slot], load_sem.at[0, slot]),
            pltpu.make_async_copy(dog_ref.at[block], dobuf.at[slot], load_sem.at[1, slot]),
        )

    def put_wait(slot):
        for which, buf in enumerate((pd, pe)):
            pltpu.make_async_copy(buf.at[slot], buf.at[slot], put_sem.at[which, slot]).wait()

    def dgate_copy(block):
        d = lax.rem(block - me + n, n)
        return remote(dgate_out.at[block], dgates_ref.at[me], dgate_s.at[d], dgate_r.at[d], block)

    for copy in load(me, 0):
        copy.start()

    @pl.loop(0, n)
    def _(i):
        k, j, d, other, chip, block = step_of(i)
        slot = lax.rem(i, 2)
        for copy in load(block, slot):
            copy.wait()

        @pl.when(i > 0)
        def _():
            away = lax.rem(me - block + n, n)
            remote(gate_in.at[block], gate_in.at[block], gate_s.at[away], gate_r.at[away], place.sibling).wait_recv()

        gate = jnp.transpose(gate_in[block])[:, :1]
        x = xbuf[slot]
        gu = mul(x, wgu_ref[...], 1, 0)
        g, u = gu[:, :hidden_width], gu[:, hidden_width:]
        s = 1.0 / (1.0 + jnp.exp(-g))
        gs = g * s
        hid = gs * u
        hidg = (hid * gate).astype(bf16)

        @pl.when(i >= 2)
        def _():
            put_wait(slot)

        pd[slot] = mul(hidg, wd_ref[...], 1, 0).astype(bf16)

        @pl.when(i < 2)
        def _():
            for t in range(2):
                for dd in (0, 1):
                    pump(dd, 1, i * 2 + t)

        @pl.when(jnp.logical_and(i >= 2, k + 1 < half))
        def _():
            for dd in (0, 1):
                pump(dd, k + 1, j)

        @pl.when(k + 1 == half)
        def _():
            pump(jnp.where(j < QUARTERS // 2, 0, 1), half, j, last=True)

        nk, nj, nd, nother, nchip, nblock = step_of(i + 1)

        @pl.when(jnp.logical_and(i + 1 < n, nother == 1))
        def _():
            for q in range(QUARTERS):
                dd = jnp.where(nk == half, 0 if q < QUARTERS // 2 else 1, nd)
                b = nblock
                remote(
                    xg_ref.at[b, at(q)], xg_ref.at[b, at(q)], cross_s.at[dd, nk, q], cross_r.at[dd, nk, q], place.sibling
                ).wait_recv()

        @pl.when(i + 1 < n)
        def _():
            for copy in load(nblock, 1 - slot):
                copy.start()

        do = dobuf[slot]
        dh = mul(do, wd_ref[...], 1, 1)
        dgate = jnp.sum(dh * hid, axis=1, keepdims=True)
        dgate_out[block] = jnp.transpose(jnp.broadcast_to(dgate, (rows, 128)))[:8]
        dh = dh * gate
        d_g = (dh * u * s * (1.0 + g * (1.0 - s))).astype(bf16)
        d_u = (dh * gs).astype(bf16)
        dgu = jnp.concatenate([d_g, d_u], axis=1)
        pe[slot] = mul(dgu, wgu_ref[...], 1, 1).astype(bf16)

        @pl.when(i > 0)
        def _():
            dgate_copy(block).start()

        @pl.when(i == 0)
        def _():
            dgates_ref[me] = dgate_out[me]

        @pl.when(other == 0)
        def _():
            pltpu.make_async_copy(pd.at[slot], od_ref.at[chip], put_sem.at[0, slot]).start()
            pltpu.make_async_copy(pe.at[slot], oe_ref.at[chip], put_sem.at[1, slot]).start()

        @pl.when(other == 1)
        def _():
            remote(pd.at[slot], sd_ref.at[chip], put_sem.at[0, slot], sib_r.at[0, chip], place.sibling).start()
            remote(pe.at[slot], se_ref.at[chip], put_sem.at[1, slot], sib_r.at[1, chip], place.sibling).start()

        acc_gu[...] += mul(x, dgu, 0, 0)
        acc_d[...] += mul(hidg, do, 0, 0)

    put_wait(0)
    put_wait(1)
    ggu_ref[...] = acc_gu[...].astype(bf16)
    gd_ref[...] = acc_d[...].astype(bf16)

    def other_wait(chip):
        remote(se_ref.at[chip], se_ref.at[chip], put_sem.at[1, 0], sib_r.at[1, chip], place.sibling).wait_recv()

    def write(at, columns, total):
        de_ref[at, columns] = total

    for _ in ring_reduce(
        place, lambda chip: oe_ref.at[chip], lambda chip: se_ref.at[chip], other_wait, width, write, reduce_refs
    ):
        pass

    @pl.loop(0, ring)
    def _(chip):
        remote(sd_ref.at[chip], sd_ref.at[chip], put_sem.at[0, 0], sib_r.at[0, chip], place.sibling).wait_recv()

    @pl.loop(1, n)
    def _(d):
        gate_copy(d).wait_send()
        source = lax.rem(me - d + n, n)
        remote(dgates_ref.at[source], dgates_ref.at[source], dgate_s.at[d], dgate_r.at[d], place.sibling).wait()

    for q in range(QUARTERS):
        across(0, 0, q).wait_send()
        for d in (0, 1):
            for k in range(1, half + 1):
                if k < half or ((q < QUARTERS // 2) == (d == 0)):
                    along(d, k, q).wait_send()
                    across(d, k, q).wait_send()


def experts(n, mixed_in, d_gathered, gate_rows, wgu, wd, collective_id):
    half, ring = n // 4, n // 2
    rows, width = mixed_in.shape
    blocks = jax.ShapeDtypeStruct((ring, rows, width), bf16)
    hidden_width = wd.shape[0]
    out = pl.pallas_call(
        functools.partial(expert_kernel, n),
        out_shape=[
            jax.ShapeDtypeStruct((rows, width), f32),
            jax.ShapeDtypeStruct((n, 8, rows), f32),
            jax.ShapeDtypeStruct(wgu.shape, bf16),
            jax.ShapeDtypeStruct(wd.shape, bf16),
            blocks,
            blocks,
            blocks,
            blocks,
            jax.ShapeDtypeStruct((n, rows, width), bf16),
        ],
        in_specs=[ANY, ANY, VMEM, VMEM, VMEM],
        out_specs=[VMEM, VMEM, VMEM, VMEM, ANY, ANY, ANY, ANY, ANY],
        scratch_shapes=[
            pltpu.VMEM(wgu.shape, f32),
            pltpu.VMEM(wd.shape, f32),
            pltpu.VMEM((n, 8, rows), f32),
            pltpu.VMEM((n, 8, rows), f32),
            pltpu.VMEM((2, rows, width), bf16),
            pltpu.VMEM((2, rows, width), bf16),
            pltpu.VMEM((2, rows, width), bf16),
            pltpu.VMEM((2, rows, width), bf16),
            DMA((1,)),
            DMA((2, half, QUARTERS)),
            DMA((2, half, QUARTERS)),
            DMA((2, half + 1, QUARTERS)),
            DMA((2, half + 1, QUARTERS)),
            DMA((2, 2)),
            DMA((2, 2)),
            DMA((2, ring)),
            DMA((n,)),
            DMA((n,)),
            DMA((n,)),
            DMA((n,)),
        ]
        + reduce_scratch(rows, width, half, 2),
        compiler_params=pltpu.CompilerParams(
            collective_id=collective_id, has_side_effects=True, vmem_limit_bytes=62 * MB
        ),
    )(mixed_in, d_gathered, gate_rows, wgu, wd)
    return out[:6]


def rotate(values, cosine, sines):
    half_dim = values.shape[-1] // 2
    first_half = values[..., :half_dim]
    second_half = values[..., half_dim:]
    return jnp.concatenate(
        [first_half * cosine - second_half * sines, second_half * cosine + first_half * sines], -1
    )


def rope_tables(length, head_dim):
    half_dim = head_dim // 2
    positions = jnp.arange(length).astype(f32)
    inverse = jnp.power(f32(10000.0), -jnp.arange(half_dim).astype(f32) / half_dim)
    angles = positions[:, None] * inverse[None, :]
    return (jnp.cos(angles)[:, None, :], jnp.sin(angles)[:, None, :])


def dp_sum(value, size):
    if size == 2:
        return value.astype(f32) + lax.ppermute(value, "dp", [(0, 1), (1, 0)]).astype(f32)
    return lax.psum(value, "dp").astype(f32)


def per_device(
    n,
    dp,
    tokens,
    cotangent,
    lengths,
    routes,
    norm1_gain,
    w_query,
    w_kv,
    w_out,
    norm2_gain,
    w_router,
    expert_gate,
    expert_up,
    expert_down,
):
    tok_rows, model_width = tokens.shape
    expert_count = w_router.shape[1]
    head_dim = HD
    kv_width, q_width = w_kv.shape[1], w_query.shape[1]
    kv_count = kv_width // (2 * head_dim)
    head_count = q_width // head_dim
    per_group = head_count // kv_count
    score_scale = head_dim ** (-0.5)
    shard = w_query.shape[0]
    live = (jnp.arange(tok_rows) < lengths[0]).astype(f32)
    d_out_low = (cotangent.astype(f32) * live[:, None]).astype(bf16)
    extra = jnp.concatenate(
        [
            w_router,
            norm1_gain[:, None],
            norm2_gain[:, None],
            jnp.zeros((shard, 128 - expert_count - 2), bf16),
        ],
        axis=1,
    )
    wall, d_gathered = gather(n, [jnp.concatenate([w_query, w_kv, w_out, extra], axis=1), d_out_low], 0)
    wall = wall.reshape(-1, wall.shape[-1])
    edges = [0, q_width, q_width + kv_width, q_width + kv_width + model_width]
    query_w, kv_w, out_w = (wall[:, a:b] for a, b in zip(edges[:-1], edges[1:]))
    router_w = wall[:, edges[3] : edges[3] + expert_count]
    gain_one = wall[:, edges[3] + expert_count].astype(f32)
    gain_two = wall[:, edges[3] + expert_count + 1].astype(f32)

    inputs = tokens.astype(f32)
    inv_one = lax.rsqrt(jnp.mean(inputs * inputs, axis=-1, keepdims=True) + EPSILON)
    normed_one = (inputs * inv_one * gain_one).astype(bf16)
    query_proj = jnp.dot(normed_one, query_w, preferred_element_type=f32)
    kv_proj = jnp.dot(normed_one, kv_w, preferred_element_type=f32)
    cosine, sines = rope_tables(tok_rows, head_dim)
    queries = (
        rotate(query_proj.reshape(tok_rows, head_count, head_dim), cosine, sines)
        .astype(bf16)
        .reshape(tok_rows, kv_count, per_group, head_dim)
    )
    keys = rotate(
        kv_proj[:, : kv_count * head_dim].reshape(tok_rows, kv_count, head_dim), cosine, sines
    ).astype(bf16)
    values = kv_proj[:, kv_count * head_dim :].reshape(tok_rows, kv_count, head_dim).astype(bf16)
    causal = jnp.arange(tok_rows)[:, None] >= jnp.arange(tok_rows)[None, :]

    def masked_scores():
        scores = (
            jnp.einsum("tgjd,ugd->gjtu", queries, keys, preferred_element_type=f32) * score_scale
        )
        return jnp.where(causal[None, None], scores, -1e30)

    masked = masked_scores()
    row_peak = jnp.max(masked, axis=-1, keepdims=True)
    exp_scores = jnp.exp(masked - row_peak)
    row_total = jnp.sum(exp_scores, axis=-1, keepdims=True)
    probs_low = (exp_scores / row_total).astype(bf16)
    attended = (
        jnp.einsum("gjtu,ugd->tgjd", probs_low, values, preferred_element_type=f32)
        .astype(bf16)
        .reshape(tok_rows, head_count * head_dim)
    )
    middle = inputs + jnp.dot(attended, out_w, preferred_element_type=f32)
    inv_two = lax.rsqrt(jnp.mean(middle * middle, axis=-1, keepdims=True) + EPSILON)
    mixed_in = (middle * inv_two * gain_two).astype(bf16)
    logits = jnp.dot(mixed_in, router_w, preferred_element_type=f32)
    chosen = jnp.any(routes[:, :, None] == jnp.arange(expert_count)[None, None, :], axis=1)
    chosen_logits = jnp.where(chosen, logits, -jnp.inf)
    weights = jnp.exp(chosen_logits - jnp.max(chosen_logits, axis=-1, keepdims=True))
    gates = weights / jnp.sum(weights, axis=-1, keepdims=True)

    gate_rows = jnp.broadcast_to(gates.T[:, None, :], (expert_count, 8, tok_rows))
    wgu = jnp.concatenate([expert_gate[0], expert_up[0]], axis=1)
    d_mixed_experts, d_gate_rows, grad_gu, grad_down, own_d, other_d = experts(
        n, mixed_in, d_gathered, gate_rows, wgu, expert_down[0], 1
    )

    turns = [jnp.tile(table.reshape(tok_rows, -1), (1, 4)) for table in (cosine, sines)]
    gains = jnp.concatenate([gain_one[None], gain_two[None], jnp.zeros((6, model_width), f32)])
    output, input_grad, dense_sum = backward(
        n,
        dp,
        own_d,
        other_d,
        wall,
        (
            d_mixed_experts,
            d_gate_rows,
            jnp.pad(gates, ((0, 0), (0, 128 - expert_count))),
            middle,
            mixed_in,
            d_out_low,
            tokens,
            normed_one.T,
            attended.T,
            queries.reshape(tok_rows, -1),
            keys.reshape(tok_rows, -1),
            values.reshape(tok_rows, -1),
            *turns,
            gains,
        ),
        2,
    )
    grad_gu = dp_sum(grad_gu, dp)
    grad_down = dp_sum(grad_down, dp)
    hidden_width = grad_gu.shape[1] // 2
    return (
        output,
        input_grad,
        dense_sum[:, edges[3] + expert_count],
        dense_sum[:, : edges[1]],
        dense_sum[:, edges[1] : edges[2]],
        dense_sum[:, edges[2] : edges[3]],
        dense_sum[:, edges[3] + expert_count + 1],
        dense_sum[:, edges[3] : edges[3] + expert_count],
        grad_gu[None, :, :hidden_width],
        grad_gu[None, :, hidden_width:],
        grad_down[None],
    )


def solution(mesh):
    rows, own = P(("dp", "expert"), None), P("expert", None)
    expert = P("expert", None, None)
    return jax.shard_map(
        functools.partial(per_device, mesh.shape["expert"], mesh.shape["dp"]),
        mesh=mesh,
        in_specs=(rows, rows, P(("dp", "expert")), rows, P("expert"), own, own, own, P("expert"), own)
        + (expert,) * 3,
        out_specs=(rows, rows, P("expert"), own, own, own, P("expert"), own) + (expert,) * 3,
        check_vma=False,
    )
```

```python
import functools

import jax
import jax.numpy as jnp
from jax import lax
from jax.experimental import pallas as pl
from jax.experimental.pallas import tpu as pltpu
from jax.sharding import PartitionSpec as P

HD = 64
EPSILON = 1e-05
MESH = pl.DeviceIdType.MESH
ANY = pl.BlockSpec(memory_space=pl.ANY)
VMEM = pl.BlockSpec(memory_space=pltpu.VMEM)
DMA = pltpu.SemaphoreType.DMA
MB = 2**20
f32 = jnp.float32
bf16 = jnp.bfloat16


def mul(a, b, ca, cb):
    return lax.dot_general(a, b, (((ca,), (cb,)), ((), ())), preferred_element_type=f32)


class Place:
    def __init__(self, n):
        self.n, self.mid, self.ring = n, n // 8, n // 2
        self.half = self.ring // 2
        self.me = lax.axis_index("expert")
        self.chip, self.core = lax.div(self.me, 2), lax.rem(self.me, 2)
        outer, inner = lax.div(self.chip, self.mid), lax.rem(self.chip, self.mid)
        row = 3 - outer
        step = jnp.where(lax.rem(row, 2) == 0, inner - 1, self.mid - 1 - inner)
        self.at = jnp.where(inner == 0, outer, 4 + row * (self.mid - 1) + step)
        self.sibling = self.chip * 2 + 1 - self.core
        self.right, self.left = self.device(1), self.device(-1)

    def chip_at(self, distance):
        p = lax.rem(self.at + distance + self.ring, self.ring)
        wide = max(self.mid - 1, 1)
        row, k = lax.div(lax.max(p - 4, 0), wide), lax.rem(lax.max(p - 4, 0), wide)
        inner = jnp.where(lax.rem(row, 2) == 0, 1 + k, self.mid - 1 - k)
        return jnp.where(p < 4, p * self.mid, (3 - row) * self.mid + inner)

    def device(self, distance):
        return self.chip_at(distance) * 2 + self.core


def remote(src, dst, send, recv, device):
    return pltpu.make_async_remote_copy(
        src_ref=src, dst_ref=dst, send_sem=send, recv_sem=recv, device_id={"expert": device}, device_id_type=MESH
    )


def meet(targets):
    barrier = pltpu.get_barrier_semaphore()
    for target in targets:
        pl.semaphore_signal(barrier, inc=1, device_id={"expert": target}, device_id_type=MESH)
    pl.semaphore_wait(barrier, len(targets))


def meet_all(place):
    barrier = pltpu.get_barrier_semaphore()

    @pl.loop(1, place.n)
    def _(d):
        other = lax.rem(place.me + d, place.n)
        pl.semaphore_signal(barrier, inc=1, device_id={"expert": other}, device_id_type=MESH)

    pl.semaphore_wait(barrier, place.n - 1)


def column_cuts(width, parts):
    tiles = width // 128
    edges = [128 * (tiles * i // parts) for i in range(parts + 1)]
    return [(edges[i], edges[i + 1] - edges[i]) for i in range(parts)]


def forward_kernel(
    n,
    wall_ref,
    dout_ref,
    tokens_ref,
    chosen_ref,
    cos_ref,
    sin_ref,
    wallg_ref,
    doutg_ref,
    q_ref,
    k_ref,
    v_ref,
    normed_t_ref,
    attended_t_ref,
    middle_ref,
    mixed_ref,
    gates_ref,
    gate_rows_ref,
    gains_ref,
    weights,
    out_w,
    proj,
    attended,
    own_sem,
    load_sem,
    ss,
    rs,
    css,
    crs,
):
    place = Place(n)
    half, me = place.half, place.me
    rows, width = tokens_ref.shape
    shard = wall_ref.shape[0]
    q_width, kv_width = q_ref.shape[1], 2 * k_ref.shape[1]
    qkv_width = q_width + kv_width
    near = qkv_width + 128
    meet((place.right, place.left, place.sibling))
    started = []

    def begin(copy):
        copy.start()
        started.append(copy)

    flows = (
        (wall_ref, wallg_ref, column_cuts(near, 2), weights),
        (wall_ref, wallg_ref, [(near + s, z) for s, z in column_cuts(width, 2)], out_w),
        (dout_ref, doutg_ref, column_cuts(width, 2), None),
    )

    def part(a, ref, q):
        return ref.at[:, pl.ds(*flows[a][2][q])]

    def block_at(d, k):
        return me if k == 0 else (place.device(-k) if d == 0 else place.device(k))

    def along(a, d, k, q):
        x_ref, o_ref = flows[a][:2]
        b = block_at(d, k - 1)
        return remote(
            part(a, x_ref if k == 1 else o_ref.at[b], q),
            part(a, o_ref.at[b], q),
            ss.at[a, d, k - 1, q],
            rs.at[a, d, k - 1, q],
            place.right if d == 0 else place.left,
        )

    def across(a, d, k, q):
        x_ref, o_ref = flows[a][:2]
        b = block_at(d, k)
        return remote(
            part(a, x_ref if k == 0 else o_ref.at[b], q),
            part(a, o_ref.at[b], q),
            css.at[a, d, k, q],
            crs.at[a, d, k, q],
            place.sibling,
        )

    def take(a, b, q, src=None):
        x_ref, o_ref, cuts, local = flows[a]
        if local is not None:
            start, size = cuts[q]
            at = pl.ds(pl.multiple_of(b * shard, 16), shard)
            pltpu.make_async_copy(
                part(a, o_ref.at[b] if src is None else src, q),
                local.at[at, pl.ds(start - cuts[0][0], size)],
                load_sem.at[a],
            ).start()

    def first(a):
        for q in range(2):
            begin(along(a, 0, 1, q))
            begin(along(a, 1, 1, 1 - q))
            begin(across(a, 0, 0, q))
            take(a, me, q, flows[a][0])

    def sibling_of(b):
        return b + 1 - 2 * lax.rem(b, 2)

    def met(a, k):
        for q in range(2):
            for d in (0, 1):
                if (k == 0 and d == 0) or (k > 0 and goes(d, k, q, half, 2)):
                    b = sibling_of(block_at(d, k))
                    o_ref = flows[a][1]
                    piece = part(a, o_ref.at[b], q)
                    remote(piece, piece, css.at[a, d, k, q], crs.at[a, d, k, q], place.sibling).wait_recv()
                    take(a, b, q)

    def flow():
        first(0)
        for a in range(len(flows)):
            for k in range(2, half + 2):
                for i in range(2):
                    for d in (0, 1):
                        q = i if d == 0 else 1 - i
                        if goes(d, k - 1, q, half, 2):
                            along(a, d, k - 1, q).wait_recv()
                            if k <= half and goes(d, k, q, half, 2):
                                begin(along(a, d, k, q))
                            begin(across(a, d, k - 1, q))
                            take(a, block_at(d, k - 1), q)
                            yield
                if k == half and a + 1 < len(flows):
                    first(a + 1)
                met(a, k - 2)
            met(a, half - 0)
            yield

    per_flow = (half - 1) * 4 + 2 + 1
    moving = flow()
    done = [0]

    def pump(steps):
        while done[0] < steps:
            next(moving)
            done[0] += 1

    own = [
        pltpu.make_async_copy(x_ref, o_ref.at[me], own_sem.at[i])
        for i, (x_ref, o_ref) in enumerate(((wall_ref, wallg_ref), (dout_ref, doutg_ref)))
    ]
    pump(1)
    for copy in own:
        copy.start()
    pump(per_flow)
    pltpu.make_async_copy(weights, weights, load_sem.at[0]).wait()

    lane = lax.broadcasted_iota(jnp.int32, (rows, 128), 1)
    turned = jnp.transpose(weights[:, pl.ds(qkv_width, 128)].astype(f32))
    gains_ref[...] = jnp.concatenate([turned[n : n + 1], turned[n + 1 : n + 2], jnp.zeros((6, width), f32)], axis=0)
    inputs = tokens_ref[...].astype(f32)
    inv = lax.rsqrt(jnp.mean(inputs * inputs, axis=1, keepdims=True) + EPSILON)
    normed = (inputs * inv * gains_ref[0:1]).astype(bf16)
    proj[...] = mul(normed, weights[:, pl.ds(0, qkv_width)], 1, 0)
    normed_t_ref[...] = jnp.transpose(normed)
    cosine, sine = cos_ref[...], sin_ref[...]
    sine_on = jnp.where(lane % HD < HD // 2, -sine, sine)

    def turn(at):
        block = proj[:, at]
        return (block * cosine + swap_halves(block, lane) * sine_on).astype(bf16)

    for b in range(q_width // 128):
        q_ref[:, pl.ds(128 * b, 128)] = turn(pl.ds(128 * b, 128))
    for b in range(kv_width // 256):
        k_ref[:, pl.ds(128 * b, 128)] = turn(pl.ds(q_width + 128 * b, 128))
    v_ref[...] = proj[:, pl.ds(q_width + kv_width // 2, kv_width // 2)].astype(bf16)
    t_at = lax.broadcasted_iota(jnp.int32, (rows, rows), 0)
    u_at = lax.broadcasted_iota(jnp.int32, (rows, rows), 1)
    causal = t_at >= u_at
    kv_count = k_ref.shape[1] // HD
    per_group = q_width // HD // kv_count
    kept = None
    for g in range(kv_count):
        pair = pl.ds(128 * (g // 2), 128)
        k_parts = head_halves(k_ref[:, pair].astype(f32), lane, g % 2)
        v_parts = head_halves(v_ref[:, pair].astype(f32), lane, g % 2)
        for h in range(per_group * g, per_group * (g + 1)):
            at = pl.ds(128 * (h // 2), 128)
            probs = softmax_rows(q_ref[:, at], k_parts[h % 2], causal).astype(bf16)
            kept_new = mul(probs, v_parts[h % 2], 1, 0)
            if h % 2 == 0:
                kept = kept_new
            else:
                attended[:, at] = (kept + kept_new).astype(bf16)
        pump(per_flow + per_flow * (g + 1) // kv_count)
    attended_t_ref[...] = jnp.transpose(attended[...])
    pltpu.make_async_copy(out_w, out_w, load_sem.at[1]).wait()
    middle_ref[...] = tokens_ref[...].astype(f32) + mul(attended[...], out_w[...], 1, 0)
    tile = 32

    @pl.loop(0, rows // tile)
    def _(r):
        at = pl.ds(pl.multiple_of(r * tile, tile), tile)
        middle = middle_ref[at]
        scale = lax.rsqrt(jnp.mean(middle * middle, axis=1, keepdims=True) + EPSILON)
        mixed_ref[at] = (middle * scale * gains_ref[1:2]).astype(bf16)

    logits = mul(mixed_ref[...], weights[:, pl.ds(qkv_width, 128)], 1, 0)
    chosen = chosen_ref[...] > 0
    logits = jnp.where(chosen, logits, -1e30)
    e = jnp.where(chosen, jnp.exp(logits - jnp.max(logits, axis=1, keepdims=True)), 0.0)
    gates = e / jnp.sum(e, axis=1, keepdims=True)
    gates_ref[...] = gates
    across_gates = jnp.transpose(gates)
    for e in range(n):
        gate_rows_ref[e] = jnp.broadcast_to(across_gates[e : e + 1], (8, rows))
    for _ in moving:
        pass
    for copy in own:
        copy.wait()
    for copy in started:
        copy.wait_send()


def forward(n, wall, d_out, tokens, chosen, turns, q_width, kv_width, collective_id):
    half = n // 4
    rows, width = tokens.shape
    shard, full_width = wall.shape
    near = q_width + kv_width + 128
    shape = jax.ShapeDtypeStruct
    return pl.pallas_call(
        functools.partial(forward_kernel, n),
        out_shape=[
            shape((n, shard, full_width), bf16),
            shape((n, rows, width), bf16),
            shape((rows, q_width), bf16),
            shape((rows, kv_width // 2), bf16),
            shape((rows, kv_width // 2), bf16),
            shape((width, rows), bf16),
            shape((q_width, rows), bf16),
            shape((rows, width), f32),
            shape((rows, width), bf16),
            shape((rows, 128), f32),
            shape((n, 8, rows), f32),
            shape((8, width), f32),
        ],
        in_specs=[ANY] * 2 + [VMEM] * 4,
        out_specs=[ANY] * 2 + [VMEM] * 10,
        scratch_shapes=[
            pltpu.VMEM((width, near), bf16),
            pltpu.VMEM((q_width, width), bf16),
            pltpu.VMEM((rows, q_width + kv_width), f32),
            pltpu.VMEM((rows, q_width), bf16),
            DMA((2,)),
            DMA((2,)),
            DMA((3, 2, half, 2)),
            DMA((3, 2, half, 2)),
            DMA((3, 2, half + 1, 2)),
            DMA((3, 2, half + 1, 2)),
        ],
        compiler_params=pltpu.CompilerParams(
            collective_id=collective_id, has_side_effects=True, vmem_limit_bytes=56 * MB
        ),
    )(wall, d_out, tokens, chosen, *turns)


SLOTS = 4


def ring_work(half, parts):
    work = []
    for k in range(half, 0, -1):
        for i in range(parts):
            for d in (0, 1):
                q = i if d == 0 else parts - 1 - i
                if goes(d, k, q, half, parts):
                    work.append((d, k, q))
    return work + [(None, 0, q) for q in range(parts)]


def goes(d, k, q, half, parts):
    return k < half or ((q < parts // 2) == (d == 0))


def widest(width, parts):
    return max(w for _, w in column_cuts(width, parts))


def reduce_scratch(rows, width, half, parts):
    return [
        pltpu.VMEM((2, half, rows, width), bf16),
        pltpu.VMEM((SLOTS, rows, widest(width, parts)), bf16),
        pltpu.VMEM((SLOTS, rows, widest(width, parts)), bf16),
        DMA((SLOTS,)),
        DMA((SLOTS,)),
        DMA((SLOTS,)),
        DMA((2, half, parts)),
    ]


def ring_reduce(place, own_at, other_at, other_wait, width, write, scratch):
    arrived, mine, theirs, mine_sem, theirs_sem, send_sem, recv_sem = scratch
    half = place.half
    parts = recv_sem.shape[2]
    cuts = column_cuts(width, parts)
    rows = arrived.shape[2]
    tile = 16
    work = ring_work(half, parts)

    def chip_of(d, k):
        return place.chip_at(k if d != 1 else -k)

    def loads(i):
        d, k, q = work[i]
        slot, chip, (start, size) = i % SLOTS, chip_of(d, k), cuts[q]
        return (
            pltpu.make_async_copy(
                own_at(chip).at[:, pl.ds(start, size)], mine.at[slot, :, pl.ds(0, size)], mine_sem.at[slot]
            ),
            pltpu.make_async_copy(
                other_at(chip).at[:, pl.ds(start, size)], theirs.at[slot, :, pl.ds(0, size)], theirs_sem.at[slot]
            ),
        )

    def send(i):
        d, k, q = work[i]
        start, size = cuts[q]
        return remote(
            mine.at[i % SLOTS, :, pl.ds(0, size)],
            arrived.at[d, k - 1, :, pl.ds(start, size)],
            send_sem.at[i % SLOTS],
            recv_sem.at[d, k - 1, q],
            place.right if d == 0 else place.left,
        )

    waited = set()

    def fetch(i):
        if i >= len(work):
            return
        d, k, q = work[i]
        if i >= SLOTS:
            send(i - SLOTS).wait_send()
        key = (0 if k in (0, half) else d, k)
        if key not in waited:
            waited.add(key)
            other_wait(chip_of(d, k))
        for copy in loads(i):
            copy.start()

    ahead = SLOTS // 2
    for i in range(ahead):
        fetch(i)
    for i, (d, k, q) in enumerate(work):
        fetch(i + ahead)
        for copy in loads(i):
            copy.wait()
        start, size = cuts[q]
        slot = i % SLOTS
        come = []
        for dd in (0, 1) if d is None else (d,):
            if k + 1 <= half and goes(dd, k + 1, q, half, parts):
                piece = arrived.at[dd, k, :, pl.ds(start, size)]
                remote(piece, piece, send_sem.at[slot], recv_sem.at[dd, k, q], place.sibling).wait_recv()
                come.append(dd)

        @pl.loop(0, rows // tile)
        def _(r):
            at = pl.ds(pl.multiple_of(r * tile, tile), tile)
            total = mine[slot, at, pl.ds(0, size)].astype(f32) + theirs[slot, at, pl.ds(0, size)].astype(f32)
            for dd in come:
                total += arrived[dd, k, at, pl.ds(start, size)].astype(f32)
            if d is None:
                write(at, pl.ds(start, size), total)
            else:
                mine[slot, at, pl.ds(0, size)] = total.astype(bf16)

        if d is not None:
            send(i).start()
        yield
    sends = len(work) - parts
    for i in range(max(0, len(work) - SLOTS), sends):
        send(i).wait_send()


DENSE_PARTS = 4


def swap_halves(values, lane):
    width = values.shape[1]
    return jnp.where(lane % HD < HD // 2, pltpu.roll(values, width - HD // 2, 1), pltpu.roll(values, HD // 2, 1))


def head_halves(block, lane, low):
    turned = pltpu.roll(block, HD, 1)
    lower, upper = (block, turned) if low == 0 else (turned, block)
    zero = jnp.zeros_like(block)
    return jnp.where(lane < HD, lower, zero).astype(bf16), jnp.where(lane < HD, zero, upper).astype(bf16)


def softmax_rows(q, k, causal):
    scores = jnp.where(causal, mul(q, k, 1, 1) * HD**-0.5, -1e30)
    e = jnp.exp(scores - jnp.max(scores, axis=1, keepdims=True))
    return e * (1.0 / jnp.sum(e, axis=1, keepdims=True))


def backward_kernel(
    n,
    dp,
    od_ref,
    sd_ref,
    wall_ref,
    dmix_ref,
    dgate_ref,
    gates_ref,
    middle_ref,
    mixed_ref,
    dout_ref,
    tokens_ref,
    normed_t_ref,
    attended_t_ref,
    q_ref,
    k_ref,
    v_ref,
    cos_ref,
    sin_ref,
    gains_ref,
    output_ref,
    input_grad_ref,
    dense_ref,
    weights,
    extra_w,
    d_middle,
    d_middle_low,
    d_att,
    d_qkv,
    d_normed,
    extra,
    logits_low,
    own_f,
    stage_f,
    other_f,
    come_f,
    copies_f,
    weight_sem,
    stage_sem,
    other_sem,
    send_f,
    recv_f,
    copy_s,
    copy_r,
    *scratch_d,
):
    place = Place(n)
    half, ring = place.half, place.ring
    rank = lax.axis_index("dp")
    rows, width = middle_ref.shape
    q_width, kv_width = q_ref.shape[1], 2 * k_ref.shape[1]
    qkv_width = q_width + kv_width
    shard = own_f.shape[1]
    full_width = own_f.shape[2]
    barrier = pltpu.get_barrier_semaphore()
    for target in (place.right, place.left, place.sibling):
        pl.semaphore_signal(barrier, inc=1, device_id={"expert": target}, device_id_type=MESH)
    for turn in range(1, dp):
        pl.semaphore_signal(barrier, inc=1, device_id={"dp": lax.rem(rank + turn, dp)}, device_id_type=MESH)
    out_w = pltpu.make_async_copy(
        wall_ref.at[:, pl.ds(qkv_width + 128, width)], weights.at[:, pl.ds(0, width)], weight_sem.at[0]
    )
    extra_copy = pltpu.make_async_copy(wall_ref.at[:, pl.ds(qkv_width, 128)], extra_w, weight_sem.at[1])
    qkv_w = pltpu.make_async_copy(wall_ref.at[:, pl.ds(0, qkv_width)], weights, weight_sem.at[2])
    out_w.start()
    extra_copy.start()
    pl.semaphore_wait(barrier, 3 + dp - 1)

    def write_output(at, columns, total):
        output_ref[at, columns] = (middle_ref[at, columns] + total).astype(bf16)

    background = ring_reduce(
        place, lambda chip: od_ref.at[chip], lambda chip: sd_ref.at[chip], lambda chip: None, width, write_output, scratch_d
    )
    items = len(ring_work(half, scratch_d[6].shape[2]))
    done = [0]

    def pump(share):
        while done[0] < min(items, int(items * share + 0.5)):
            next(background)
            done[0] += 1

    pump(0.07)
    d_rows = jnp.concatenate([dgate_ref[:, 0, :], jnp.zeros((128 - n, rows), f32)], axis=0)
    d_gates = jnp.transpose(d_rows)
    gates = gates_ref[...]
    d_sel = gates * (d_gates - jnp.sum(gates * d_gates, axis=1, keepdims=True))
    logits_low[...] = d_sel.astype(bf16)
    extra_copy.wait()
    d_normed[...] = mul(logits_low[...], extra_w[...], 1, 1)
    gain_one, gain_two = gains_ref[0:1], gains_ref[1:2]
    tile = 32

    @pl.loop(0, rows // tile)
    def _(r):
        at = pl.ds(pl.multiple_of(r * tile, tile), tile)
        middle = middle_ref[at]
        d_mixed = dmix_ref[at] + d_normed[at]
        inv = lax.rsqrt(jnp.mean(middle * middle, axis=1, keepdims=True) + EPSILON)
        scaled = d_mixed * gain_two
        back = jnp.mean(scaled * middle, axis=1, keepdims=True)
        total = dout_ref[at].astype(f32) + inv * scaled - middle * (inv * inv * inv * back)
        d_middle[at] = total
        d_middle_low[at] = total.astype(bf16)
        d_att[at] = (d_mixed * middle * inv).astype(bf16)

    lane = lax.broadcasted_iota(jnp.int32, (rows, 128), 1)
    extra[...] = mul(mixed_ref[...], logits_low[...], 0, 0) + mul(
        d_att[...], (lane == n + 1).astype(bf16), 0, 0
    )
    pump(0.14)
    out_w.wait()
    d_att[...] = mul(d_middle_low[...], weights[:, pl.ds(0, width)], 1, 1).astype(bf16)
    qkv_w.start()
    pump(0.21)

    t_at = lax.broadcasted_iota(jnp.int32, (rows, rows), 0)
    u_at = lax.broadcasted_iota(jnp.int32, (rows, rows), 1)
    causal = t_at >= u_at
    cosine, sine = cos_ref[...], sin_ref[...]
    sine_back = jnp.where(lane % HD < HD // 2, sine, -sine)
    kv_count = k_ref.shape[1] // HD
    per_group = q_width // HD // kv_count
    d_normed[...] = jnp.zeros_like(d_normed)
    pair_k, pair_v = None, None
    for g in range(kv_count):
        pair = pl.ds(128 * (g // 2), 128)
        k_parts = head_halves(k_ref[:, pair].astype(f32), lane, g % 2)
        v_parts = head_halves(v_ref[:, pair].astype(f32), lane, g % 2)
        d_k, d_v = [None, None], [None, None]
        for h in range(per_group * g, per_group * (g + 1)):
            at = pl.ds(128 * (h // 2), 128)
            low = h % 2
            query, d_a = q_ref[:, at], d_att[:, at]
            probs = softmax_rows(query, k_parts[low], causal)
            probs_low = probs.astype(bf16)
            d_probs = mul(d_a, v_parts[low], 1, 1)
            weighted = probs * d_probs
            d_scores = (weighted - probs * jnp.sum(weighted, axis=1, keepdims=True)).astype(bf16)
            d_normed[:, at] += mul(d_scores, k_parts[low], 1, 0)
            step_k, step_v = mul(d_scores, query, 0, 0), mul(probs_low, d_a, 0, 0)
            d_k[low] = step_k if d_k[low] is None else d_k[low] + step_k
            d_v[low] = step_v if d_v[low] is None else d_v[low] + step_v

        def gathered(parts):
            stay, turn = parts[g % 2], parts[1 - g % 2]
            return stay if turn is None else (pltpu.roll(turn, HD, 1) if stay is None else stay + pltpu.roll(turn, HD, 1))

        if g % 2 == 0:
            pair_k, pair_v = gathered(d_k), gathered(d_v)
        if g % 2 == 1 or g + 1 == kv_count:
            total_k = jnp.where(lane < HD, pair_k, gathered(d_k)) * HD**-0.5
            total_v = jnp.where(lane < HD, pair_v, gathered(d_v))
            turned = total_k * cosine + swap_halves(total_k, lane) * sine_back
            d_qkv[:, pl.ds(q_width + 128 * (g // 2), 128)] = turned.astype(bf16)
            d_qkv[:, pl.ds(q_width + kv_width // 2 + 128 * (g // 2), 128)] = total_v.astype(bf16)
        pump(0.21 + 0.6 * (g + 1) / kv_count)
    for b in range(q_width // 128):
        at = pl.ds(128 * b, 128)
        total = d_normed[:, at] * HD**-0.5
        d_qkv[:, at] = (total * cosine + swap_halves(total, lane) * sine_back).astype(bf16)
    pump(0.85)
    qkv_w.wait()
    d_normed[...] = mul(d_qkv[...], weights[...], 1, 1)

    @pl.loop(0, rows // tile)
    def _(r):
        at = pl.ds(pl.multiple_of(r * tile, tile), tile)
        inputs = tokens_ref[at].astype(f32)
        d = d_normed[at]
        inv = lax.rsqrt(jnp.mean(inputs * inputs, axis=1, keepdims=True) + EPSILON)
        scaled = d * gain_one
        back = jnp.mean(scaled * inputs, axis=1, keepdims=True)
        total = d_middle[at] + inv * scaled - inputs * (inv * inv * inv * back)
        input_grad_ref[at] = total.astype(bf16)
        d_att[at] = (d * inputs * inv).astype(bf16)

    extra[...] += mul(d_att[...], (lane == n).astype(bf16), 0, 0)
    pump(1.0)
    for _ in background:
        pass

    def cross(chip, slot):
        return remote(stage_f.at[slot], other_f.at[chip], stage_sem.at[slot], other_sem.at[chip], place.sibling)

    def fill(ref, device):
        at = pl.ds(pl.multiple_of(device * shard, 16), shard)
        ref[:, pl.ds(0, qkv_width)] = mul(normed_t_ref[at], d_qkv[...], 1, 0).astype(bf16)
        ref[:, pl.ds(qkv_width, 128)] = extra[at].astype(bf16)
        ref[:, pl.ds(qkv_width + 128, width)] = mul(attended_t_ref[at], d_middle_low[...], 1, 0).astype(bf16)

    @pl.loop(0, ring)
    def _(i):
        away = half - lax.div(i + 1, 2)
        chip = place.chip_at(jnp.where(lax.rem(i, 2) == 0, away, -away))
        slot = lax.rem(i, 2)

        @pl.when(i >= 2)
        def _():
            cross(chip, slot).wait_send()

        fill(stage_f.at[slot], chip * 2 + 1 - place.core)
        cross(chip, slot).start()
        fill(own_f.at[chip], chip * 2 + place.core)

    for slot in range(2):
        cross(place.chip, slot).wait_send()
    cuts = column_cuts(full_width, DENSE_PARTS)
    work = ring_work(half, DENSE_PARTS)

    def send(d, k, q):
        chip = place.chip_at(k if d == 0 else -k)
        at = pl.ds(*cuts[q])
        return remote(
            own_f.at[chip, :, at],
            come_f.at[d, k - 1, :, at],
            send_f.at[d, k - 1, q],
            recv_f.at[d, k - 1, q],
            place.right if d == 0 else place.left,
        )

    def spread(turn, q):
        at = pl.ds(*cuts[q])
        return pltpu.make_async_remote_copy(
            src_ref=copies_f.at[rank, :, at],
            dst_ref=copies_f.at[rank, :, at],
            send_sem=copy_s.at[turn, q],
            recv_sem=copy_r.at[turn, q],
            device_id={"dp": lax.rem(rank + turn, dp)},
            device_id_type=MESH,
        )

    met = set()
    for d, k, q in work:
        chip = place.chip_at(0 if d is None else (k if d == 0 else -k))
        key = (0 if k in (0, half) else d, k)
        if key not in met:
            met.add(key)
            remote(other_f.at[chip], other_f.at[chip], stage_sem.at[0], other_sem.at[chip], place.sibling).wait_recv()
        at = pl.ds(*cuts[q])
        total = own_f[chip, :, at].astype(f32) + other_f[chip, :, at].astype(f32)
        for dd in (0, 1) if d is None else (d,):
            if k + 1 <= half and goes(dd, k + 1, q, half, DENSE_PARTS):
                piece = come_f.at[dd, k, :, at]
                remote(piece, piece, send_f.at[dd, k, q], recv_f.at[dd, k, q], place.sibling).wait_recv()
                total += piece[...].astype(f32)
        if d is not None:
            own_f[chip, :, at] = total.astype(bf16)
            send(d, k, q).start()
        else:
            copies_f[rank, :, at] = total.astype(bf16)
            for turn in range(1, dp):
                spread(turn, q).start()
    for q in range(DENSE_PARTS):
        for turn in range(1, dp):
            spread(turn, q).wait()
        at = pl.ds(*cuts[q])
        total = copies_f[0, :, at].astype(f32)
        for r in range(1, dp):
            total += copies_f[r, :, at].astype(f32)
        dense_ref[:, at] = total
    for d, k, q in work:
        if d is not None:
            send(d, k, q).wait_send()


def backward(n, dp, own_d, other_d, wall, others, collective_id):
    half, ring = n // 4, n // 2
    rows, width = own_d.shape[1:]
    full_width = wall.shape[1]
    qkv_width = full_width - width - 128
    shard = wall.shape[0] // n
    q_width = others[9].shape[1]
    return pl.pallas_call(
        functools.partial(backward_kernel, n, dp),
        out_shape=[
            jax.ShapeDtypeStruct((rows, width), bf16),
            jax.ShapeDtypeStruct((rows, width), bf16),
            jax.ShapeDtypeStruct((shard, full_width), f32),
        ],
        in_specs=[ANY] * 3 + [VMEM] * len(others),
        out_specs=[VMEM] * 3,
        scratch_shapes=[
            pltpu.VMEM((width, qkv_width), bf16),
            pltpu.VMEM((width, 128), bf16),
            pltpu.VMEM((rows, width), f32),
            pltpu.VMEM((rows, width), bf16),
            pltpu.VMEM((rows, q_width), bf16),
            pltpu.VMEM((rows, qkv_width), bf16),
            pltpu.VMEM((rows, width), f32),
            pltpu.VMEM((width, 128), f32),
            pltpu.VMEM((rows, 128), bf16),
            pltpu.VMEM((ring, shard, full_width), bf16),
            pltpu.VMEM((2, shard, full_width), bf16),
            pltpu.VMEM((ring, shard, full_width), bf16),
            pltpu.VMEM((2, half, shard, full_width), bf16),
            pltpu.VMEM((dp, shard, full_width), bf16),
            DMA((3,)),
            DMA((2,)),
            DMA((ring,)),
            DMA((2, half, DENSE_PARTS)),
            DMA((2, half, DENSE_PARTS)),
            DMA((dp, DENSE_PARTS)),
            DMA((dp, DENSE_PARTS)),
        ]
        + reduce_scratch(rows, width, half, 4),
        compiler_params=pltpu.CompilerParams(
            collective_id=collective_id, has_side_effects=True, vmem_limit_bytes=63 * MB
        ),
    )(own_d, other_d, wall, *others)


QUARTERS = 4


def expert_kernel(
    n,
    x_ref,
    dog_ref,
    gates_ref,
    wgu_ref,
    wd_ref,
    de_ref,
    dgates_ref,
    ggu_ref,
    gd_ref,
    od_ref,
    sd_ref,
    oe_ref,
    se_ref,
    xg_ref,
    hg_ref,
    acc_gu,
    acc_d,
    gate_in,
    dgate_out,
    xbuf,
    dobuf,
    pd,
    pe,
    hbuf,
    own_sem,
    ring_s,
    ring_r,
    cross_s,
    cross_r,
    load_sem,
    put_sem,
    sib_r,
    gate_s,
    gate_r,
    dgate_s,
    dgate_r,
    *reduce_refs,
):
    place = Place(n)
    half, ring, me = place.half, place.ring, place.me
    rows, width = x_ref.shape
    hidden_width = wd_ref.shape[0]
    piece = rows // QUARTERS
    meet_all(place)

    own = pltpu.make_async_copy(xbuf.at[0], xg_ref.at[me], own_sem.at[0])

    def at(q):
        return pl.ds(pl.multiple_of(q * piece, piece), piece)

    def block_of(d, k):
        return jnp.where(d == 0, place.device(-k), place.device(k))

    def along(d, k, q, first=False):
        b = me if first else block_of(d, k - 1)
        return remote(
            x_ref.at[at(q)] if first else xg_ref.at[b, at(q)],
            xg_ref.at[b, at(q)],
            ring_s.at[d, k - 1, q],
            ring_r.at[d, k - 1, q],
            jnp.where(d == 0, place.right, place.left),
        )

    def across(d, k, q, first=False):
        b = me if first else block_of(d, k)
        src = x_ref.at[at(q)] if first else xg_ref.at[b, at(q)]
        return remote(src, xg_ref.at[b, at(q)], cross_s.at[d, k, q], cross_r.at[d, k, q], place.sibling)

    def gate_copy(d):
        to = lax.rem(me + d, n)
        return remote(gates_ref.at[to], gate_in.at[me], gate_s.at[d], gate_r.at[d], to)

    for q in range(QUARTERS):
        for d in (0, 1):
            along(d, 1, q, first=True).start()
        across(0, 0, q, first=True).start()

    @pl.loop(1, n)
    def _(d):
        gate_copy(d).start()

    gate_in[me] = gates_ref[me]
    acc_gu[...] = jnp.zeros_like(acc_gu)
    acc_d[...] = jnp.zeros_like(acc_d)

    def step_of(i):
        k = jnp.where(i < 2, 0, lax.div(i + 2, 4))
        j = jnp.where(i < 2, i, lax.rem(i + 2, 4))
        edge = jnp.logical_or(k == 0, k == half)
        d = jnp.where(edge, 0, lax.rem(j, 2))
        other = jnp.where(edge, j, lax.div(j, 2))
        chip = jnp.where(d == 0, place.chip_at(-k), place.chip_at(k))
        core = jnp.where(other == 0, place.core, 1 - place.core)
        return k, j, d, other, chip, chip * 2 + core

    def pump(d, k, q, last=False):
        along(d, k, q).wait_recv()
        if not last:
            near = jnp.where(q < QUARTERS // 2, 0, 1) == d

            @pl.when(jnp.logical_or(k + 1 < half, near))
            def _():
                along(d, k + 1, q).start()

        across(d, k, q).start()

    def load(block, slot):
        return (
            pltpu.make_async_copy(xg_ref.at[block], xbuf.at[slot], load_sem.at[0, slot]),
            pltpu.make_async_copy(dog_ref.at[block], dobuf.at[slot], load_sem.at[1, slot]),
        )

    def put_wait(slot):
        for which, buf in enumerate((pd, pe, hbuf)):
            pltpu.make_async_copy(buf.at[slot], buf.at[slot], put_sem.at[which, slot]).wait()

    def dgate_copy(block):
        d = lax.rem(block - me + n, n)
        return remote(dgate_out.at[block], dgates_ref.at[me], dgate_s.at[d], dgate_r.at[d], block)

    def load_rest(block, slot):
        return (
            pltpu.make_async_copy(xg_ref.at[block], xbuf.at[slot], load_sem.at[0, slot]),
            pltpu.make_async_copy(dog_ref.at[block], dobuf.at[slot], load_sem.at[1, slot]),
            pltpu.make_async_copy(hg_ref.at[block], hbuf.at[slot], load_sem.at[2, slot]),
        )

    pltpu.make_async_copy(x_ref, xbuf.at[0], load_sem.at[0, 0]).start()
    pltpu.make_async_copy(dog_ref.at[me], dobuf.at[0], load_sem.at[1, 0]).start()

    @pl.loop(0, n)
    def _(i):
        k, j, d, other, chip, block = step_of(i)
        slot = lax.rem(i, 2)
        for copy in load(block, slot):
            copy.wait()

        @pl.when(i == 0)
        def _():
            own.start()

        @pl.when(i > 0)
        def _():
            away = lax.rem(me - block + n, n)
            remote(gate_in.at[block], gate_in.at[block], gate_s.at[away], gate_r.at[away], place.sibling).wait_recv()

        gate = jnp.transpose(gate_in[block])[:, :1]
        x = xbuf[slot]
        gu = mul(x, wgu_ref[...], 1, 0)
        g, u = gu[:, :hidden_width], gu[:, hidden_width:]
        s = 1.0 / (1.0 + jnp.exp(-g))
        gs = g * s
        hid = gs * u
        hidg = (hid * gate).astype(bf16)

        @pl.when(i >= 2)
        def _():
            put_wait(slot)

        pd[slot] = mul(hidg, wd_ref[...], 1, 0).astype(bf16)

        @pl.when(i < 2)
        def _():
            for t in range(2):
                for dd in (0, 1):
                    pump(dd, 1, i * 2 + t)

        @pl.when(jnp.logical_and(i >= 2, k + 1 < half))
        def _():
            for dd in (0, 1):
                pump(dd, k + 1, j)

        @pl.when(k + 1 == half)
        def _():
            pump(jnp.where(j < QUARTERS // 2, 0, 1), half, j, last=True)

        nk, nj, nd, nother, nchip, nblock = step_of(i + 1)

        @pl.when(jnp.logical_and(i + 1 < n, nother == 1))
        def _():
            for q in range(QUARTERS):
                dd = jnp.where(nk == half, 0 if q < QUARTERS // 2 else 1, nd)
                b = nblock
                remote(
                    xg_ref.at[b, at(q)], xg_ref.at[b, at(q)], cross_s.at[dd, nk, q], cross_r.at[dd, nk, q], place.sibling
                ).wait_recv()

        @pl.when(i == 0)
        def _():
            own.wait()

        @pl.when(i + 1 < n)
        def _():
            for copy in load(nblock, 1 - slot):
                copy.start()

        do = dobuf[slot]
        dh = mul(do, wd_ref[...], 1, 1)
        dgate = jnp.sum(dh * hid, axis=1, keepdims=True)
        dgate_out[block] = jnp.transpose(jnp.broadcast_to(dgate, (rows, 128)))[:8]
        dh = dh * gate
        d_g = (dh * u * s * (1.0 + g * (1.0 - s))).astype(bf16)
        d_u = (dh * gs).astype(bf16)
        dgu = jnp.concatenate([d_g, d_u], axis=1)
        hbuf[slot] = jnp.concatenate([d_g, d_u, hidg], axis=1)
        pltpu.make_async_copy(hbuf.at[slot], hg_ref.at[block], put_sem.at[2, slot]).start()
        pe[slot] = mul(dgu, wgu_ref[...], 1, 1).astype(bf16)

        @pl.when(i > 0)
        def _():
            dgate_copy(block).start()

        @pl.when(i == 0)
        def _():
            dgates_ref[me] = dgate_out[me]

        @pl.when(other == 0)
        def _():
            pltpu.make_async_copy(pd.at[slot], od_ref.at[chip], put_sem.at[0, slot]).start()
            pltpu.make_async_copy(pe.at[slot], oe_ref.at[chip], put_sem.at[1, slot]).start()

        @pl.when(other == 1)
        def _():
            remote(pd.at[slot], sd_ref.at[chip], put_sem.at[0, slot], sib_r.at[0, chip], place.sibling).start()
            remote(pe.at[slot], se_ref.at[chip], put_sem.at[1, slot], sib_r.at[1, chip], place.sibling).start()

    put_wait(0)
    put_wait(1)

    def other_wait(chip):
        remote(se_ref.at[chip], se_ref.at[chip], put_sem.at[1, 0], sib_r.at[1, chip], place.sibling).wait_recv()

    def write(at, columns, total):
        de_ref[at, columns] = total

    for copy in load_rest(0, 0):
        copy.start()

    def gradients(first, last):
        @pl.loop(first, last)
        def _(b):
            slot = lax.rem(b, 2)
            for copy in load_rest(b, slot):
                copy.wait()

            @pl.when(b + 1 < n)
            def _():
                for copy in load_rest(b + 1, 1 - slot):
                    copy.start()

            acc_gu[...] += mul(xbuf[slot], hbuf[slot, :, pl.ds(0, 2 * hidden_width)], 0, 0)
            acc_d[...] += mul(hbuf[slot, :, pl.ds(2 * hidden_width, hidden_width)], dobuf[slot], 0, 0)

    steps = len(ring_work(half, 2)) // 2
    back = ring_reduce(
        place, lambda chip: oe_ref.at[chip], lambda chip: se_ref.at[chip], other_wait, width, write, reduce_refs
    )
    for step in range(steps):
        next(back)
        next(back)
        gradients(n * step // steps, n * (step + 1) // steps)
    for _ in back:
        pass
    ggu_ref[...] = acc_gu[...].astype(bf16)
    gd_ref[...] = acc_d[...].astype(bf16)

    @pl.loop(0, ring)
    def _(chip):
        remote(sd_ref.at[chip], sd_ref.at[chip], put_sem.at[0, 0], sib_r.at[0, chip], place.sibling).wait_recv()

    @pl.loop(1, n)
    def _(d):
        gate_copy(d).wait_send()
        source = lax.rem(me - d + n, n)
        remote(dgates_ref.at[source], dgates_ref.at[source], dgate_s.at[d], dgate_r.at[d], place.sibling).wait()

    for q in range(QUARTERS):
        across(0, 0, q, first=True).wait_send()
        for d in (0, 1):
            for k in range(1, half + 1):
                if k < half or ((q < QUARTERS // 2) == (d == 0)):
                    along(d, k, q).wait_send()
                    across(d, k, q).wait_send()


def experts(n, mixed_in, d_gathered, gate_rows, wgu, wd, collective_id):
    half, ring = n // 4, n // 2
    rows, width = mixed_in.shape
    blocks = jax.ShapeDtypeStruct((ring, rows, width), bf16)
    hidden_width = wd.shape[0]
    out = pl.pallas_call(
        functools.partial(expert_kernel, n),
        out_shape=[
            jax.ShapeDtypeStruct((rows, width), f32),
            jax.ShapeDtypeStruct((n, 8, rows), f32),
            jax.ShapeDtypeStruct(wgu.shape, bf16),
            jax.ShapeDtypeStruct(wd.shape, bf16),
            blocks,
            blocks,
            blocks,
            blocks,
            jax.ShapeDtypeStruct((n, rows, width), bf16),
            jax.ShapeDtypeStruct((n, rows, 3 * hidden_width), bf16),
        ],
        in_specs=[ANY, ANY, VMEM, VMEM, VMEM],
        out_specs=[VMEM, VMEM, VMEM, VMEM, ANY, ANY, ANY, ANY, ANY, ANY],
        scratch_shapes=[
            pltpu.VMEM(wgu.shape, f32),
            pltpu.VMEM(wd.shape, f32),
            pltpu.VMEM((n, 8, rows), f32),
            pltpu.VMEM((n, 8, rows), f32),
            pltpu.VMEM((2, rows, width), bf16),
            pltpu.VMEM((2, rows, width), bf16),
            pltpu.VMEM((2, rows, width), bf16),
            pltpu.VMEM((2, rows, width), bf16),
            pltpu.VMEM((2, rows, 3 * hidden_width), bf16),
            DMA((1,)),
            DMA((2, half, QUARTERS)),
            DMA((2, half, QUARTERS)),
            DMA((2, half + 1, QUARTERS)),
            DMA((2, half + 1, QUARTERS)),
            DMA((3, 2)),
            DMA((3, 2)),
            DMA((2, ring)),
            DMA((n,)),
            DMA((n,)),
            DMA((n,)),
            DMA((n,)),
        ]
        + reduce_scratch(rows, width, half, 2),
        compiler_params=pltpu.CompilerParams(
            collective_id=collective_id, has_side_effects=True, vmem_limit_bytes=62 * MB
        ),
    )(mixed_in, d_gathered, gate_rows, wgu, wd)
    return out[:6]


def rope_tables(length, head_dim):
    half_dim = head_dim // 2
    positions = jnp.arange(length).astype(f32)
    inverse = jnp.power(f32(10000.0), -jnp.arange(half_dim).astype(f32) / half_dim)
    angles = positions[:, None] * inverse[None, :]
    return (jnp.cos(angles)[:, None, :], jnp.sin(angles)[:, None, :])


def dp_sum(value, size):
    if size == 2:
        return value.astype(f32) + lax.ppermute(value, "dp", [(0, 1), (1, 0)]).astype(f32)
    return lax.psum(value, "dp").astype(f32)


def per_device(
    n,
    dp,
    tokens,
    cotangent,
    lengths,
    routes,
    norm1_gain,
    w_query,
    w_kv,
    w_out,
    norm2_gain,
    w_router,
    expert_gate,
    expert_up,
    expert_down,
):
    tok_rows, model_width = tokens.shape
    expert_count = w_router.shape[1]
    head_dim = HD
    kv_width, q_width = w_kv.shape[1], w_query.shape[1]
    qkv_width = q_width + kv_width
    shard = w_query.shape[0]
    live = (jnp.arange(tok_rows) < lengths[0]).astype(f32)
    d_out_low = (cotangent.astype(f32) * live[:, None]).astype(bf16)
    extra = jnp.concatenate(
        [
            w_router,
            norm1_gain[:, None],
            norm2_gain[:, None],
            jnp.zeros((shard, 128 - expert_count - 2), bf16),
        ],
        axis=1,
    )
    chosen = jnp.any(routes[:, :, None] == jnp.arange(128)[None, None, :], axis=1).astype(f32)
    cosine, sines = rope_tables(tok_rows, head_dim)
    turns = [jnp.tile(table.reshape(tok_rows, -1), (1, 4)) for table in (cosine, sines)]
    wall = jnp.concatenate([w_query, w_kv, extra, w_out], axis=1)
    (wall, d_gathered, queries, keys, values, normed_t, attended_t, middle, mixed_in, gates, gate_rows, gains) = forward(
        n, wall, d_out_low, tokens, chosen, turns, q_width, kv_width, 0
    )
    wall = wall.reshape(-1, wall.shape[-1])
    wgu = jnp.concatenate([expert_gate[0], expert_up[0]], axis=1)
    d_mixed_experts, d_gate_rows, grad_gu, grad_down, own_d, other_d = experts(
        n, mixed_in, d_gathered, gate_rows, wgu, expert_down[0], 1
    )

    output, input_grad, dense_sum = backward(
        n,
        dp,
        own_d,
        other_d,
        wall,
        (
            d_mixed_experts,
            d_gate_rows,
            gates,
            middle,
            mixed_in,
            d_out_low,
            tokens,
            normed_t,
            attended_t,
            queries,
            keys,
            values,
            *turns,
            gains,
        ),
        2,
    )
    grad_gu = dp_sum(grad_gu, dp)
    grad_down = dp_sum(grad_down, dp)
    hidden_width = grad_gu.shape[1] // 2
    return (
        output,
        input_grad,
        dense_sum[:, qkv_width + expert_count],
        dense_sum[:, :q_width],
        dense_sum[:, q_width:qkv_width],
        dense_sum[:, qkv_width + 128 :],
        dense_sum[:, qkv_width + expert_count + 1],
        dense_sum[:, qkv_width : qkv_width + expert_count],
        grad_gu[None, :, :hidden_width],
        grad_gu[None, :, hidden_width:],
        grad_down[None],
    )


def solution(mesh):
    rows, own = P(("dp", "expert"), None), P("expert", None)
    expert = P("expert", None, None)
    return jax.shard_map(
        functools.partial(per_device, mesh.shape["expert"], mesh.shape["dp"]),
        mesh=mesh,
        in_specs=(rows, rows, P(("dp", "expert")), rows, P("expert"), own, own, own, P("expert"), own)
        + (expert,) * 3,
        out_specs=(rows, rows, P("expert"), own, own, own, P("expert"), own) + (expert,) * 3,
        check_vma=False,
    )
```

```python
import functools

import jax
import jax.numpy as jnp
import numpy as np
from jax import lax
from jax.experimental import pallas as pl
from jax.experimental.pallas import tpu as pltpu
from jax.sharding import PartitionSpec as P

HD = 64
EPSILON = 1e-05
MESH = pl.DeviceIdType.MESH
ANY = pl.BlockSpec(memory_space=pl.ANY)
VMEM = pl.BlockSpec(memory_space=pltpu.VMEM)
DMA = pltpu.SemaphoreType.DMA
MB = 2**20
f32 = jnp.float32
bf16 = jnp.bfloat16


def mul(a, b, ca, cb):
    return lax.dot_general(a, b, (((ca,), (cb,)), ((), ())), preferred_element_type=f32)


class Place:
    def __init__(self, n):
        self.n, self.mid, self.ring = n, n // 8, n // 2
        self.half = self.ring // 2
        self.me = lax.axis_index("expert")
        self.chip, self.core = lax.div(self.me, 2), lax.rem(self.me, 2)
        outer, inner = lax.div(self.chip, self.mid), lax.rem(self.chip, self.mid)
        row = 3 - outer
        step = jnp.where(lax.rem(row, 2) == 0, inner - 1, self.mid - 1 - inner)
        self.at = jnp.where(inner == 0, outer, 4 + row * (self.mid - 1) + step)
        self.sibling = self.chip * 2 + 1 - self.core
        self.right, self.left = self.device(1), self.device(-1)

    def chip_at(self, distance):
        p = lax.rem(self.at + distance + self.ring, self.ring)
        wide = max(self.mid - 1, 1)
        row, k = lax.div(lax.max(p - 4, 0), wide), lax.rem(lax.max(p - 4, 0), wide)
        inner = jnp.where(lax.rem(row, 2) == 0, 1 + k, self.mid - 1 - k)
        return jnp.where(p < 4, p * self.mid, (3 - row) * self.mid + inner)

    def device(self, distance):
        return self.chip_at(distance) * 2 + self.core


def remote(src, dst, send, recv, device):
    return pltpu.make_async_remote_copy(
        src_ref=src, dst_ref=dst, send_sem=send, recv_sem=recv, device_id={"expert": device}, device_id_type=MESH
    )


def meet(targets):
    barrier = pltpu.get_barrier_semaphore()
    for target in targets:
        pl.semaphore_signal(barrier, inc=1, device_id={"expert": target}, device_id_type=MESH)
    pl.semaphore_wait(barrier, len(targets))


def meet_all(place):
    barrier = pltpu.get_barrier_semaphore()

    @pl.loop(1, place.n)
    def _(d):
        other = lax.rem(place.me + d, place.n)
        pl.semaphore_signal(barrier, inc=1, device_id={"expert": other}, device_id_type=MESH)

    pl.semaphore_wait(barrier, place.n - 1)


def column_cuts(width, parts):
    tiles = width // 128
    edges = [128 * (tiles * i // parts) for i in range(parts + 1)]
    return [(edges[i], edges[i + 1] - edges[i]) for i in range(parts)]


def forward_kernel(
    n,
    w_query_ref,
    w_kv_ref,
    w_extra_ref,
    w_out_ref,
    lengths_ref,
    cotangent_ref,
    tokens_ref,
    routes_ref,
    cos_ref,
    sin_ref,
    wallg_ref,
    doutg_ref,
    dout_ref,
    q_ref,
    k_ref,
    v_ref,
    normed_t_ref,
    attended_t_ref,
    middle_ref,
    mixed_ref,
    gates_ref,
    gate_rows_ref,
    gains_ref,
    wall_ref,
    weights,
    out_w,
    proj,
    attended,
    own_sem,
    piece_sem,
    load_sem,
    ss,
    rs,
    css,
    crs,
):
    place = Place(n)
    half, me = place.half, place.me
    rows, width = tokens_ref.shape
    shard = wall_ref.shape[0]
    q_width, kv_width = q_ref.shape[1], 2 * k_ref.shape[1]
    qkv_width = q_width + kv_width
    near = qkv_width + 128
    edges = (0, q_width, qkv_width, near, near + width)
    pieces = [
        pltpu.make_async_copy(ref, wall_ref.at[:, pl.ds(edges[i], edges[i + 1] - edges[i])], piece_sem.at[i])
        for i, ref in enumerate((w_query_ref, w_kv_ref, w_extra_ref, w_out_ref))
    ]
    for copy in pieces:
        copy.start()
    meet((place.right, place.left, place.sibling))
    for copy in pieces:
        copy.wait()
    started = []

    def begin(copy):
        copy.start()
        started.append(copy)

    flows = (
        (wall_ref, wallg_ref, column_cuts(near, 2), weights),
        (wall_ref, wallg_ref, [(near + s, z) for s, z in column_cuts(width, 2)], out_w),
        (dout_ref, doutg_ref, column_cuts(width, 2), None),
    )

    def part(a, ref, q):
        return ref.at[:, pl.ds(*flows[a][2][q])]

    def block_at(d, k):
        return me if k == 0 else (place.device(-k) if d == 0 else place.device(k))

    def along(a, d, k, q):
        x_ref, o_ref = flows[a][:2]
        b = block_at(d, k - 1)
        return remote(
            part(a, x_ref if k == 1 else o_ref.at[b], q),
            part(a, o_ref.at[b], q),
            ss.at[a, d, k - 1, q],
            rs.at[a, d, k - 1, q],
            place.right if d == 0 else place.left,
        )

    def across(a, d, k, q):
        x_ref, o_ref = flows[a][:2]
        b = block_at(d, k)
        return remote(
            part(a, x_ref if k == 0 else o_ref.at[b], q),
            part(a, o_ref.at[b], q),
            css.at[a, d, k, q],
            crs.at[a, d, k, q],
            place.sibling,
        )

    def take(a, b, q, src=None):
        x_ref, o_ref, cuts, local = flows[a]
        if local is not None:
            start, size = cuts[q]
            at = pl.ds(pl.multiple_of(b * shard, 16), shard)
            pltpu.make_async_copy(
                part(a, o_ref.at[b] if src is None else src, q),
                local.at[at, pl.ds(start - cuts[0][0], size)],
                load_sem.at[a],
            ).start()

    def first(a):
        for q in range(2):
            begin(along(a, 0, 1, q))
            begin(along(a, 1, 1, 1 - q))
            begin(across(a, 0, 0, q))
            take(a, me, q, flows[a][0])

    def sibling_of(b):
        return b + 1 - 2 * lax.rem(b, 2)

    def met(a, k):
        for q in range(2):
            for d in (0, 1):
                if (k == 0 and d == 0) or (k > 0 and goes(d, k, q, half, 2)):
                    b = sibling_of(block_at(d, k))
                    o_ref = flows[a][1]
                    piece = part(a, o_ref.at[b], q)
                    remote(piece, piece, css.at[a, d, k, q], crs.at[a, d, k, q], place.sibling).wait_recv()
                    take(a, b, q)

    def flow():
        first(0)
        for a in range(len(flows)):
            for k in range(2, half + 2):
                for i in range(2):
                    for d in (0, 1):
                        q = i if d == 0 else 1 - i
                        if goes(d, k - 1, q, half, 2):
                            along(a, d, k - 1, q).wait_recv()
                            if k <= half and goes(d, k, q, half, 2):
                                begin(along(a, d, k, q))
                            begin(across(a, d, k - 1, q))
                            take(a, block_at(d, k - 1), q)
                            yield
                if k == half and a + 1 < len(flows):
                    first(a + 1)
                met(a, k - 2)
            met(a, half - 0)
            yield

    per_flow = (half - 1) * 4 + 2 + 1
    moving = flow()
    done = [0]

    def pump(steps):
        while done[0] < steps:
            next(moving)
            done[0] += 1

    own = [
        pltpu.make_async_copy(x_ref, o_ref.at[me], own_sem.at[i])
        for i, (x_ref, o_ref) in enumerate(((wall_ref, wallg_ref), (dout_ref, doutg_ref)))
    ]
    alive = lax.broadcasted_iota(jnp.int32, (rows, width), 0) < lengths_ref[0]
    dout_ref[...] = jnp.where(alive, cotangent_ref[...].astype(f32), 0.0).astype(bf16)
    pump(1)
    for copy in own:
        copy.start()
    pump(per_flow)
    pltpu.make_async_copy(weights, weights, load_sem.at[0]).wait()

    lane = lax.broadcasted_iota(jnp.int32, (rows, 128), 1)
    turned = jnp.transpose(weights[:, pl.ds(qkv_width, 128)].astype(f32))
    gains_ref[...] = jnp.concatenate([turned[n : n + 1], turned[n + 1 : n + 2], jnp.zeros((6, width), f32)], axis=0)
    inputs = tokens_ref[...].astype(f32)
    inv = lax.rsqrt(jnp.mean(inputs * inputs, axis=1, keepdims=True) + EPSILON)
    normed = (inputs * inv * gains_ref[0:1]).astype(bf16)
    proj[...] = mul(normed, weights[:, pl.ds(0, qkv_width)], 1, 0)
    normed_t_ref[...] = jnp.transpose(normed)
    cosine, sine = cos_ref[...], sin_ref[...]
    sine_on = jnp.where(lane % HD < HD // 2, -sine, sine)

    def turn(at):
        block = proj[:, at]
        return (block * cosine + swap_halves(block, lane) * sine_on).astype(bf16)

    for b in range(q_width // 128):
        q_ref[:, pl.ds(128 * b, 128)] = turn(pl.ds(128 * b, 128))
    for b in range(kv_width // 256):
        k_ref[:, pl.ds(128 * b, 128)] = turn(pl.ds(q_width + 128 * b, 128))
    v_ref[...] = proj[:, pl.ds(q_width + kv_width // 2, kv_width // 2)].astype(bf16)
    t_at = lax.broadcasted_iota(jnp.int32, (rows, rows), 0)
    u_at = lax.broadcasted_iota(jnp.int32, (rows, rows), 1)
    causal = t_at >= u_at
    kv_count = k_ref.shape[1] // HD
    per_group = q_width // HD // kv_count
    kept = None
    for g in range(kv_count):
        pair = pl.ds(128 * (g // 2), 128)
        k_parts = head_halves(k_ref[:, pair].astype(f32), lane, g % 2)
        v_parts = head_halves(v_ref[:, pair].astype(f32), lane, g % 2)
        for h in range(per_group * g, per_group * (g + 1)):
            at = pl.ds(128 * (h // 2), 128)
            probs = softmax_rows(q_ref[:, at], k_parts[h % 2], causal).astype(bf16)
            kept_new = mul(probs, v_parts[h % 2], 1, 0)
            if h % 2 == 0:
                kept = kept_new
            else:
                attended[:, at] = (kept + kept_new).astype(bf16)
        pump(per_flow + per_flow * (g + 1) // kv_count)
    attended_t_ref[...] = jnp.transpose(attended[...])
    pltpu.make_async_copy(out_w, out_w, load_sem.at[1]).wait()
    middle_ref[...] = tokens_ref[...].astype(f32) + mul(attended[...], out_w[...], 1, 0)
    tile = 32

    @pl.loop(0, rows // tile)
    def _(r):
        at = pl.ds(pl.multiple_of(r * tile, tile), tile)
        middle = middle_ref[at]
        scale = lax.rsqrt(jnp.mean(middle * middle, axis=1, keepdims=True) + EPSILON)
        mixed_ref[at] = (middle * scale * gains_ref[1:2]).astype(bf16)

    logits = mul(mixed_ref[...], weights[:, pl.ds(qkv_width, 128)], 1, 0)
    chosen = lane == routes_ref[:, 0:1]
    for choice in range(1, routes_ref.shape[1]):
        chosen = jnp.logical_or(chosen, lane == routes_ref[:, choice : choice + 1])
    logits = jnp.where(chosen, logits, -1e30)
    e = jnp.where(chosen, jnp.exp(logits - jnp.max(logits, axis=1, keepdims=True)), 0.0)
    gates = e / jnp.sum(e, axis=1, keepdims=True)
    gates_ref[...] = gates
    across_gates = jnp.transpose(gates)
    for e in range(n):
        gate_rows_ref[e] = jnp.broadcast_to(across_gates[e : e + 1], (8, rows))
    for _ in moving:
        pass
    for copy in own:
        copy.wait()
    for copy in started:
        copy.wait_send()


def forward(n, w_query, w_kv, w_extra, w_out, lengths, cotangent, tokens, routes, turns, collective_id):
    half = n // 4
    rows, width = tokens.shape
    shard, q_width = w_query.shape
    kv_width = w_kv.shape[1]
    full_width = q_width + kv_width + 128 + width
    near = q_width + kv_width + 128
    shape = jax.ShapeDtypeStruct
    return pl.pallas_call(
        functools.partial(forward_kernel, n),
        out_shape=[
            shape((n, shard, full_width), bf16),
            shape((n, rows, width), bf16),
            shape((rows, width), bf16),
            shape((rows, q_width), bf16),
            shape((rows, kv_width // 2), bf16),
            shape((rows, kv_width // 2), bf16),
            shape((width, rows), bf16),
            shape((q_width, rows), bf16),
            shape((rows, width), f32),
            shape((rows, width), bf16),
            shape((rows, 128), f32),
            shape((n, 8, rows), f32),
            shape((8, width), f32),
        ],
        in_specs=[ANY] * 4 + [pl.BlockSpec(memory_space=pltpu.SMEM)] + [VMEM] * 5,
        out_specs=[ANY] * 2 + [VMEM] * 11,
        scratch_shapes=[
            pltpu.VMEM((shard, full_width), bf16),
            pltpu.VMEM((width, near), bf16),
            pltpu.VMEM((q_width, width), bf16),
            pltpu.VMEM((rows, q_width + kv_width), f32),
            pltpu.VMEM((rows, q_width), bf16),
            DMA((2,)),
            DMA((4,)),
            DMA((2,)),
            DMA((3, 2, half, 2)),
            DMA((3, 2, half, 2)),
            DMA((3, 2, half + 1, 2)),
            DMA((3, 2, half + 1, 2)),
        ],
        compiler_params=pltpu.CompilerParams(
            collective_id=collective_id, has_side_effects=True, vmem_limit_bytes=56 * MB
        ),
    )(w_query, w_kv, w_extra, w_out, lengths, cotangent, tokens, routes, *turns)


SLOTS = 4


def ring_work(half, parts):
    work = []
    for k in range(half, 0, -1):
        for q in range(parts):
            for d in (0, 1):
                if goes(d, k, q, half, parts):
                    work.append((d, k, q))
    return work + [(None, 0, q) for q in range(parts)]


def goes(d, k, q, half, parts):
    return k < half or ((q < parts // 2) == (d == 0))


def widest(width, parts):
    return max(w for _, w in column_cuts(width, parts))


def reduce_scratch(rows, width, half, parts):
    return [
        pltpu.VMEM((2, half, rows, width), bf16),
        pltpu.VMEM((SLOTS, rows, widest(width, parts)), bf16),
        pltpu.VMEM((SLOTS, rows, widest(width, parts)), bf16),
        DMA((SLOTS,)),
        DMA((SLOTS,)),
        DMA((SLOTS,)),
        DMA((2, half, parts)),
    ]


def ring_reduce(place, own_at, other_at, other_wait, width, write, scratch, first=0):
    arrived, mine, theirs, mine_sem, theirs_sem, send_sem, recv_sem = scratch
    half = place.half
    parts = recv_sem.shape[2]
    cuts = column_cuts(width, parts)
    rows = arrived.shape[2]
    tile = 16
    work = ring_work(half, parts)

    def chip_of(d, k):
        return place.chip_at(k if d != 1 else -k)

    def loads(i):
        d, k, q = work[i]
        slot, chip, (start, size) = i % SLOTS, chip_of(d, k), cuts[q]
        return (
            pltpu.make_async_copy(
                own_at(chip).at[:, pl.ds(start, size)], mine.at[slot, :, pl.ds(0, size)], mine_sem.at[slot]
            ),
            pltpu.make_async_copy(
                other_at(chip).at[:, pl.ds(start, size)], theirs.at[slot, :, pl.ds(0, size)], theirs_sem.at[slot]
            ),
        )

    def send(i):
        d, k, q = work[i]
        start, size = cuts[q]
        return remote(
            mine.at[i % SLOTS, :, pl.ds(0, size)],
            arrived.at[d, k - 1, :, pl.ds(start, size)],
            send_sem.at[i % SLOTS],
            recv_sem.at[d, k - 1, q],
            place.right if d == 0 else place.left,
        )

    waited = set()
    fetched = [0]

    def fetch(last):
        while fetched[0] <= min(last, len(work) - 1):
            fetch_one(fetched[0])
            fetched[0] += 1

    def fetch_one(i):
        d, k, q = work[i]
        if i >= SLOTS:
            send(i - SLOTS).wait_send()
        key = (0 if k in (0, half) else d, k)
        if key not in waited:
            waited.add(key)
            other_wait(chip_of(d, k))
        for copy in loads(i):
            copy.start()

    ahead = SLOTS // 2
    for i, (d, k, q) in enumerate(work):
        fetch(i + ahead if i >= first else min(i + ahead, first - 1))
        for copy in loads(i):
            copy.wait()
        start, size = cuts[q]
        slot = i % SLOTS
        come = []
        for dd in (0, 1) if d is None else (d,):
            if k + 1 <= half and goes(dd, k + 1, q, half, parts):
                piece = arrived.at[dd, k, :, pl.ds(start, size)]
                remote(piece, piece, send_sem.at[slot], recv_sem.at[dd, k, q], place.sibling).wait_recv()
                come.append(dd)

        @pl.loop(0, rows // tile)
        def _(r):
            at = pl.ds(pl.multiple_of(r * tile, tile), tile)
            total = mine[slot, at, pl.ds(0, size)].astype(f32) + theirs[slot, at, pl.ds(0, size)].astype(f32)
            for dd in come:
                total += arrived[dd, k, at, pl.ds(start, size)].astype(f32)
            if d is None:
                write(at, pl.ds(start, size), total)
            else:
                mine[slot, at, pl.ds(0, size)] = total.astype(bf16)

        if d is not None:
            send(i).start()
        yield
    sends = len(work) - parts
    for i in range(max(0, len(work) - SLOTS), sends):
        send(i).wait_send()


DENSE_PARTS = 4


def swap_halves(values, lane):
    width = values.shape[1]
    return jnp.where(lane % HD < HD // 2, pltpu.roll(values, width - HD // 2, 1), pltpu.roll(values, HD // 2, 1))


def head_halves(block, lane, low):
    turned = pltpu.roll(block, HD, 1)
    lower, upper = (block, turned) if low == 0 else (turned, block)
    zero = jnp.zeros_like(block)
    return jnp.where(lane < HD, lower, zero).astype(bf16), jnp.where(lane < HD, zero, upper).astype(bf16)


def softmax_rows(q, k, causal):
    scores = jnp.where(causal, mul(q, k, 1, 1) * HD**-0.5, -1e30)
    e = jnp.exp(scores - jnp.max(scores, axis=1, keepdims=True))
    return e * (1.0 / jnp.sum(e, axis=1, keepdims=True))


def backward_kernel(
    n,
    dp,
    od_ref,
    sd_ref,
    wall_ref,
    ggu_ref,
    gd_ref,
    dmix_ref,
    dgate_ref,
    gates_ref,
    middle_ref,
    mixed_ref,
    dout_ref,
    tokens_ref,
    normed_t_ref,
    attended_t_ref,
    q_ref,
    k_ref,
    v_ref,
    cos_ref,
    sin_ref,
    gains_ref,
    output_ref,
    input_grad_ref,
    dense_ref,
    ggu_sum,
    gd_sum,
    ggu_in,
    gd_in,
    weights,
    extra_w,
    d_middle,
    d_middle_low,
    d_att,
    d_qkv,
    d_normed,
    extra,
    logits_low,
    own_f,
    stage_f,
    other_f,
    come_f,
    copies_f,
    weight_sem,
    stage_sem,
    other_sem,
    send_f,
    recv_f,
    copy_s,
    copy_r,
    expert_s,
    expert_r,
    tile_in,
    tile_out,
    *scratch_d,
):
    place = Place(n)
    half, ring = place.half, place.ring
    rank = lax.axis_index("dp")
    rows, width = middle_ref.shape
    q_width, kv_width = q_ref.shape[1], 2 * k_ref.shape[1]
    qkv_width = q_width + kv_width
    shard = own_f.shape[1]
    full_width = own_f.shape[2]
    barrier = pltpu.get_barrier_semaphore()
    for target in (place.right, place.left, place.sibling):
        pl.semaphore_signal(barrier, inc=1, device_id={"expert": target}, device_id_type=MESH)
    for turn in range(1, dp):
        pl.semaphore_signal(barrier, inc=1, device_id={"dp": lax.rem(rank + turn, dp)}, device_id_type=MESH)
    out_w = pltpu.make_async_copy(
        wall_ref.at[:, pl.ds(qkv_width + 128, width)], weights.at[:, pl.ds(0, width)], weight_sem.at[0]
    )
    extra_copy = pltpu.make_async_copy(wall_ref.at[:, pl.ds(qkv_width, 128)], extra_w, weight_sem.at[1])
    qkv_w = pltpu.make_async_copy(wall_ref.at[:, pl.ds(0, qkv_width)], weights, weight_sem.at[2])
    out_w.start()
    extra_copy.start()
    pl.semaphore_wait(barrier, 3 + dp - 1)

    hidden_width = ggu_ref.shape[1] // 2
    tiles = [(ggu_ref, ggu_in, r) for r in range(0, ggu_ref.shape[0], rows)]
    tiles += [(gd_ref, gd_in, r) for r in range(0, gd_ref.shape[0], rows)]

    def spread_tile(turn, t):
        own, come, r = tiles[t]
        return pltpu.make_async_remote_copy(
            src_ref=own.at[pl.ds(r, rows)],
            dst_ref=come.at[rank, pl.ds(r, rows)],
            send_sem=expert_s.at[turn, t],
            recv_sem=expert_r.at[turn, t],
            device_id={"dp": lax.rem(rank + turn, dp)},
            device_id_type=MESH,
        )

    for t in range(len(tiles)):
        for turn in range(1, dp):
            spread_tile(turn, t).start()

    def write_output(at, columns, total):
        output_ref[at, columns] = (middle_ref[at, columns] + total).astype(bf16)

    background = ring_reduce(
        place, lambda chip: od_ref.at[chip], lambda chip: sd_ref.at[chip], lambda chip: None, width, write_output, scratch_d
    )
    items = len(ring_work(half, scratch_d[6].shape[2]))
    done = [0]

    def pump(share):
        while done[0] < min(items, int(items * share + 0.5)):
            next(background)
            done[0] += 1

    pump(0.06)
    d_rows = jnp.concatenate([dgate_ref[:, 0, :], jnp.zeros((128 - n, rows), f32)], axis=0)
    d_gates = jnp.transpose(d_rows)
    gates = gates_ref[...]
    d_sel = gates * (d_gates - jnp.sum(gates * d_gates, axis=1, keepdims=True))
    logits_low[...] = d_sel.astype(bf16)
    extra_copy.wait()
    d_normed[...] = mul(logits_low[...], extra_w[...], 1, 1)
    gain_one, gain_two = gains_ref[0:1], gains_ref[1:2]
    tile = 32

    @pl.loop(0, rows // tile)
    def _(r):
        at = pl.ds(pl.multiple_of(r * tile, tile), tile)
        middle = middle_ref[at]
        d_mixed = dmix_ref[at] + d_normed[at]
        inv = lax.rsqrt(jnp.mean(middle * middle, axis=1, keepdims=True) + EPSILON)
        scaled = d_mixed * gain_two
        back = jnp.mean(scaled * middle, axis=1, keepdims=True)
        total = dout_ref[at].astype(f32) + inv * scaled - middle * (inv * inv * inv * back)
        d_middle[at] = total
        d_middle_low[at] = total.astype(bf16)
        d_att[at] = (d_mixed * middle * inv).astype(bf16)

    lane = lax.broadcasted_iota(jnp.int32, (rows, 128), 1)
    extra[...] = mul(mixed_ref[...], logits_low[...], 0, 0) + mul(
        d_att[...], (lane == n + 1).astype(bf16), 0, 0
    )
    pump(0.12)
    out_w.wait()
    d_att[...] = mul(d_middle_low[...], weights[:, pl.ds(0, width)], 1, 1).astype(bf16)
    qkv_w.start()
    pump(0.18)

    t_at = lax.broadcasted_iota(jnp.int32, (rows, rows), 0)
    u_at = lax.broadcasted_iota(jnp.int32, (rows, rows), 1)
    causal = t_at >= u_at
    cosine, sine = cos_ref[...], sin_ref[...]
    sine_back = jnp.where(lane % HD < HD // 2, sine, -sine)
    kv_count = k_ref.shape[1] // HD
    per_group = q_width // HD // kv_count
    d_normed[...] = jnp.zeros_like(d_normed)
    pair_k, pair_v = None, None
    for g in range(kv_count):
        pair = pl.ds(128 * (g // 2), 128)
        k_parts = head_halves(k_ref[:, pair].astype(f32), lane, g % 2)
        v_parts = head_halves(v_ref[:, pair].astype(f32), lane, g % 2)
        d_k, d_v = [None, None], [None, None]
        for h in range(per_group * g, per_group * (g + 1)):
            at = pl.ds(128 * (h // 2), 128)
            low = h % 2
            query, d_a = q_ref[:, at], d_att[:, at]
            probs = softmax_rows(query, k_parts[low], causal)
            probs_low = probs.astype(bf16)
            d_probs = mul(d_a, v_parts[low], 1, 1)
            weighted = probs * d_probs
            d_scores = (weighted - probs * jnp.sum(weighted, axis=1, keepdims=True)).astype(bf16)
            d_normed[:, at] += mul(d_scores, k_parts[low], 1, 0)
            step_k, step_v = mul(d_scores, query, 0, 0), mul(probs_low, d_a, 0, 0)
            d_k[low] = step_k if d_k[low] is None else d_k[low] + step_k
            d_v[low] = step_v if d_v[low] is None else d_v[low] + step_v

        def gathered(parts):
            stay, turn = parts[g % 2], parts[1 - g % 2]
            return stay if turn is None else (pltpu.roll(turn, HD, 1) if stay is None else stay + pltpu.roll(turn, HD, 1))

        if g % 2 == 0:
            pair_k, pair_v = gathered(d_k), gathered(d_v)
        if g % 2 == 1 or g + 1 == kv_count:
            total_k = jnp.where(lane < HD, pair_k, gathered(d_k)) * HD**-0.5
            total_v = jnp.where(lane < HD, pair_v, gathered(d_v))
            turned = total_k * cosine + swap_halves(total_k, lane) * sine_back
            d_qkv[:, pl.ds(q_width + 128 * (g // 2), 128)] = turned.astype(bf16)
            d_qkv[:, pl.ds(q_width + kv_width // 2 + 128 * (g // 2), 128)] = total_v.astype(bf16)
        pump(0.18 + 0.3 * (g + 1) / kv_count)
    for b in range(q_width // 128):
        at = pl.ds(128 * b, 128)
        total = d_normed[:, at] * HD**-0.5
        d_qkv[:, at] = (total * cosine + swap_halves(total, lane) * sine_back).astype(bf16)
    pump(0.53)
    qkv_w.wait()
    d_normed[...] = mul(d_qkv[...], weights[...], 1, 1)

    @pl.loop(0, rows // tile)
    def _(r):
        at = pl.ds(pl.multiple_of(r * tile, tile), tile)
        inputs = tokens_ref[at].astype(f32)
        d = d_normed[at]
        inv = lax.rsqrt(jnp.mean(inputs * inputs, axis=1, keepdims=True) + EPSILON)
        scaled = d * gain_one
        back = jnp.mean(scaled * inputs, axis=1, keepdims=True)
        total = d_middle[at] + inv * scaled - inputs * (inv * inv * inv * back)
        input_grad_ref[at] = total.astype(bf16)
        d_att[at] = (d * inputs * inv).astype(bf16)

    extra[...] += mul(d_att[...], (lane == n).astype(bf16), 0, 0)
    pump(0.66)

    def cross(chip, slot):
        return remote(stage_f.at[slot], other_f.at[chip], stage_sem.at[slot], other_sem.at[chip], place.sibling)

    def fill(ref, device):
        at = pl.ds(pl.multiple_of(device * shard, 16), shard)
        ref[:, pl.ds(0, qkv_width)] = mul(normed_t_ref[at], d_qkv[...], 1, 0).astype(bf16)
        ref[:, pl.ds(qkv_width, 128)] = extra[at].astype(bf16)
        ref[:, pl.ds(qkv_width + 128, width)] = mul(attended_t_ref[at], d_middle_low[...], 1, 0).astype(bf16)

    for k in range(half, -1, -1):
        @pl.loop(max(0, 2 * (half - k) - 1), min(ring, 2 * (half - k) + 1))
        def _(i):
            away = half - lax.div(i + 1, 2)
            chip = place.chip_at(jnp.where(lax.rem(i, 2) == 0, away, -away))
            slot = lax.rem(i, 2)

            @pl.when(i >= 2)
            def _():
                cross(chip, slot).wait_send()

            fill(stage_f.at[slot], chip * 2 + 1 - place.core)
            cross(chip, slot).start()
            fill(own_f.at[chip], chip * 2 + place.core)

        pump(1.0 - 0.34 * k / (half + 1))

    for _ in background:
        pass
    for slot in range(2):
        cross(place.chip, slot).wait_send()
    cuts = column_cuts(full_width, DENSE_PARTS)
    work = ring_work(half, DENSE_PARTS)

    def send(d, k, q):
        chip = place.chip_at(k if d == 0 else -k)
        at = pl.ds(*cuts[q])
        return remote(
            own_f.at[chip, :, at],
            come_f.at[d, k - 1, :, at],
            send_f.at[d, k - 1, q],
            recv_f.at[d, k - 1, q],
            place.right if d == 0 else place.left,
        )

    def spread(turn, q):
        at = pl.ds(*cuts[q])
        return pltpu.make_async_remote_copy(
            src_ref=copies_f.at[rank, :, at],
            dst_ref=copies_f.at[rank, :, at],
            send_sem=copy_s.at[turn, q],
            recv_sem=copy_r.at[turn, q],
            device_id={"dp": lax.rem(rank + turn, dp)},
            device_id_type=MESH,
        )

    lanes = 2 if 2 * dp <= weights.shape[0] // rows else 1

    def tile_loads(t):
        own, come, r = tiles[t]
        size = own.shape[1]
        for source in range(dp):
            band = weights.at[pl.ds(((t % lanes) * dp + source) * rows, rows), pl.ds(0, size)]

            @pl.when(rank == source)
            def _():
                pltpu.make_async_copy(own.at[pl.ds(r, rows)], band, tile_in.at[t % lanes, source]).start()

            @pl.when(rank != source)
            def _():
                pltpu.make_async_copy(come.at[source, pl.ds(r, rows)], band, tile_in.at[t % lanes, source]).start()

    def tile_put(t):
        own, _, r = tiles[t]
        held = (d_att, d_middle_low)[t % 2].at[:, pl.ds(0, own.shape[1])]
        to = gd_sum if own is gd_ref else ggu_sum
        return pltpu.make_async_copy(held, to.at[pl.ds(r, rows)], tile_out.at[t % 2])

    def tile_here(t):
        for turn in range(1, dp):
            spread_tile(turn, t).wait_recv()
        tile_loads(t)

    def tile_sum(t):
        own, _, r = tiles[t]
        size = own.shape[1]
        held = (d_att, d_middle_low)[t % 2]
        for source in range(dp):
            band = weights.at[pl.ds(((t % lanes) * dp + source) * rows, rows), pl.ds(0, size)]
            pltpu.make_async_copy(band, band, tile_in.at[t % lanes, source]).wait()
        if t >= 2:
            tile_put(t - 2).wait()

        @pl.loop(0, rows // tile)
        def _(i):
            total = None
            for source in range(dp):
                at = pl.ds(pl.multiple_of(((t % lanes) * dp + source) * rows + i * tile, tile), tile)
                value = weights[at, pl.ds(0, size)].astype(f32)
                total = value if total is None else total + value
            held[pl.ds(pl.multiple_of(i * tile, tile), tile), pl.ds(0, size)] = total.astype(bf16)

        tile_put(t).start()

    def tile_step(t):
        if lanes == 2 and t < len(tiles):
            tile_here(t)
        if t >= 1:
            tile_sum(t - 1)
        if lanes == 1 and t < len(tiles):
            tile_here(t)

    moves = len(work) - DENSE_PARTS
    when = {moves * (t + 2) // (len(tiles) + 2): t for t in range(len(tiles) + 1)}
    met = set()
    for index, (d, k, q) in enumerate(work):
        if index in when:
            tile_step(when[index])
        chip = place.chip_at(0 if d is None else (k if d == 0 else -k))
        key = (0 if k in (0, half) else d, k)
        if key not in met:
            met.add(key)
            remote(other_f.at[chip], other_f.at[chip], stage_sem.at[0], other_sem.at[chip], place.sibling).wait_recv()
        at = pl.ds(*cuts[q])
        total = own_f[chip, :, at].astype(f32) + other_f[chip, :, at].astype(f32)
        for dd in (0, 1) if d is None else (d,):
            if k + 1 <= half and goes(dd, k + 1, q, half, DENSE_PARTS):
                piece = come_f.at[dd, k, :, at]
                remote(piece, piece, send_f.at[dd, k, q], recv_f.at[dd, k, q], place.sibling).wait_recv()
                total += piece[...].astype(f32)
        if d is not None:
            own_f[chip, :, at] = total.astype(bf16)
            send(d, k, q).start()
        else:
            copies_f[rank, :, at] = total.astype(bf16)
            for turn in range(1, dp):
                spread(turn, q).start()
    for t in range(len(tiles) - 2, len(tiles)):
        tile_put(t).wait()
    for q in range(DENSE_PARTS):
        for turn in range(1, dp):
            spread(turn, q).wait()
    total = copies_f[0].astype(f32)
    for r in range(1, dp):
        total += copies_f[r].astype(f32)
    dense_ref[...] = total.astype(bf16)
    for t in range(len(tiles)):
        for turn in range(1, dp):
            spread_tile(turn, t).wait_send()
    for d, k, q in work:
        if d is not None:
            send(d, k, q).wait_send()


def backward(n, dp, own_d, other_d, wall, grad_gu, grad_down, others, collective_id):
    half, ring = n // 4, n // 2
    rows, width = own_d.shape[1:]
    full_width = wall.shape[1]
    qkv_width = full_width - width - 128
    shard = wall.shape[0] // n
    q_width = others[9].shape[1]
    return pl.pallas_call(
        functools.partial(backward_kernel, n, dp),
        out_shape=[
            jax.ShapeDtypeStruct((rows, width), bf16),
            jax.ShapeDtypeStruct((rows, width), bf16),
            jax.ShapeDtypeStruct((shard, full_width), bf16),
            jax.ShapeDtypeStruct(grad_gu.shape, bf16),
            jax.ShapeDtypeStruct(grad_down.shape, bf16),
            jax.ShapeDtypeStruct((dp,) + grad_gu.shape, bf16),
            jax.ShapeDtypeStruct((dp,) + grad_down.shape, bf16),
        ],
        in_specs=[ANY] * 5 + [VMEM] * len(others),
        out_specs=[VMEM] * 3 + [ANY] * 4,
        scratch_shapes=[
            pltpu.VMEM((width, qkv_width), bf16),
            pltpu.VMEM((width, 128), bf16),
            pltpu.VMEM((rows, width), f32),
            pltpu.VMEM((rows, width), bf16),
            pltpu.VMEM((rows, q_width), bf16),
            pltpu.VMEM((rows, qkv_width), bf16),
            pltpu.VMEM((rows, width), f32),
            pltpu.VMEM((width, 128), f32),
            pltpu.VMEM((rows, 128), bf16),
            pltpu.VMEM((ring, shard, full_width), bf16),
            pltpu.VMEM((2, shard, full_width), bf16),
            pltpu.VMEM((ring, shard, full_width), bf16),
            pltpu.VMEM((2, half, shard, full_width), bf16),
            pltpu.VMEM((dp, shard, full_width), bf16),
            DMA((3,)),
            DMA((2,)),
            DMA((ring,)),
            DMA((2, half, DENSE_PARTS)),
            DMA((2, half, DENSE_PARTS)),
            DMA((dp, DENSE_PARTS)),
            DMA((dp, DENSE_PARTS)),
            DMA((dp, (width + grad_down.shape[0]) // rows)),
            DMA((dp, (width + grad_down.shape[0]) // rows)),
            DMA((2, dp)),
            DMA((2,)),
        ]
        + reduce_scratch(rows, width, half, 4),
        compiler_params=pltpu.CompilerParams(
            collective_id=collective_id, has_side_effects=True, vmem_limit_bytes=63 * MB
        ),
    )(own_d, other_d, wall, grad_gu, grad_down, *others)[:5]


def finish_kernel(
    experts_n, output_in, grad_in, dense_in, gu_in, down_in, output, grad, q, kv, out, router, one, two, gate, up, down
):
    output[...] = output_in[...]
    grad[...] = grad_in[...]
    hidden_width = gate.shape[1]
    gate[...] = gu_in[:, pl.ds(0, hidden_width)].astype(f32)
    up[...] = gu_in[:, pl.ds(hidden_width, hidden_width)].astype(f32)
    down[...] = down_in[...].astype(f32)

    @pl.when(pl.program_id(0) == 0)
    def _():
        start = 0
        for ref in (q, kv):
            ref[...] = dense_in[:, pl.ds(start, ref.shape[1])].astype(f32)
            start += ref.shape[1]
        extra = dense_in[:, pl.ds(start, 128)].astype(f32)
        router[...] = extra[:, :experts_n]
        turned = jnp.transpose(extra)
        one[...] = turned[experts_n : experts_n + 1]
        two[...] = turned[experts_n + 1 : experts_n + 2]
        out[...] = dense_in[:, pl.ds(start + 128, out.shape[1])].astype(f32)


def finish(output, grad, dense, gu, down, experts_n, q_width, kv_width):
    steps = 8
    rows, width = output.shape
    shard = dense.shape[0]
    hidden_width = gu.shape[1] // 2

    def tiles(a, b):
        return pl.BlockSpec((a // steps, b), lambda i: (i, 0))

    def whole(a, b):
        return pl.BlockSpec((a, b), lambda i: (0, 0))

    shape = jax.ShapeDtypeStruct
    return pl.pallas_call(
        functools.partial(finish_kernel, experts_n),
        grid=(steps,),
        in_specs=[
            tiles(rows, width),
            tiles(rows, width),
            whole(*dense.shape),
            tiles(*gu.shape),
            tiles(*down.shape),
        ],
        out_specs=[
            tiles(rows, width),
            tiles(rows, width),
            whole(shard, q_width),
            whole(shard, kv_width),
            whole(shard, width),
            whole(shard, experts_n),
            whole(1, shard),
            whole(1, shard),
            tiles(gu.shape[0], hidden_width),
            tiles(gu.shape[0], hidden_width),
            tiles(*down.shape),
        ],
        out_shape=[
            shape((rows, width), bf16),
            shape((rows, width), bf16),
            shape((shard, q_width), f32),
            shape((shard, kv_width), f32),
            shape((shard, width), f32),
            shape((shard, experts_n), f32),
            shape((1, shard), f32),
            shape((1, shard), f32),
            shape((gu.shape[0], hidden_width), f32),
            shape((gu.shape[0], hidden_width), f32),
            shape(down.shape, f32),
        ],
        compiler_params=pltpu.CompilerParams(vmem_limit_bytes=63 * MB),
    )(output, grad, dense, gu, down)


QUARTERS = 4


def expert_kernel(
    n,
    x_ref,
    dog_ref,
    gates_ref,
    gate_any,
    up_any,
    wd_any,
    de_ref,
    dgates_ref,
    ggu_out,
    gd_out,
    od_ref,
    sd_ref,
    oe_ref,
    se_ref,
    xg_ref,
    hg_ref,
    wgu_ref,
    wd_ref,
    ggu_ref,
    gd_ref,
    acc_gu,
    acc_d,
    gate_in,
    dgate_out,
    xbuf,
    dobuf,
    pd,
    pe,
    hbuf,
    own_sem,
    weight_sem,
    ring_s,
    ring_r,
    cross_s,
    cross_r,
    load_sem,
    put_sem,
    sib_r,
    gate_s,
    gate_r,
    dgate_s,
    dgate_r,
    *reduce_refs,
):
    place = Place(n)
    half, ring, me = place.half, place.ring, place.me
    rows, width = x_ref.shape
    hidden_width = wd_ref.shape[0]
    piece = rows // QUARTERS
    weight_copies = [
        pltpu.make_async_copy(gate_any, wgu_ref.at[:, pl.ds(0, hidden_width)], weight_sem.at[0]),
        pltpu.make_async_copy(up_any, wgu_ref.at[:, pl.ds(hidden_width, hidden_width)], weight_sem.at[1]),
        pltpu.make_async_copy(wd_any, wd_ref, weight_sem.at[2]),
    ]
    for copy in weight_copies:
        copy.start()
    pltpu.make_async_copy(x_ref, xbuf.at[0], load_sem.at[0, 0]).start()
    pltpu.make_async_copy(dog_ref.at[me], dobuf.at[0], load_sem.at[1, 0]).start()
    meet_all(place)

    own = pltpu.make_async_copy(xbuf.at[0], xg_ref.at[me], own_sem.at[0])

    def at(q):
        return pl.ds(pl.multiple_of(q * piece, piece), piece)

    def block_of(d, k):
        return jnp.where(d == 0, place.device(-k), place.device(k))

    def along(d, k, q, first=False):
        b = me if first else block_of(d, k - 1)
        return remote(
            x_ref.at[at(q)] if first else xg_ref.at[b, at(q)],
            xg_ref.at[b, at(q)],
            ring_s.at[d, k - 1, q],
            ring_r.at[d, k - 1, q],
            jnp.where(d == 0, place.right, place.left),
        )

    def across(d, k, q, first=False):
        b = me if first else block_of(d, k)
        src = x_ref.at[at(q)] if first else xg_ref.at[b, at(q)]
        return remote(src, xg_ref.at[b, at(q)], cross_s.at[d, k, q], cross_r.at[d, k, q], place.sibling)

    def gate_copy(d):
        to = lax.rem(me + d, n)
        return remote(gates_ref.at[to], gate_in.at[me], gate_s.at[d], gate_r.at[d], to)

    for q in range(QUARTERS):
        for d in (0, 1):
            along(d, 1, q, first=True).start()
        across(0, 0, q, first=True).start()

    @pl.loop(1, n)
    def _(d):
        gate_copy(d).start()

    gate_in[me] = gates_ref[me]
    acc_gu[...] = jnp.zeros_like(acc_gu)
    acc_d[...] = jnp.zeros_like(acc_d)

    def step_of(i):
        late = jnp.where(i < n - 4, i, jnp.where(i < n - 2, i + 2, i - 2))
        k = jnp.where(late < 2, 0, lax.div(late + 2, 4))
        j = jnp.where(late < 2, late, lax.rem(late + 2, 4))
        edge = jnp.logical_or(k == 0, k == half)
        d = jnp.where(edge, 0, lax.rem(j, 2))
        other = jnp.where(edge, j, lax.div(j, 2))
        chip = jnp.where(d == 0, place.chip_at(-k), place.chip_at(k))
        core = jnp.where(other == 0, place.core, 1 - place.core)
        return k, j, d, other, chip, chip * 2 + core

    def pump(d, k, q, last=False):
        along(d, k, q).wait_recv()
        if not last:
            near = jnp.where(q < QUARTERS // 2, 0, 1) == d

            @pl.when(jnp.logical_or(k + 1 < half, near))
            def _():
                along(d, k + 1, q).start()

        across(d, k, q).start()

    def load(block, slot):
        return (
            pltpu.make_async_copy(xg_ref.at[block], xbuf.at[slot], load_sem.at[0, slot]),
            pltpu.make_async_copy(dog_ref.at[block], dobuf.at[slot], load_sem.at[1, slot]),
        )

    def put_wait(slot):
        for which, buf in enumerate((pd, pe, hbuf)):
            pltpu.make_async_copy(buf.at[slot], buf.at[slot], put_sem.at[which, slot]).wait()

    def dgate_copy(block):
        d = lax.rem(block - me + n, n)
        return remote(dgate_out.at[block], dgates_ref.at[me], dgate_s.at[d], dgate_r.at[d], block)

    def load_rest(block, slot):
        return (
            pltpu.make_async_copy(xg_ref.at[block], xbuf.at[slot], load_sem.at[0, slot]),
            pltpu.make_async_copy(dog_ref.at[block], dobuf.at[slot], load_sem.at[1, slot]),
            pltpu.make_async_copy(hg_ref.at[block], hbuf.at[slot], load_sem.at[2, slot]),
        )

    for copy in weight_copies:
        copy.wait()

    def work_on(i):
        k, j, d, other, chip, block = step_of(i)
        slot = lax.rem(i, 2)
        for copy in load(block, slot):
            copy.wait()

        @pl.when(i == 0)
        def _():
            own.start()

        @pl.when(i > 0)
        def _():
            away = lax.rem(me - block + n, n)
            remote(gate_in.at[block], gate_in.at[block], gate_s.at[away], gate_r.at[away], place.sibling).wait_recv()

        gate = jnp.transpose(gate_in[block])[:, :1]
        x = xbuf[slot]
        gu = mul(x, wgu_ref[...], 1, 0)
        g, u = gu[:, :hidden_width], gu[:, hidden_width:]
        s = 1.0 / (1.0 + jnp.exp(-g))
        gs = g * s
        hid = gs * u
        hidg = (hid * gate).astype(bf16)

        @pl.when(jnp.logical_and(i >= 2, i < n - 2))
        def _():
            put_wait(slot)

        pd[slot] = mul(hidg, wd_ref[...], 1, 0).astype(bf16)

        @pl.when(i < 2)
        def _():
            for t in range(2):
                for dd in (0, 1):
                    pump(dd, 1, i * 2 + t)

        @pl.when(jnp.logical_and(i >= 2, k + 1 < half))
        def _():
            for dd in (0, 1):
                pump(dd, k + 1, j)

        @pl.when(jnp.logical_and(k + 1 == half, j < 2))
        def _():
            for dd in (0, 1):
                pump(dd, half, j + dd * (QUARTERS // 2), last=True)

        nk, nj, nd, nother, nchip, nblock = step_of(i + 1)

        @pl.when(jnp.logical_and(i + 1 < n, nother == 1))
        def _():
            for q in range(QUARTERS):
                dd = jnp.where(nk == half, 0 if q < QUARTERS // 2 else 1, nd)
                b = nblock
                remote(
                    xg_ref.at[b, at(q)], xg_ref.at[b, at(q)], cross_s.at[dd, nk, q], cross_r.at[dd, nk, q], place.sibling
                ).wait_recv()

        @pl.when(i == 0)
        def _():
            own.wait()

        @pl.when(i + 1 < n)
        def _():
            for copy in load(nblock, 1 - slot):
                copy.start()

        do = dobuf[slot]
        dh = mul(do, wd_ref[...], 1, 1)
        dgate = jnp.sum(dh * hid, axis=1, keepdims=True)
        dgate_out[block] = jnp.transpose(jnp.broadcast_to(dgate, (rows, 128)))[:8]
        dh = dh * gate
        d_g = (dh * u * s * (1.0 + g * (1.0 - s))).astype(bf16)
        d_u = (dh * gs).astype(bf16)
        dgu = jnp.concatenate([d_g, d_u], axis=1)
        hbuf[slot] = jnp.concatenate([d_g, d_u, hidg], axis=1)
        pltpu.make_async_copy(hbuf.at[slot], hg_ref.at[block], put_sem.at[2, slot]).start()
        pe[slot] = mul(dgu, wgu_ref[...], 1, 1).astype(bf16)

        @pl.when(i > 0)
        def _():
            dgate_copy(block).start()

        @pl.when(i == 0)
        def _():
            dgates_ref[me] = dgate_out[me]

        @pl.when(other == 0)
        def _():
            pltpu.make_async_copy(pd.at[slot], od_ref.at[chip], put_sem.at[0, slot]).start()
            pltpu.make_async_copy(pe.at[slot], oe_ref.at[chip], put_sem.at[1, slot]).start()

        @pl.when(other == 1)
        def _():
            remote(pd.at[slot], sd_ref.at[chip], put_sem.at[0, slot], sib_r.at[0, chip], place.sibling).start()
            remote(pe.at[slot], se_ref.at[chip], put_sem.at[1, slot], sib_r.at[1, chip], place.sibling).start()

    @pl.loop(0, n - 2)
    def _(i):
        work_on(i)

    put_wait(0)
    put_wait(1)

    def other_wait(chip):
        remote(se_ref.at[chip], se_ref.at[chip], put_sem.at[1, 0], sib_r.at[1, chip], place.sibling).wait_recv()

    def write(at, columns, total):
        de_ref[at, columns] = total

    back = ring_reduce(
        place, lambda chip: oe_ref.at[chip], lambda chip: se_ref.at[chip], other_wait, width, write, reduce_refs, 2
    )
    next(back)
    next(back)

    @pl.loop(n - 2, n)
    def _(i):
        work_on(i)

    put_wait(0)
    put_wait(1)

    for copy in load_rest(0, 0):
        copy.start()

    def gradients(first, last):
        @pl.loop(first, last)
        def _(b):
            slot = lax.rem(b, 2)
            for copy in load_rest(b, slot):
                copy.wait()

            @pl.when(b + 1 < n)
            def _():
                for copy in load_rest(b + 1, 1 - slot):
                    copy.start()

            acc_gu[...] += mul(xbuf[slot], hbuf[slot, :, pl.ds(0, 2 * hidden_width)], 0, 0)
            acc_d[...] += mul(hbuf[slot, :, pl.ds(2 * hidden_width, hidden_width)], dobuf[slot], 0, 0)

    steps = len(ring_work(half, 2)) // 2 - 2
    for step in range(steps):
        next(back)
        next(back)
        gradients(n * step // steps, n * (step + 1) // steps)
    ggu_ref[...] = acc_gu[...].astype(bf16)
    gd_ref[...] = acc_d[...].astype(bf16)
    out_copies = [
        pltpu.make_async_copy(ggu_ref, ggu_out, weight_sem.at[0]),
        pltpu.make_async_copy(gd_ref, gd_out, weight_sem.at[1]),
    ]
    for copy in out_copies:
        copy.start()
    for _ in back:
        pass
    for copy in out_copies:
        copy.wait()

    @pl.loop(0, ring)
    def _(chip):
        remote(sd_ref.at[chip], sd_ref.at[chip], put_sem.at[0, 0], sib_r.at[0, chip], place.sibling).wait_recv()

    @pl.loop(1, n)
    def _(d):
        gate_copy(d).wait_send()
        source = lax.rem(me - d + n, n)
        remote(dgates_ref.at[source], dgates_ref.at[source], dgate_s.at[d], dgate_r.at[d], place.sibling).wait()

    for q in range(QUARTERS):
        across(0, 0, q, first=True).wait_send()
        for d in (0, 1):
            for k in range(1, half + 1):
                if k < half or ((q < QUARTERS // 2) == (d == 0)):
                    along(d, k, q).wait_send()
                    across(d, k, q).wait_send()


def experts(n, mixed_in, d_gathered, gate_rows, gate_w, up_w, wd, collective_id):
    half, ring = n // 4, n // 2
    rows, width = mixed_in.shape
    blocks = jax.ShapeDtypeStruct((ring, rows, width), bf16)
    hidden_width = wd.shape[0]
    both = (width, 2 * hidden_width)
    out = pl.pallas_call(
        functools.partial(expert_kernel, n),
        out_shape=[
            jax.ShapeDtypeStruct((rows, width), f32),
            jax.ShapeDtypeStruct((n, 8, rows), f32),
            jax.ShapeDtypeStruct(both, bf16),
            jax.ShapeDtypeStruct(wd.shape, bf16),
            blocks,
            blocks,
            blocks,
            blocks,
            jax.ShapeDtypeStruct((n, rows, width), bf16),
            jax.ShapeDtypeStruct((n, rows, 3 * hidden_width), bf16),
        ],
        in_specs=[ANY, ANY, VMEM, ANY, ANY, ANY],
        out_specs=[VMEM, VMEM] + [ANY] * 8,
        scratch_shapes=[
            pltpu.VMEM(both, bf16),
            pltpu.VMEM(wd.shape, bf16),
            pltpu.VMEM(both, bf16),
            pltpu.VMEM(wd.shape, bf16),
            pltpu.VMEM(both, f32),
            pltpu.VMEM(wd.shape, f32),
            pltpu.VMEM((n, 8, rows), f32),
            pltpu.VMEM((n, 8, rows), f32),
            pltpu.VMEM((2, rows, width), bf16),
            pltpu.VMEM((2, rows, width), bf16),
            pltpu.VMEM((2, rows, width), bf16),
            pltpu.VMEM((2, rows, width), bf16),
            pltpu.VMEM((2, rows, 3 * hidden_width), bf16),
            DMA((1,)),
            DMA((3,)),
            DMA((2, half, QUARTERS)),
            DMA((2, half, QUARTERS)),
            DMA((2, half + 1, QUARTERS)),
            DMA((2, half + 1, QUARTERS)),
            DMA((3, 2)),
            DMA((3, 2)),
            DMA((2, ring)),
            DMA((n,)),
            DMA((n,)),
            DMA((n,)),
            DMA((n,)),
        ]
        + reduce_scratch(rows, width, half, 2),
        compiler_params=pltpu.CompilerParams(
            collective_id=collective_id, has_side_effects=True, vmem_limit_bytes=62 * MB
        ),
    )(mixed_in, d_gathered, gate_rows, gate_w, up_w, wd)
    return out[:6]


def rope_tables(length):
    inverse = np.float32(10000.0) ** (-np.arange(HD // 2, dtype=np.float32) / np.float32(HD // 2))
    angles = np.arange(length, dtype=np.float32)[:, None] * inverse.astype(np.float32)[None, :]
    return [np.tile(table(angles).astype(np.float32), (1, 4)) for table in (np.cos, np.sin)]


def per_device(
    n,
    dp,
    tokens,
    cotangent,
    lengths,
    routes,
    norm1_gain,
    w_query,
    w_kv,
    w_out,
    norm2_gain,
    w_router,
    expert_gate,
    expert_up,
    expert_down,
):
    tok_rows, model_width = tokens.shape
    expert_count = w_router.shape[1]
    kv_width, q_width = w_kv.shape[1], w_query.shape[1]
    shard = w_query.shape[0]
    extra = jnp.concatenate(
        [
            w_router,
            norm1_gain[:, None],
            norm2_gain[:, None],
            jnp.zeros((shard, 128 - expert_count - 2), bf16),
        ],
        axis=1,
    )
    turns = rope_tables(tok_rows)
    (
        wall,
        d_gathered,
        d_out_low,
        queries,
        keys,
        values,
        normed_t,
        attended_t,
        middle,
        mixed_in,
        gates,
        gate_rows,
        gains,
    ) = forward(n, w_query, w_kv, extra, w_out, lengths, cotangent, tokens, routes, turns, 0)
    wall = wall.reshape(-1, wall.shape[-1])
    d_mixed_experts, d_gate_rows, grad_gu, grad_down, own_d, other_d = experts(
        n, mixed_in, d_gathered, gate_rows, expert_gate[0], expert_up[0], expert_down[0], 1
    )

    sums = backward(
        n,
        dp,
        own_d,
        other_d,
        wall,
        grad_gu,
        grad_down,
        (
            d_mixed_experts,
            d_gate_rows,
            gates,
            middle,
            mixed_in,
            d_out_low,
            tokens,
            normed_t,
            attended_t,
            queries,
            keys,
            values,
            *turns,
            gains,
        ),
        2,
    )
    output, input_grad, grad_q, grad_kv, grad_out, router, gain_one, gain_two, gate, up, down = finish(
        *sums, expert_count, q_width, kv_width
    )
    return (
        output,
        input_grad,
        gain_one.reshape(-1),
        grad_q,
        grad_kv,
        grad_out,
        gain_two.reshape(-1),
        router,
        gate[None],
        up[None],
        down[None],
    )


def solution(mesh):
    rows, own = P(("dp", "expert"), None), P("expert", None)
    expert = P("expert", None, None)
    return jax.shard_map(
        functools.partial(per_device, mesh.shape["expert"], mesh.shape["dp"]),
        mesh=mesh,
        in_specs=(rows, rows, P(("dp", "expert")), rows, P("expert"), own, own, own, P("expert"), own)
        + (expert,) * 3,
        out_specs=(rows, rows, P("expert"), own, own, own, P("expert"), own) + (expert,) * 3,
        check_vma=False,
    )
```

```python
import functools

import jax
import jax.numpy as jnp
import numpy as np
from jax import lax
from jax.experimental import pallas as pl
from jax.experimental.pallas import tpu as pltpu
from jax.sharding import PartitionSpec as P

HD = 64
EPSILON = 1e-05
MESH = pl.DeviceIdType.MESH
ANY = pl.BlockSpec(memory_space=pl.ANY)
VMEM = pl.BlockSpec(memory_space=pltpu.VMEM)
DMA = pltpu.SemaphoreType.DMA
MB = 2**20
f32 = jnp.float32
bf16 = jnp.bfloat16


def mul(a, b, ca, cb):
    return lax.dot_general(a, b, (((ca,), (cb,)), ((), ())), preferred_element_type=f32)


class Place:
    def __init__(self, n):
        self.n, self.mid, self.ring = n, n // 8, n // 2
        self.half = self.ring // 2
        self.me = lax.axis_index("expert")
        self.chip, self.core = lax.div(self.me, 2), lax.rem(self.me, 2)
        outer, inner = lax.div(self.chip, self.mid), lax.rem(self.chip, self.mid)
        row = 3 - outer
        step = jnp.where(lax.rem(row, 2) == 0, inner - 1, self.mid - 1 - inner)
        self.at = jnp.where(inner == 0, outer, 4 + row * (self.mid - 1) + step)
        self.sibling = self.chip * 2 + 1 - self.core
        self.right, self.left = self.device(1), self.device(-1)

    def chip_at(self, distance):
        p = lax.rem(self.at + distance + self.ring, self.ring)
        wide = max(self.mid - 1, 1)
        row, k = lax.div(lax.max(p - 4, 0), wide), lax.rem(lax.max(p - 4, 0), wide)
        inner = jnp.where(lax.rem(row, 2) == 0, 1 + k, self.mid - 1 - k)
        return jnp.where(p < 4, p * self.mid, (3 - row) * self.mid + inner)

    def device(self, distance):
        return self.chip_at(distance) * 2 + self.core


def remote(src, dst, send, recv, device):
    return pltpu.make_async_remote_copy(
        src_ref=src, dst_ref=dst, send_sem=send, recv_sem=recv, device_id={"expert": device}, device_id_type=MESH
    )


def meet(targets):
    barrier = pltpu.get_barrier_semaphore()
    for target in targets:
        pl.semaphore_signal(barrier, inc=1, device_id={"expert": target}, device_id_type=MESH)
    pl.semaphore_wait(barrier, len(targets))


def meet_all(place):
    barrier = pltpu.get_barrier_semaphore()

    @pl.loop(1, place.n)
    def _(d):
        other = lax.rem(place.me + d, place.n)
        pl.semaphore_signal(barrier, inc=1, device_id={"expert": other}, device_id_type=MESH)

    pl.semaphore_wait(barrier, place.n - 1)


def column_cuts(width, parts):
    tiles = width // 128
    edges = [128 * (tiles * i // parts) for i in range(parts + 1)]
    return [(edges[i], edges[i + 1] - edges[i]) for i in range(parts)]


PARTS = 2


def forward_kernel(
    n,
    dp,
    w_query_ref,
    w_kv_ref,
    w_extra_ref,
    w_out_ref,
    lengths_ref,
    cotangent_ref,
    tokens_ref,
    routes_ref,
    cos_ref,
    sin_ref,
    wallg_ref,
    doutg_ref,
    dout_ref,
    q_ref,
    k_ref,
    v_ref,
    normed_t_ref,
    attended_t_ref,
    middle_ref,
    mixed_ref,
    gates_ref,
    gate_rows_ref,
    gains_ref,
    wall_ref,
    weights,
    proj,
    attended,
    own_sem,
    piece_sem,
    load_sem,
    ss,
    rs,
    css,
    crs,
    xs,
    xr,
    xcs,
    xcr,
):
    place = Place(n)
    half, me = place.half, place.me
    rank = lax.axis_index("dp")
    helping = dp == 2
    rows, width = tokens_ref.shape
    shard = wall_ref.shape[0]
    q_width, kv_width = q_ref.shape[1], 2 * k_ref.shape[1]
    qkv_width = q_width + kv_width
    near = qkv_width + 128
    edges = (0, q_width, qkv_width, near, near + width)
    pieces = [
        pltpu.make_async_copy(ref, wall_ref.at[:, pl.ds(edges[i], edges[i + 1] - edges[i])], piece_sem.at[i])
        for i, ref in enumerate((w_query_ref, w_kv_ref, w_extra_ref, w_out_ref))
    ]
    for copy in pieces:
        copy.start()
    barrier = pltpu.get_barrier_semaphore()
    for target in (place.right, place.left, place.sibling):
        pl.semaphore_signal(barrier, inc=1, device_id={"expert": target}, device_id_type=MESH)
    if helping:
        pl.semaphore_signal(barrier, inc=1, device_id={"dp": 1 - rank}, device_id_type=MESH)
    pl.semaphore_wait(barrier, 4 if helping else 3)
    for copy in pieces:
        copy.wait()
    started = []

    def begin(copy):
        copy.start()
        started.append(copy)

    alone = 128 * (edges[4] // 128 * 10 // 33)
    shared = (2 * alone, edges[4] - 2 * alone)
    if helping:
        cut_weights = (
            [(pl.multiple_of(rank * alone, 128), alone), shared],
            {0: (pl.multiple_of((1 - rank) * alone, 128), alone)},
        )
    else:
        cut_weights = (column_cuts(edges[4], PARTS), {})
    flows = (
        (wall_ref, wallg_ref, cut_weights, weights),
        (dout_ref, doutg_ref, (column_cuts(width, PARTS), {}), None),
    )

    def block_at(d, k):
        return me if k == 0 else (place.device(-k) if d == 0 else place.device(k))

    def sibling_of(b):
        return b + 1 - 2 * lax.rem(b, 2)

    def spot(a, b, cut, own=False):
        x_ref, o_ref = flows[a][:2]
        return (x_ref if own else o_ref.at[b]).at[:, pl.ds(*cut)]

    def along(a, d, k, q):
        b, cut = block_at(d, k - 1), flows[a][2][0][q]
        target = place.right if d == 0 else place.left
        return remote(spot(a, b, cut, k == 1), spot(a, b, cut), ss.at[a, d, k - 1, q], rs.at[a, d, k - 1, q], target)

    def across(a, d, k, q):
        b, cut = block_at(d, k), flows[a][2][0][q]
        return remote(
            spot(a, b, cut, k == 0), spot(a, b, cut), css.at[a, d, k, q], crs.at[a, d, k, q], place.sibling
        )

    def over(a, d, k, q):
        b, cut = block_at(d, k), flows[a][2][0][q]
        return pltpu.make_async_remote_copy(
            src_ref=spot(a, b, cut),
            dst_ref=spot(a, b, cut),
            send_sem=xs.at[a, d, k, q],
            recv_sem=xr.at[a, d, k, q],
            device_id={"dp": 1 - rank},
            device_id_type=MESH,
        )

    def over_across(a, d, k, q):
        b, cut = block_at(d, k), flows[a][2][1][q]
        return remote(spot(a, b, cut, k == 0), spot(a, b, cut), xcs.at[a, d, k, q], xcr.at[a, d, k, q], place.sibling)

    def take(a, b, cut, own=False):
        local = flows[a][3]
        if local is not None:
            at = pl.ds(pl.multiple_of(b * shard, 16), shard)
            pltpu.make_async_copy(spot(a, b, cut, own), local.at[at, pl.ds(*cut)], load_sem.at[0]).start()

    def first(a):
        parts, others = flows[a][2]
        for q in range(PARTS):
            begin(along(a, 0, 1, q))
            begin(along(a, 1, 1, q))
            begin(across(a, 0, 0, q))
            take(a, me, parts[q], True)
            if q in others:
                begin(over_across(a, 0, 0, q))
                take(a, me, others[q], True)

    def arrive(a, d, k, q):
        parts, others = flows[a][2]
        along(a, d, k, q).wait_recv()
        if k < half and goes(d, k + 1, q, half, PARTS):
            begin(along(a, d, k + 1, q))
        if q in others:
            begin(over(a, d, k, q))
        begin(across(a, d, k, q))
        take(a, block_at(d, k), parts[q])

    def places(k):
        return [
            (d, q)
            for q in range(PARTS)
            for d in (0, 1)
            if (k == 0 and d == 0) or (k > 0 and goes(d, k, q, half, PARTS))
        ]

    def aside(a, k):
        parts, others = flows[a][2]
        for d, q in places(k) if k > 0 else ():
            if q in others:
                b = block_at(d, k)
                piece = spot(a, b, others[q])
                remote(piece, piece, xs.at[a, d, k, q], xr.at[a, d, k, q], place.sibling).wait_recv()
                begin(over_across(a, d, k, q))
                take(a, b, others[q])
        for d, q in places(k):
            b = sibling_of(block_at(d, k))
            piece = spot(a, b, parts[q])
            remote(piece, piece, css.at[a, d, k, q], crs.at[a, d, k, q], place.sibling).wait_recv()
            take(a, b, parts[q])

    def aside_over(a, k):
        others = flows[a][2][1]
        for d, q in places(k):
            if q in others:
                b = sibling_of(block_at(d, k))
                piece = spot(a, b, others[q])
                remote(piece, piece, xcs.at[a, d, k, q], xcr.at[a, d, k, q], place.sibling).wait_recv()
                take(a, b, others[q])

    events, ends = [functools.partial(first, 0)], []
    for a in range(len(flows)):
        for k in range(1, half + 1):
            events += [functools.partial(arrive, a, d, k, q) for d, q in places(k)]
            if k == half - 1 and a + 1 < len(flows):
                events.append(functools.partial(first, a + 1))
            events.append(functools.partial(aside, a, k - 1))
            if k >= 2:
                events.append(functools.partial(aside_over, a, k - 2))
        events.append(functools.partial(aside, a, half))
        events += [functools.partial(aside_over, a, k) for k in (half - 1, half)]
        ends.append(len(events))
    done = [0]

    def pump(last):
        while done[0] < last:
            events[done[0]]()
            done[0] += 1

    own = [
        pltpu.make_async_copy(x_ref, o_ref.at[me], own_sem.at[i])
        for i, (x_ref, o_ref) in enumerate(((wall_ref, wallg_ref), (dout_ref, doutg_ref)))
    ]
    alive = lax.broadcasted_iota(jnp.int32, (rows, width), 0) < lengths_ref[0]
    dout_ref[...] = jnp.where(alive, cotangent_ref[...].astype(f32), 0.0).astype(bf16)
    pump(1)
    for copy in own:
        copy.start()
    pump(ends[0])
    pltpu.make_async_copy(weights, weights, load_sem.at[0]).wait()

    lane = lax.broadcasted_iota(jnp.int32, (rows, 128), 1)
    turned = jnp.transpose(weights[:, pl.ds(qkv_width, 128)].astype(f32))
    gains_ref[...] = jnp.concatenate([turned[n : n + 1], turned[n + 1 : n + 2], jnp.zeros((6, width), f32)], axis=0)
    inputs = tokens_ref[...].astype(f32)
    inv = lax.rsqrt(jnp.mean(inputs * inputs, axis=1, keepdims=True) + EPSILON)
    normed = (inputs * inv * gains_ref[0:1]).astype(bf16)
    proj[...] = mul(normed, weights[:, pl.ds(0, qkv_width)], 1, 0)
    normed_t_ref[...] = jnp.transpose(normed)
    cosine, sine = cos_ref[...], sin_ref[...]
    sine_on = jnp.where(lane % HD < HD // 2, -sine, sine)

    def turn(at):
        block = proj[:, at]
        return (block * cosine + swap_halves(block, lane) * sine_on).astype(bf16)

    for b in range(q_width // 128):
        q_ref[:, pl.ds(128 * b, 128)] = turn(pl.ds(128 * b, 128))
    for b in range(kv_width // 256):
        k_ref[:, pl.ds(128 * b, 128)] = turn(pl.ds(q_width + 128 * b, 128))
    v_ref[...] = proj[:, pl.ds(q_width + kv_width // 2, kv_width // 2)].astype(bf16)
    t_at = lax.broadcasted_iota(jnp.int32, (rows, rows), 0)
    u_at = lax.broadcasted_iota(jnp.int32, (rows, rows), 1)
    causal = t_at >= u_at
    kv_count = k_ref.shape[1] // HD
    per_group = q_width // HD // kv_count
    kept = None
    for g in range(kv_count):
        pair = pl.ds(128 * (g // 2), 128)
        k_parts = head_halves(k_ref[:, pair].astype(f32), lane, g % 2)
        v_parts = head_halves(v_ref[:, pair].astype(f32), lane, g % 2)
        for h in range(per_group * g, per_group * (g + 1)):
            at = pl.ds(128 * (h // 2), 128)
            probs = softmax_rows(q_ref[:, at], k_parts[h % 2], causal).astype(bf16)
            kept_new = mul(probs, v_parts[h % 2], 1, 0)
            if h % 2 == 0:
                kept = kept_new
            else:
                attended[:, at] = (kept + kept_new).astype(bf16)
        pump(ends[0] + 4 * (g + 1) // kv_count)
    attended_t_ref[...] = jnp.transpose(attended[...])
    middle_ref[...] = tokens_ref[...].astype(f32) + mul(attended[...], weights[:, pl.ds(near, width)], 1, 0)
    pump(ends[0] + 6)
    tile = 32

    @pl.loop(0, rows // tile)
    def _(r):
        at = pl.ds(pl.multiple_of(r * tile, tile), tile)
        middle = middle_ref[at]
        scale = lax.rsqrt(jnp.mean(middle * middle, axis=1, keepdims=True) + EPSILON)
        mixed_ref[at] = (middle * scale * gains_ref[1:2]).astype(bf16)

    pump(ends[0] + 8)
    logits = mul(mixed_ref[...], weights[:, pl.ds(qkv_width, 128)], 1, 0)
    chosen = lane == routes_ref[:, 0:1]
    for choice in range(1, routes_ref.shape[1]):
        chosen = jnp.logical_or(chosen, lane == routes_ref[:, choice : choice + 1])
    logits = jnp.where(chosen, logits, -1e30)
    e = jnp.where(chosen, jnp.exp(logits - jnp.max(logits, axis=1, keepdims=True)), 0.0)
    gates = e / jnp.sum(e, axis=1, keepdims=True)
    gates_ref[...] = gates
    across_gates = jnp.transpose(gates)
    for e in range(n):
        gate_rows_ref[e] = jnp.broadcast_to(across_gates[e : e + 1], (8, rows))
    pump(ends[1])
    for copy in own:
        copy.wait()
    for copy in started:
        copy.wait_send()


def forward(n, dp, w_query, w_kv, w_extra, w_out, lengths, cotangent, tokens, routes, turns, collective_id):
    half = n // 4
    rows, width = tokens.shape
    shard, q_width = w_query.shape
    kv_width = w_kv.shape[1]
    full_width = q_width + kv_width + 128 + width
    shape = jax.ShapeDtypeStruct
    return pl.pallas_call(
        functools.partial(forward_kernel, n, dp),
        out_shape=[
            shape((n, shard, full_width), bf16),
            shape((n, rows, width), bf16),
            shape((rows, width), bf16),
            shape((rows, q_width), bf16),
            shape((rows, kv_width // 2), bf16),
            shape((rows, kv_width // 2), bf16),
            shape((width, rows), bf16),
            shape((q_width, rows), bf16),
            shape((rows, width), f32),
            shape((rows, width), bf16),
            shape((rows, 128), f32),
            shape((n, 8, rows), f32),
            shape((8, width), f32),
        ],
        in_specs=[ANY] * 4 + [pl.BlockSpec(memory_space=pltpu.SMEM)] + [VMEM] * 5,
        out_specs=[ANY] * 2 + [VMEM] * 11,
        scratch_shapes=[
            pltpu.VMEM((shard, full_width), bf16),
            pltpu.VMEM((width, full_width), bf16),
            pltpu.VMEM((rows, q_width + kv_width), f32),
            pltpu.VMEM((rows, q_width), bf16),
            DMA((2,)),
            DMA((4,)),
            DMA((1,)),
            DMA((2, 2, half, PARTS)),
            DMA((2, 2, half, PARTS)),
            DMA((2, 2, half + 1, PARTS)),
            DMA((2, 2, half + 1, PARTS)),
        ]
        + [DMA((1, 2, half + 1, PARTS)) for _ in range(4)],
        compiler_params=pltpu.CompilerParams(
            collective_id=collective_id, has_side_effects=True, vmem_limit_bytes=56 * MB
        ),
    )(w_query, w_kv, w_extra, w_out, lengths, cotangent, tokens, routes, *turns)


SLOTS = 4


def ring_work(half, parts):
    work = []
    for k in range(half, 0, -1):
        for q in range(parts):
            for d in (0, 1):
                if goes(d, k, q, half, parts):
                    work.append((d, k, q))
    return work + [(None, 0, q) for q in range(parts)]


def goes(d, k, q, half, parts):
    return k < half or ((q < parts // 2) == (d == 0))


def widest(width, parts):
    return max(w for _, w in column_cuts(width, parts))


def reduce_scratch(rows, width, half, parts):
    return [
        pltpu.VMEM((2, half, rows, width), bf16),
        pltpu.VMEM((SLOTS, rows, widest(width, parts)), bf16),
        pltpu.VMEM((SLOTS, rows, widest(width, parts)), bf16),
        DMA((SLOTS,)),
        DMA((SLOTS,)),
        DMA((SLOTS,)),
        DMA((2, half, parts)),
    ]


def ring_reduce(place, own_at, other_at, other_wait, width, write, scratch, first=0):
    arrived, mine, theirs, mine_sem, theirs_sem, send_sem, recv_sem = scratch
    half = place.half
    parts = recv_sem.shape[2]
    cuts = column_cuts(width, parts)
    rows = arrived.shape[2]
    tile = 16
    work = ring_work(half, parts)

    def chip_of(d, k):
        return place.chip_at(k if d != 1 else -k)

    def loads(i):
        d, k, q = work[i]
        slot, chip, (start, size) = i % SLOTS, chip_of(d, k), cuts[q]
        return (
            pltpu.make_async_copy(
                own_at(chip).at[:, pl.ds(start, size)], mine.at[slot, :, pl.ds(0, size)], mine_sem.at[slot]
            ),
            pltpu.make_async_copy(
                other_at(chip).at[:, pl.ds(start, size)], theirs.at[slot, :, pl.ds(0, size)], theirs_sem.at[slot]
            ),
        )

    def send(i):
        d, k, q = work[i]
        start, size = cuts[q]
        return remote(
            mine.at[i % SLOTS, :, pl.ds(0, size)],
            arrived.at[d, k - 1, :, pl.ds(start, size)],
            send_sem.at[i % SLOTS],
            recv_sem.at[d, k - 1, q],
            place.right if d == 0 else place.left,
        )

    waited = set()
    fetched = [0]

    def fetch(last):
        while fetched[0] <= min(last, len(work) - 1):
            fetch_one(fetched[0])
            fetched[0] += 1

    def fetch_one(i):
        d, k, q = work[i]
        if i >= SLOTS:
            send(i - SLOTS).wait_send()
        key = (0 if k in (0, half) else d, k)
        if key not in waited:
            waited.add(key)
            other_wait(chip_of(d, k))
        for copy in loads(i):
            copy.start()

    ahead = SLOTS // 2
    for i, (d, k, q) in enumerate(work):
        fetch(i + ahead if i >= first else min(i + ahead, first - 1))
        for copy in loads(i):
            copy.wait()
        start, size = cuts[q]
        slot = i % SLOTS
        come = []
        for dd in (0, 1) if d is None else (d,):
            if k + 1 <= half and goes(dd, k + 1, q, half, parts):
                piece = arrived.at[dd, k, :, pl.ds(start, size)]
                remote(piece, piece, send_sem.at[slot], recv_sem.at[dd, k, q], place.sibling).wait_recv()
                come.append(dd)

        @pl.loop(0, rows // tile)
        def _(r):
            at = pl.ds(pl.multiple_of(r * tile, tile), tile)
            total = mine[slot, at, pl.ds(0, size)].astype(f32) + theirs[slot, at, pl.ds(0, size)].astype(f32)
            for dd in come:
                total += arrived[dd, k, at, pl.ds(start, size)].astype(f32)
            if d is None:
                write(at, pl.ds(start, size), total)
            else:
                mine[slot, at, pl.ds(0, size)] = total.astype(bf16)

        if d is not None:
            send(i).start()
        yield
    sends = len(work) - parts
    for i in range(max(0, len(work) - SLOTS), sends):
        send(i).wait_send()


DENSE_PARTS = 4


def swap_halves(values, lane):
    width = values.shape[1]
    return jnp.where(lane % HD < HD // 2, pltpu.roll(values, width - HD // 2, 1), pltpu.roll(values, HD // 2, 1))


def head_halves(block, lane, low):
    turned = pltpu.roll(block, HD, 1)
    lower, upper = (block, turned) if low == 0 else (turned, block)
    zero = jnp.zeros_like(block)
    return jnp.where(lane < HD, lower, zero).astype(bf16), jnp.where(lane < HD, zero, upper).astype(bf16)


def softmax_rows(q, k, causal):
    scores = jnp.where(causal, mul(q, k, 1, 1) * HD**-0.5, -1e30)
    e = jnp.exp(scores - jnp.max(scores, axis=1, keepdims=True))
    return e * (1.0 / jnp.sum(e, axis=1, keepdims=True))


def backward_kernel(
    n,
    dp,
    od_ref,
    sd_ref,
    wall_ref,
    ggu_ref,
    gd_ref,
    dmix_ref,
    dgate_ref,
    gates_ref,
    middle_ref,
    mixed_ref,
    dout_ref,
    tokens_ref,
    normed_t_ref,
    attended_t_ref,
    q_ref,
    k_ref,
    v_ref,
    cos_ref,
    sin_ref,
    gains_ref,
    output_ref,
    input_grad_ref,
    dense_ref,
    ggu_sum,
    gd_sum,
    ggu_in,
    gd_in,
    weights,
    extra_w,
    d_middle,
    d_middle_low,
    d_att,
    d_qkv,
    d_normed,
    extra,
    logits_low,
    own_f,
    stage_f,
    other_f,
    come_f,
    copies_f,
    weight_sem,
    stage_sem,
    other_sem,
    send_f,
    recv_f,
    copy_s,
    copy_r,
    expert_s,
    expert_r,
    tile_in,
    tile_out,
    *scratch_d,
):
    place = Place(n)
    half, ring = place.half, place.ring
    rank = lax.axis_index("dp")
    rows, width = middle_ref.shape
    q_width, kv_width = q_ref.shape[1], 2 * k_ref.shape[1]
    qkv_width = q_width + kv_width
    shard = own_f.shape[1]
    full_width = own_f.shape[2]
    barrier = pltpu.get_barrier_semaphore()
    for target in (place.right, place.left, place.sibling):
        pl.semaphore_signal(barrier, inc=1, device_id={"expert": target}, device_id_type=MESH)
    for turn in range(1, dp):
        pl.semaphore_signal(barrier, inc=1, device_id={"dp": lax.rem(rank + turn, dp)}, device_id_type=MESH)
    out_w = pltpu.make_async_copy(
        wall_ref.at[:, pl.ds(qkv_width + 128, width)], weights.at[:, pl.ds(0, width)], weight_sem.at[0]
    )
    extra_copy = pltpu.make_async_copy(wall_ref.at[:, pl.ds(qkv_width, 128)], extra_w, weight_sem.at[1])
    qkv_w = pltpu.make_async_copy(wall_ref.at[:, pl.ds(0, qkv_width)], weights, weight_sem.at[2])
    out_w.start()
    extra_copy.start()
    pl.semaphore_wait(barrier, 3 + dp - 1)

    hidden_width = ggu_ref.shape[1] // 2
    tiles = [(ggu_ref, ggu_in, r) for r in range(0, ggu_ref.shape[0], rows)]
    tiles += [(gd_ref, gd_in, r) for r in range(0, gd_ref.shape[0], rows)]

    def spread_tile(turn, t):
        own, come, r = tiles[t]
        return pltpu.make_async_remote_copy(
            src_ref=own.at[pl.ds(r, rows)],
            dst_ref=come.at[rank, pl.ds(r, rows)],
            send_sem=expert_s.at[turn, t],
            recv_sem=expert_r.at[turn, t],
            device_id={"dp": lax.rem(rank + turn, dp)},
            device_id_type=MESH,
        )

    for t in range(len(tiles)):
        for turn in range(1, dp):
            spread_tile(turn, t).start()

    def write_output(at, columns, total):
        output_ref[at, columns] = (middle_ref[at, columns] + total).astype(bf16)

    background = ring_reduce(
        place, lambda chip: od_ref.at[chip], lambda chip: sd_ref.at[chip], lambda chip: None, width, write_output, scratch_d
    )
    items = len(ring_work(half, scratch_d[6].shape[2]))
    done = [0]

    def pump(share):
        while done[0] < min(items, int(items * share + 0.5)):
            next(background)
            done[0] += 1

    pump(0.06)
    d_rows = jnp.concatenate([dgate_ref[:, 0, :], jnp.zeros((128 - n, rows), f32)], axis=0)
    d_gates = jnp.transpose(d_rows)
    gates = gates_ref[...]
    d_sel = gates * (d_gates - jnp.sum(gates * d_gates, axis=1, keepdims=True))
    logits_low[...] = d_sel.astype(bf16)
    extra_copy.wait()
    d_normed[...] = mul(logits_low[...], extra_w[...], 1, 1)
    gain_one, gain_two = gains_ref[0:1], gains_ref[1:2]
    tile = 32

    @pl.loop(0, rows // tile)
    def _(r):
        at = pl.ds(pl.multiple_of(r * tile, tile), tile)
        middle = middle_ref[at]
        d_mixed = dmix_ref[at] + d_normed[at]
        inv = lax.rsqrt(jnp.mean(middle * middle, axis=1, keepdims=True) + EPSILON)
        scaled = d_mixed * gain_two
        back = jnp.mean(scaled * middle, axis=1, keepdims=True)
        total = dout_ref[at].astype(f32) + inv * scaled - middle * (inv * inv * inv * back)
        d_middle[at] = total
        d_middle_low[at] = total.astype(bf16)
        d_att[at] = (d_mixed * middle * inv).astype(bf16)

    lane = lax.broadcasted_iota(jnp.int32, (rows, 128), 1)
    extra[...] = mul(mixed_ref[...], logits_low[...], 0, 0) + mul(
        d_att[...], (lane == n + 1).astype(bf16), 0, 0
    )
    pump(0.12)
    out_w.wait()
    d_att[...] = mul(d_middle_low[...], weights[:, pl.ds(0, width)], 1, 1).astype(bf16)
    qkv_w.start()
    pump(0.18)

    t_at = lax.broadcasted_iota(jnp.int32, (rows, rows), 0)
    u_at = lax.broadcasted_iota(jnp.int32, (rows, rows), 1)
    causal = t_at >= u_at
    cosine, sine = cos_ref[...], sin_ref[...]
    sine_back = jnp.where(lane % HD < HD // 2, sine, -sine)
    kv_count = k_ref.shape[1] // HD
    per_group = q_width // HD // kv_count
    d_normed[...] = jnp.zeros_like(d_normed)
    pair_k, pair_v = None, None
    for g in range(kv_count):
        pair = pl.ds(128 * (g // 2), 128)
        k_parts = head_halves(k_ref[:, pair].astype(f32), lane, g % 2)
        v_parts = head_halves(v_ref[:, pair].astype(f32), lane, g % 2)
        d_k, d_v = [None, None], [None, None]
        for h in range(per_group * g, per_group * (g + 1)):
            at = pl.ds(128 * (h // 2), 128)
            low = h % 2
            query, d_a = q_ref[:, at], d_att[:, at]
            probs = softmax_rows(query, k_parts[low], causal)
            probs_low = probs.astype(bf16)
            d_probs = mul(d_a, v_parts[low], 1, 1)
            weighted = probs * d_probs
            d_scores = (weighted - probs * jnp.sum(weighted, axis=1, keepdims=True)).astype(bf16)
            d_normed[:, at] += mul(d_scores, k_parts[low], 1, 0)
            step_k, step_v = mul(d_scores, query, 0, 0), mul(probs_low, d_a, 0, 0)
            d_k[low] = step_k if d_k[low] is None else d_k[low] + step_k
            d_v[low] = step_v if d_v[low] is None else d_v[low] + step_v

        def gathered(parts):
            stay, turn = parts[g % 2], parts[1 - g % 2]
            return stay if turn is None else (pltpu.roll(turn, HD, 1) if stay is None else stay + pltpu.roll(turn, HD, 1))

        if g % 2 == 0:
            pair_k, pair_v = gathered(d_k), gathered(d_v)
        if g % 2 == 1 or g + 1 == kv_count:
            total_k = jnp.where(lane < HD, pair_k, gathered(d_k)) * HD**-0.5
            total_v = jnp.where(lane < HD, pair_v, gathered(d_v))
            turned = total_k * cosine + swap_halves(total_k, lane) * sine_back
            d_qkv[:, pl.ds(q_width + 128 * (g // 2), 128)] = turned.astype(bf16)
            d_qkv[:, pl.ds(q_width + kv_width // 2 + 128 * (g // 2), 128)] = total_v.astype(bf16)
        pump(0.18 + 0.3 * (g + 1) / kv_count)
    for b in range(q_width // 128):
        at = pl.ds(128 * b, 128)
        total = d_normed[:, at] * HD**-0.5
        d_qkv[:, at] = (total * cosine + swap_halves(total, lane) * sine_back).astype(bf16)
    pump(0.53)
    qkv_w.wait()
    d_normed[...] = mul(d_qkv[...], weights[...], 1, 1)

    @pl.loop(0, rows // tile)
    def _(r):
        at = pl.ds(pl.multiple_of(r * tile, tile), tile)
        inputs = tokens_ref[at].astype(f32)
        d = d_normed[at]
        inv = lax.rsqrt(jnp.mean(inputs * inputs, axis=1, keepdims=True) + EPSILON)
        scaled = d * gain_one
        back = jnp.mean(scaled * inputs, axis=1, keepdims=True)
        total = d_middle[at] + inv * scaled - inputs * (inv * inv * inv * back)
        input_grad_ref[at] = total.astype(bf16)
        d_att[at] = (d * inputs * inv).astype(bf16)

    extra[...] += mul(d_att[...], (lane == n).astype(bf16), 0, 0)
    pump(0.66)

    def cross(chip, slot):
        return remote(stage_f.at[slot], other_f.at[chip], stage_sem.at[slot], other_sem.at[chip], place.sibling)

    def fill(ref, device):
        at = pl.ds(pl.multiple_of(device * shard, 16), shard)
        ref[:, pl.ds(0, qkv_width)] = mul(normed_t_ref[at], d_qkv[...], 1, 0).astype(bf16)
        ref[:, pl.ds(qkv_width, 128)] = extra[at].astype(bf16)
        ref[:, pl.ds(qkv_width + 128, width)] = mul(attended_t_ref[at], d_middle_low[...], 1, 0).astype(bf16)

    for k in range(half, -1, -1):
        @pl.loop(max(0, 2 * (half - k) - 1), min(ring, 2 * (half - k) + 1))
        def _(i):
            away = half - lax.div(i + 1, 2)
            chip = place.chip_at(jnp.where(lax.rem(i, 2) == 0, away, -away))
            slot = lax.rem(i, 2)

            @pl.when(i >= 2)
            def _():
                cross(chip, slot).wait_send()

            fill(stage_f.at[slot], chip * 2 + 1 - place.core)
            cross(chip, slot).start()
            fill(own_f.at[chip], chip * 2 + place.core)

        pump(1.0 - 0.34 * k / (half + 1))

    for _ in background:
        pass
    for slot in range(2):
        cross(place.chip, slot).wait_send()
    cuts = column_cuts(full_width, DENSE_PARTS)
    work = ring_work(half, DENSE_PARTS)

    def send(d, k, q):
        chip = place.chip_at(k if d == 0 else -k)
        at = pl.ds(*cuts[q])
        return remote(
            own_f.at[chip, :, at],
            come_f.at[d, k - 1, :, at],
            send_f.at[d, k - 1, q],
            recv_f.at[d, k - 1, q],
            place.right if d == 0 else place.left,
        )

    def spread(turn, q):
        at = pl.ds(*cuts[q])
        return pltpu.make_async_remote_copy(
            src_ref=copies_f.at[rank, :, at],
            dst_ref=copies_f.at[rank, :, at],
            send_sem=copy_s.at[turn, q],
            recv_sem=copy_r.at[turn, q],
            device_id={"dp": lax.rem(rank + turn, dp)},
            device_id_type=MESH,
        )

    lanes = 2 if 2 * dp <= weights.shape[0] // rows else 1

    def tile_loads(t):
        own, come, r = tiles[t]
        size = own.shape[1]
        for source in range(dp):
            band = weights.at[pl.ds(((t % lanes) * dp + source) * rows, rows), pl.ds(0, size)]

            @pl.when(rank == source)
            def _():
                pltpu.make_async_copy(own.at[pl.ds(r, rows)], band, tile_in.at[t % lanes, source]).start()

            @pl.when(rank != source)
            def _():
                pltpu.make_async_copy(come.at[source, pl.ds(r, rows)], band, tile_in.at[t % lanes, source]).start()

    def tile_put(t):
        own, _, r = tiles[t]
        held = (d_att, d_middle_low)[t % 2].at[:, pl.ds(0, own.shape[1])]
        to = gd_sum if own is gd_ref else ggu_sum
        return pltpu.make_async_copy(held, to.at[pl.ds(r, rows)], tile_out.at[t % 2])

    def tile_here(t):
        for turn in range(1, dp):
            spread_tile(turn, t).wait_recv()
        tile_loads(t)

    def tile_sum(t):
        own, _, r = tiles[t]
        size = own.shape[1]
        held = (d_att, d_middle_low)[t % 2]
        for source in range(dp):
            band = weights.at[pl.ds(((t % lanes) * dp + source) * rows, rows), pl.ds(0, size)]
            pltpu.make_async_copy(band, band, tile_in.at[t % lanes, source]).wait()
        if t >= 2:
            tile_put(t - 2).wait()

        @pl.loop(0, rows // tile)
        def _(i):
            total = None
            for source in range(dp):
                at = pl.ds(pl.multiple_of(((t % lanes) * dp + source) * rows + i * tile, tile), tile)
                value = weights[at, pl.ds(0, size)].astype(f32)
                total = value if total is None else total + value
            held[pl.ds(pl.multiple_of(i * tile, tile), tile), pl.ds(0, size)] = total.astype(bf16)

        tile_put(t).start()

    def tile_step(t):
        if lanes == 2 and t < len(tiles):
            tile_here(t)
        if t >= 1:
            tile_sum(t - 1)
        if lanes == 1 and t < len(tiles):
            tile_here(t)

    moves = len(work) - DENSE_PARTS
    when = {moves * (t + 2) // (len(tiles) + 2): t for t in range(len(tiles) + 1)}
    met = set()
    for index, (d, k, q) in enumerate(work):
        if index in when:
            tile_step(when[index])
        chip = place.chip_at(0 if d is None else (k if d == 0 else -k))
        key = (0 if k in (0, half) else d, k)
        if key not in met:
            met.add(key)
            remote(other_f.at[chip], other_f.at[chip], stage_sem.at[0], other_sem.at[chip], place.sibling).wait_recv()
        at = pl.ds(*cuts[q])
        total = own_f[chip, :, at].astype(f32) + other_f[chip, :, at].astype(f32)
        for dd in (0, 1) if d is None else (d,):
            if k + 1 <= half and goes(dd, k + 1, q, half, DENSE_PARTS):
                piece = come_f.at[dd, k, :, at]
                remote(piece, piece, send_f.at[dd, k, q], recv_f.at[dd, k, q], place.sibling).wait_recv()
                total += piece[...].astype(f32)
        if d is not None:
            own_f[chip, :, at] = total.astype(bf16)
            send(d, k, q).start()
        else:
            copies_f[rank, :, at] = total.astype(bf16)
            for turn in range(1, dp):
                spread(turn, q).start()
    for t in range(len(tiles) - 2, len(tiles)):
        tile_put(t).wait()
    for q in range(DENSE_PARTS):
        for turn in range(1, dp):
            spread(turn, q).wait()
    total = copies_f[0].astype(f32)
    for r in range(1, dp):
        total += copies_f[r].astype(f32)
    dense_ref[...] = total.astype(bf16)
    for t in range(len(tiles)):
        for turn in range(1, dp):
            spread_tile(turn, t).wait_send()
    for d, k, q in work:
        if d is not None:
            send(d, k, q).wait_send()


def backward(n, dp, own_d, other_d, wall, grad_gu, grad_down, others, collective_id):
    half, ring = n // 4, n // 2
    rows, width = own_d.shape[1:]
    full_width = wall.shape[1]
    qkv_width = full_width - width - 128
    shard = wall.shape[0] // n
    q_width = others[9].shape[1]
    return pl.pallas_call(
        functools.partial(backward_kernel, n, dp),
        out_shape=[
            jax.ShapeDtypeStruct((rows, width), bf16),
            jax.ShapeDtypeStruct((rows, width), bf16),
            jax.ShapeDtypeStruct((shard, full_width), bf16),
            jax.ShapeDtypeStruct(grad_gu.shape, bf16),
            jax.ShapeDtypeStruct(grad_down.shape, bf16),
            jax.ShapeDtypeStruct((dp,) + grad_gu.shape, bf16),
            jax.ShapeDtypeStruct((dp,) + grad_down.shape, bf16),
        ],
        in_specs=[ANY] * 5 + [VMEM] * len(others),
        out_specs=[VMEM] * 3 + [ANY] * 4,
        scratch_shapes=[
            pltpu.VMEM((width, qkv_width), bf16),
            pltpu.VMEM((width, 128), bf16),
            pltpu.VMEM((rows, width), f32),
            pltpu.VMEM((rows, width), bf16),
            pltpu.VMEM((rows, q_width), bf16),
            pltpu.VMEM((rows, qkv_width), bf16),
            pltpu.VMEM((rows, width), f32),
            pltpu.VMEM((width, 128), f32),
            pltpu.VMEM((rows, 128), bf16),
            pltpu.VMEM((ring, shard, full_width), bf16),
            pltpu.VMEM((2, shard, full_width), bf16),
            pltpu.VMEM((ring, shard, full_width), bf16),
            pltpu.VMEM((2, half, shard, full_width), bf16),
            pltpu.VMEM((dp, shard, full_width), bf16),
            DMA((3,)),
            DMA((2,)),
            DMA((ring,)),
            DMA((2, half, DENSE_PARTS)),
            DMA((2, half, DENSE_PARTS)),
            DMA((dp, DENSE_PARTS)),
            DMA((dp, DENSE_PARTS)),
            DMA((dp, (width + grad_down.shape[0]) // rows)),
            DMA((dp, (width + grad_down.shape[0]) // rows)),
            DMA((2, dp)),
            DMA((2,)),
        ]
        + reduce_scratch(rows, width, half, 2),
        compiler_params=pltpu.CompilerParams(
            collective_id=collective_id, has_side_effects=True, vmem_limit_bytes=63 * MB
        ),
    )(own_d, other_d, wall, grad_gu, grad_down, *others)[:5]


def finish_kernel(
    experts_n, output_in, grad_in, dense_in, gu_in, down_in, output, grad, q, kv, out, router, one, two, gate, up, down
):
    output[...] = output_in[...]
    grad[...] = grad_in[...]
    hidden_width = gate.shape[1]
    gate[...] = gu_in[:, pl.ds(0, hidden_width)].astype(f32)
    up[...] = gu_in[:, pl.ds(hidden_width, hidden_width)].astype(f32)
    down[...] = down_in[...].astype(f32)

    @pl.when(pl.program_id(0) == 0)
    def _():
        start = 0
        for ref in (q, kv):
            ref[...] = dense_in[:, pl.ds(start, ref.shape[1])].astype(f32)
            start += ref.shape[1]
        extra = dense_in[:, pl.ds(start, 128)].astype(f32)
        router[...] = extra[:, :experts_n]
        turned = jnp.transpose(extra)
        one[...] = turned[experts_n : experts_n + 1]
        two[...] = turned[experts_n + 1 : experts_n + 2]
        out[...] = dense_in[:, pl.ds(start + 128, out.shape[1])].astype(f32)


def finish(output, grad, dense, gu, down, experts_n, q_width, kv_width):
    steps = 8
    rows, width = output.shape
    shard = dense.shape[0]
    hidden_width = gu.shape[1] // 2

    def tiles(a, b):
        return pl.BlockSpec((a // steps, b), lambda i: (i, 0))

    def whole(a, b):
        return pl.BlockSpec((a, b), lambda i: (0, 0))

    shape = jax.ShapeDtypeStruct
    return pl.pallas_call(
        functools.partial(finish_kernel, experts_n),
        grid=(steps,),
        in_specs=[
            tiles(rows, width),
            tiles(rows, width),
            whole(*dense.shape),
            tiles(*gu.shape),
            tiles(*down.shape),
        ],
        out_specs=[
            tiles(rows, width),
            tiles(rows, width),
            whole(shard, q_width),
            whole(shard, kv_width),
            whole(shard, width),
            whole(shard, experts_n),
            whole(1, shard),
            whole(1, shard),
            tiles(gu.shape[0], hidden_width),
            tiles(gu.shape[0], hidden_width),
            tiles(*down.shape),
        ],
        out_shape=[
            shape((rows, width), bf16),
            shape((rows, width), bf16),
            shape((shard, q_width), f32),
            shape((shard, kv_width), f32),
            shape((shard, width), f32),
            shape((shard, experts_n), f32),
            shape((1, shard), f32),
            shape((1, shard), f32),
            shape((gu.shape[0], hidden_width), f32),
            shape((gu.shape[0], hidden_width), f32),
            shape(down.shape, f32),
        ],
        compiler_params=pltpu.CompilerParams(vmem_limit_bytes=63 * MB),
    )(output, grad, dense, gu, down)


QUARTERS = 4


def expert_kernel(
    n,
    x_ref,
    dog_ref,
    gates_ref,
    gate_any,
    up_any,
    wd_any,
    de_ref,
    dgates_ref,
    ggu_out,
    gd_out,
    od_ref,
    sd_ref,
    oe_ref,
    se_ref,
    xg_ref,
    hg_ref,
    wgu_ref,
    wd_ref,
    ggu_ref,
    gd_ref,
    acc_gu,
    acc_d,
    gate_in,
    dgate_out,
    xbuf,
    dobuf,
    pd,
    pe,
    hbuf,
    own_sem,
    weight_sem,
    ring_s,
    ring_r,
    cross_s,
    cross_r,
    load_sem,
    put_sem,
    sib_r,
    gate_s,
    gate_r,
    dgate_s,
    dgate_r,
    *reduce_refs,
):
    place = Place(n)
    half, ring, me = place.half, place.ring, place.me
    rows, width = x_ref.shape
    hidden_width = wd_ref.shape[0]
    piece = rows // QUARTERS
    weight_copies = [
        pltpu.make_async_copy(gate_any, wgu_ref.at[:, pl.ds(0, hidden_width)], weight_sem.at[0]),
        pltpu.make_async_copy(up_any, wgu_ref.at[:, pl.ds(hidden_width, hidden_width)], weight_sem.at[1]),
        pltpu.make_async_copy(wd_any, wd_ref, weight_sem.at[2]),
    ]
    for copy in weight_copies:
        copy.start()
    pltpu.make_async_copy(x_ref, xbuf.at[0], load_sem.at[0, 0]).start()
    pltpu.make_async_copy(dog_ref.at[me], dobuf.at[0], load_sem.at[1, 0]).start()
    meet_all(place)

    own = pltpu.make_async_copy(xbuf.at[0], xg_ref.at[me], own_sem.at[0])

    def at(q):
        return pl.ds(pl.multiple_of(q * piece, piece), piece)

    def block_of(d, k):
        return jnp.where(d == 0, place.device(-k), place.device(k))

    def along(d, k, q, first=False):
        b = me if first else block_of(d, k - 1)
        return remote(
            x_ref.at[at(q)] if first else xg_ref.at[b, at(q)],
            xg_ref.at[b, at(q)],
            ring_s.at[d, k - 1, q],
            ring_r.at[d, k - 1, q],
            jnp.where(d == 0, place.right, place.left),
        )

    def across(d, k, q, first=False):
        b = me if first else block_of(d, k)
        src = x_ref.at[at(q)] if first else xg_ref.at[b, at(q)]
        return remote(src, xg_ref.at[b, at(q)], cross_s.at[d, k, q], cross_r.at[d, k, q], place.sibling)

    def gate_copy(d):
        to = lax.rem(me + d, n)
        return remote(gates_ref.at[to], gate_in.at[me], gate_s.at[d], gate_r.at[d], to)

    for q in range(QUARTERS):
        for d in (0, 1):
            along(d, 1, q, first=True).start()
        across(0, 0, q, first=True).start()

    @pl.loop(1, n)
    def _(d):
        gate_copy(d).start()

    gate_in[me] = gates_ref[me]
    acc_gu[...] = jnp.zeros_like(acc_gu)
    acc_d[...] = jnp.zeros_like(acc_d)

    def step_of(i):
        late = jnp.where(i < n - 4, i, jnp.where(i < n - 2, i + 2, i - 2))
        k = jnp.where(late < 2, 0, lax.div(late + 2, 4))
        j = jnp.where(late < 2, late, lax.rem(late + 2, 4))
        edge = jnp.logical_or(k == 0, k == half)
        d = jnp.where(edge, 0, lax.rem(j, 2))
        other = jnp.where(edge, j, lax.div(j, 2))
        chip = jnp.where(d == 0, place.chip_at(-k), place.chip_at(k))
        core = jnp.where(other == 0, place.core, 1 - place.core)
        return k, j, d, other, chip, chip * 2 + core

    def pump(d, k, q, last=False):
        along(d, k, q).wait_recv()
        if not last:
            near = jnp.where(q < QUARTERS // 2, 0, 1) == d

            @pl.when(jnp.logical_or(k + 1 < half, near))
            def _():
                along(d, k + 1, q).start()

        across(d, k, q).start()

    def load(block, slot):
        return (
            pltpu.make_async_copy(xg_ref.at[block], xbuf.at[slot], load_sem.at[0, slot]),
            pltpu.make_async_copy(dog_ref.at[block], dobuf.at[slot], load_sem.at[1, slot]),
        )

    def put_wait(slot):
        for which, buf in enumerate((pd, pe, hbuf)):
            pltpu.make_async_copy(buf.at[slot], buf.at[slot], put_sem.at[which, slot]).wait()

    def dgate_copy(block):
        d = lax.rem(block - me + n, n)
        return remote(dgate_out.at[block], dgates_ref.at[me], dgate_s.at[d], dgate_r.at[d], block)

    def load_rest(block, slot):
        return (
            pltpu.make_async_copy(xg_ref.at[block], xbuf.at[slot], load_sem.at[0, slot]),
            pltpu.make_async_copy(dog_ref.at[block], dobuf.at[slot], load_sem.at[1, slot]),
            pltpu.make_async_copy(hg_ref.at[block], hbuf.at[slot], load_sem.at[2, slot]),
        )

    for copy in weight_copies:
        copy.wait()

    def work_on(i):
        k, j, d, other, chip, block = step_of(i)
        slot = lax.rem(i, 2)
        for copy in load(block, slot):
            copy.wait()

        @pl.when(i == 0)
        def _():
            own.start()

        @pl.when(i > 0)
        def _():
            away = lax.rem(me - block + n, n)
            remote(gate_in.at[block], gate_in.at[block], gate_s.at[away], gate_r.at[away], place.sibling).wait_recv()

        gate = jnp.transpose(gate_in[block])[:, :1]
        x = xbuf[slot]
        gu = mul(x, wgu_ref[...], 1, 0)
        g, u = gu[:, :hidden_width], gu[:, hidden_width:]
        s = 1.0 / (1.0 + jnp.exp(-g))
        gs = g * s
        hid = gs * u
        hidg = (hid * gate).astype(bf16)

        @pl.when(jnp.logical_and(i >= 2, i < n - 2))
        def _():
            put_wait(slot)

        pd[slot] = mul(hidg, wd_ref[...], 1, 0).astype(bf16)

        @pl.when(i < 2)
        def _():
            for t in range(2):
                for dd in (0, 1):
                    pump(dd, 1, i * 2 + t)

        @pl.when(jnp.logical_and(i >= 2, k + 1 < half))
        def _():
            for dd in (0, 1):
                pump(dd, k + 1, j)

        @pl.when(jnp.logical_and(k + 1 == half, j < 2))
        def _():
            for dd in (0, 1):
                pump(dd, half, j + dd * (QUARTERS // 2), last=True)

        nk, nj, nd, nother, nchip, nblock = step_of(i + 1)

        @pl.when(jnp.logical_and(i + 1 < n, nother == 1))
        def _():
            for q in range(QUARTERS):
                dd = jnp.where(nk == half, 0 if q < QUARTERS // 2 else 1, nd)
                b = nblock
                remote(
                    xg_ref.at[b, at(q)], xg_ref.at[b, at(q)], cross_s.at[dd, nk, q], cross_r.at[dd, nk, q], place.sibling
                ).wait_recv()

        @pl.when(i == 0)
        def _():
            own.wait()

        @pl.when(i + 1 < n)
        def _():
            for copy in load(nblock, 1 - slot):
                copy.start()

        do = dobuf[slot]
        dh = mul(do, wd_ref[...], 1, 1)
        dgate = jnp.sum(dh * hid, axis=1, keepdims=True)
        dgate_out[block] = jnp.transpose(jnp.broadcast_to(dgate, (rows, 128)))[:8]
        dh = dh * gate
        d_g = (dh * u * s * (1.0 + g * (1.0 - s))).astype(bf16)
        d_u = (dh * gs).astype(bf16)
        dgu = jnp.concatenate([d_g, d_u], axis=1)
        hbuf[slot] = jnp.concatenate([d_g, d_u, hidg], axis=1)
        pltpu.make_async_copy(hbuf.at[slot], hg_ref.at[block], put_sem.at[2, slot]).start()
        pe[slot] = mul(dgu, wgu_ref[...], 1, 1).astype(bf16)

        @pl.when(i > 0)
        def _():
            dgate_copy(block).start()

        @pl.when(i == 0)
        def _():
            dgates_ref[me] = dgate_out[me]

        @pl.when(other == 0)
        def _():
            pltpu.make_async_copy(pd.at[slot], od_ref.at[chip], put_sem.at[0, slot]).start()
            pltpu.make_async_copy(pe.at[slot], oe_ref.at[chip], put_sem.at[1, slot]).start()

        @pl.when(other == 1)
        def _():
            remote(pd.at[slot], sd_ref.at[chip], put_sem.at[0, slot], sib_r.at[0, chip], place.sibling).start()
            remote(pe.at[slot], se_ref.at[chip], put_sem.at[1, slot], sib_r.at[1, chip], place.sibling).start()

    @pl.loop(0, n - 2)
    def _(i):
        work_on(i)

    put_wait(0)
    put_wait(1)

    def other_wait(chip):
        remote(se_ref.at[chip], se_ref.at[chip], put_sem.at[1, 0], sib_r.at[1, chip], place.sibling).wait_recv()

    def write(at, columns, total):
        de_ref[at, columns] = total

    back = ring_reduce(
        place, lambda chip: oe_ref.at[chip], lambda chip: se_ref.at[chip], other_wait, width, write, reduce_refs, 2
    )
    next(back)
    next(back)

    @pl.loop(n - 2, n)
    def _(i):
        work_on(i)

    put_wait(0)
    put_wait(1)

    for copy in load_rest(0, 0):
        copy.start()

    def gradients(first, last):
        @pl.loop(first, last)
        def _(b):
            slot = lax.rem(b, 2)
            for copy in load_rest(b, slot):
                copy.wait()

            @pl.when(b + 1 < n)
            def _():
                for copy in load_rest(b + 1, 1 - slot):
                    copy.start()

            acc_gu[...] += mul(xbuf[slot], hbuf[slot, :, pl.ds(0, 2 * hidden_width)], 0, 0)
            acc_d[...] += mul(hbuf[slot, :, pl.ds(2 * hidden_width, hidden_width)], dobuf[slot], 0, 0)

    steps = len(ring_work(half, 2)) // 2 - 2
    for step in range(steps):
        next(back)
        next(back)
        gradients(n * step // steps, n * (step + 1) // steps)
    ggu_ref[...] = acc_gu[...].astype(bf16)
    gd_ref[...] = acc_d[...].astype(bf16)
    out_copies = [
        pltpu.make_async_copy(ggu_ref, ggu_out, weight_sem.at[0]),
        pltpu.make_async_copy(gd_ref, gd_out, weight_sem.at[1]),
    ]
    for copy in out_copies:
        copy.start()
    for _ in back:
        pass
    for copy in out_copies:
        copy.wait()

    @pl.loop(0, ring)
    def _(chip):
        remote(sd_ref.at[chip], sd_ref.at[chip], put_sem.at[0, 0], sib_r.at[0, chip], place.sibling).wait_recv()

    @pl.loop(1, n)
    def _(d):
        gate_copy(d).wait_send()
        source = lax.rem(me - d + n, n)
        remote(dgates_ref.at[source], dgates_ref.at[source], dgate_s.at[d], dgate_r.at[d], place.sibling).wait()

    for q in range(QUARTERS):
        across(0, 0, q, first=True).wait_send()
        for d in (0, 1):
            for k in range(1, half + 1):
                if k < half or ((q < QUARTERS // 2) == (d == 0)):
                    along(d, k, q).wait_send()
                    across(d, k, q).wait_send()


def experts(n, mixed_in, d_gathered, gate_rows, gate_w, up_w, wd, collective_id):
    half, ring = n // 4, n // 2
    rows, width = mixed_in.shape
    blocks = jax.ShapeDtypeStruct((ring, rows, width), bf16)
    hidden_width = wd.shape[0]
    both = (width, 2 * hidden_width)
    out = pl.pallas_call(
        functools.partial(expert_kernel, n),
        out_shape=[
            jax.ShapeDtypeStruct((rows, width), f32),
            jax.ShapeDtypeStruct((n, 8, rows), f32),
            jax.ShapeDtypeStruct(both, bf16),
            jax.ShapeDtypeStruct(wd.shape, bf16),
            blocks,
            blocks,
            blocks,
            blocks,
            jax.ShapeDtypeStruct((n, rows, width), bf16),
            jax.ShapeDtypeStruct((n, rows, 3 * hidden_width), bf16),
        ],
        in_specs=[ANY, ANY, VMEM, ANY, ANY, ANY],
        out_specs=[VMEM, VMEM] + [ANY] * 8,
        scratch_shapes=[
            pltpu.VMEM(both, bf16),
            pltpu.VMEM(wd.shape, bf16),
            pltpu.VMEM(both, bf16),
            pltpu.VMEM(wd.shape, bf16),
            pltpu.VMEM(both, f32),
            pltpu.VMEM(wd.shape, f32),
            pltpu.VMEM((n, 8, rows), f32),
            pltpu.VMEM((n, 8, rows), f32),
            pltpu.VMEM((2, rows, width), bf16),
            pltpu.VMEM((2, rows, width), bf16),
            pltpu.VMEM((2, rows, width), bf16),
            pltpu.VMEM((2, rows, width), bf16),
            pltpu.VMEM((2, rows, 3 * hidden_width), bf16),
            DMA((1,)),
            DMA((3,)),
            DMA((2, half, QUARTERS)),
            DMA((2, half, QUARTERS)),
            DMA((2, half + 1, QUARTERS)),
            DMA((2, half + 1, QUARTERS)),
            DMA((3, 2)),
            DMA((3, 2)),
            DMA((2, ring)),
            DMA((n,)),
            DMA((n,)),
            DMA((n,)),
            DMA((n,)),
        ]
        + reduce_scratch(rows, width, half, 2),
        compiler_params=pltpu.CompilerParams(
            collective_id=collective_id, has_side_effects=True, vmem_limit_bytes=62 * MB
        ),
    )(mixed_in, d_gathered, gate_rows, gate_w, up_w, wd)
    return out[:6]


def rope_tables(length):
    inverse = np.float32(10000.0) ** (-np.arange(HD // 2, dtype=np.float32) / np.float32(HD // 2))
    angles = np.arange(length, dtype=np.float32)[:, None] * inverse.astype(np.float32)[None, :]
    return [np.tile(table(angles).astype(np.float32), (1, 4)) for table in (np.cos, np.sin)]


def per_device(
    n,
    dp,
    tokens,
    cotangent,
    lengths,
    routes,
    norm1_gain,
    w_query,
    w_kv,
    w_out,
    norm2_gain,
    w_router,
    expert_gate,
    expert_up,
    expert_down,
):
    tok_rows, model_width = tokens.shape
    expert_count = w_router.shape[1]
    kv_width, q_width = w_kv.shape[1], w_query.shape[1]
    shard = w_query.shape[0]
    extra = jnp.concatenate(
        [
            w_router,
            norm1_gain[:, None],
            norm2_gain[:, None],
            jnp.zeros((shard, 128 - expert_count - 2), bf16),
        ],
        axis=1,
    )
    turns = rope_tables(tok_rows)
    (
        wall,
        d_gathered,
        d_out_low,
        queries,
        keys,
        values,
        normed_t,
        attended_t,
        middle,
        mixed_in,
        gates,
        gate_rows,
        gains,
    ) = forward(n, dp, w_query, w_kv, extra, w_out, lengths, cotangent, tokens, routes, turns, 0)
    wall = wall.reshape(-1, wall.shape[-1])
    d_mixed_experts, d_gate_rows, grad_gu, grad_down, own_d, other_d = experts(
        n, mixed_in, d_gathered, gate_rows, expert_gate[0], expert_up[0], expert_down[0], 1
    )

    sums = backward(
        n,
        dp,
        own_d,
        other_d,
        wall,
        grad_gu,
        grad_down,
        (
            d_mixed_experts,
            d_gate_rows,
            gates,
            middle,
            mixed_in,
            d_out_low,
            tokens,
            normed_t,
            attended_t,
            queries,
            keys,
            values,
            *turns,
            gains,
        ),
        2,
    )
    output, input_grad, grad_q, grad_kv, grad_out, router, gain_one, gain_two, gate, up, down = finish(
        *sums, expert_count, q_width, kv_width
    )
    return (
        output,
        input_grad,
        gain_one.reshape(-1),
        grad_q,
        grad_kv,
        grad_out,
        gain_two.reshape(-1),
        router,
        gate[None],
        up[None],
        down[None],
    )


def solution(mesh):
    rows, own = P(("dp", "expert"), None), P("expert", None)
    expert = P("expert", None, None)
    return jax.shard_map(
        functools.partial(per_device, mesh.shape["expert"], mesh.shape["dp"]),
        mesh=mesh,
        in_specs=(rows, rows, P(("dp", "expert")), rows, P("expert"), own, own, own, P("expert"), own)
        + (expert,) * 3,
        out_specs=(rows, rows, P("expert"), own, own, own, P("expert"), own) + (expert,) * 3,
        check_vma=False,
    )
```

```python
import functools

import jax
import jax.numpy as jnp
import numpy as np
from jax import lax
from jax.experimental import pallas as pl
from jax.experimental.pallas import tpu as pltpu
from jax.sharding import PartitionSpec as P

HD = 64
EPSILON = 1e-05
MESH = pl.DeviceIdType.MESH
ANY = pl.BlockSpec(memory_space=pl.ANY)
VMEM = pl.BlockSpec(memory_space=pltpu.VMEM)
DMA = pltpu.SemaphoreType.DMA
MB = 2**20
f32 = jnp.float32
bf16 = jnp.bfloat16


def mul(a, b, ca, cb):
    return lax.dot_general(a, b, (((ca,), (cb,)), ((), ())), preferred_element_type=f32)


class Place:
    def __init__(self, n):
        self.n, self.mid, self.ring = n, n // 8, n // 2
        self.half = self.ring // 2
        self.me = lax.axis_index("expert")
        self.chip, self.core = lax.div(self.me, 2), lax.rem(self.me, 2)
        outer, inner = lax.div(self.chip, self.mid), lax.rem(self.chip, self.mid)
        row = 3 - outer
        step = jnp.where(lax.rem(row, 2) == 0, inner - 1, self.mid - 1 - inner)
        self.at = jnp.where(inner == 0, outer, 4 + row * (self.mid - 1) + step)
        self.sibling = self.chip * 2 + 1 - self.core
        self.right, self.left = self.device(1), self.device(-1)

    def chip_at(self, distance):
        p = lax.rem(self.at + distance + self.ring, self.ring)
        wide = max(self.mid - 1, 1)
        row, k = lax.div(lax.max(p - 4, 0), wide), lax.rem(lax.max(p - 4, 0), wide)
        inner = jnp.where(lax.rem(row, 2) == 0, 1 + k, self.mid - 1 - k)
        return jnp.where(p < 4, p * self.mid, (3 - row) * self.mid + inner)

    def device(self, distance):
        return self.chip_at(distance) * 2 + self.core


def remote(src, dst, send, recv, device):
    return pltpu.make_async_remote_copy(
        src_ref=src, dst_ref=dst, send_sem=send, recv_sem=recv, device_id={"expert": device}, device_id_type=MESH
    )


def meet(targets):
    barrier = pltpu.get_barrier_semaphore()
    for target in targets:
        pl.semaphore_signal(barrier, inc=1, device_id={"expert": target}, device_id_type=MESH)
    pl.semaphore_wait(barrier, len(targets))


def meet_all(place):
    barrier = pltpu.get_barrier_semaphore()

    @pl.loop(1, place.n)
    def _(d):
        other = lax.rem(place.me + d, place.n)
        pl.semaphore_signal(barrier, inc=1, device_id={"expert": other}, device_id_type=MESH)

    pl.semaphore_wait(barrier, place.n - 1)


def column_cuts(width, parts):
    tiles = width // 128
    edges = [128 * (tiles * i // parts) for i in range(parts + 1)]
    return [(edges[i], edges[i + 1] - edges[i]) for i in range(parts)]


PARTS = 2


def forward_kernel(
    n,
    dp,
    w_query_ref,
    w_kv_ref,
    w_extra_ref,
    w_out_ref,
    lengths_ref,
    cotangent_ref,
    tokens_ref,
    routes_ref,
    cos_ref,
    sin_ref,
    wallg_ref,
    doutg_ref,
    dout_ref,
    q_ref,
    k_ref,
    v_ref,
    normed_t_ref,
    attended_t_ref,
    middle_ref,
    mixed_ref,
    gates_ref,
    gate_rows_ref,
    gains_ref,
    wall_ref,
    weights,
    proj,
    attended,
    own_sem,
    piece_sem,
    load_sem,
    ss,
    rs,
    css,
    crs,
    xs,
    xr,
    xcs,
    xcr,
):
    place = Place(n)
    half, me = place.half, place.me
    rank = lax.axis_index("dp")
    helping = dp == 2
    rows, width = tokens_ref.shape
    shard = wall_ref.shape[0]
    q_width, kv_width = q_ref.shape[1], 2 * k_ref.shape[1]
    qkv_width = q_width + kv_width
    near = qkv_width + 128
    edges = (0, q_width, qkv_width, near, near + width)
    pieces = [
        pltpu.make_async_copy(ref, wall_ref.at[:, pl.ds(edges[i], edges[i + 1] - edges[i])], piece_sem.at[i])
        for i, ref in enumerate((w_query_ref, w_kv_ref, w_extra_ref, w_out_ref))
    ]
    for copy in pieces:
        copy.start()
    barrier = pltpu.get_barrier_semaphore()
    for target in (place.right, place.left, place.sibling):
        pl.semaphore_signal(barrier, inc=1, device_id={"expert": target}, device_id_type=MESH)
    if helping:
        pl.semaphore_signal(barrier, inc=1, device_id={"dp": 1 - rank}, device_id_type=MESH)
    pl.semaphore_wait(barrier, 4 if helping else 3)
    for copy in pieces:
        copy.wait()
    started = []

    def begin(copy):
        copy.start()
        started.append(copy)

    alone = 128 * (edges[4] // 128 * 10 // 33)
    shared = (2 * alone, edges[4] - 2 * alone)
    if helping:
        cut_weights = (
            [(pl.multiple_of(rank * alone, 128), alone), shared],
            {0: (pl.multiple_of((1 - rank) * alone, 128), alone)},
        )
    else:
        cut_weights = (column_cuts(edges[4], PARTS), {})
    flows = (
        (wall_ref, wallg_ref, cut_weights, weights),
        (dout_ref, doutg_ref, (column_cuts(width, PARTS), {}), None),
    )

    def block_at(d, k):
        return me if k == 0 else (place.device(-k) if d == 0 else place.device(k))

    def sibling_of(b):
        return b + 1 - 2 * lax.rem(b, 2)

    def spot(a, b, cut, own=False):
        x_ref, o_ref = flows[a][:2]
        return (x_ref if own else o_ref.at[b]).at[:, pl.ds(*cut)]

    def along(a, d, k, q):
        b, cut = block_at(d, k - 1), flows[a][2][0][q]
        target = place.right if d == 0 else place.left
        return remote(spot(a, b, cut, k == 1), spot(a, b, cut), ss.at[a, d, k - 1, q], rs.at[a, d, k - 1, q], target)

    def across(a, d, k, q):
        b, cut = block_at(d, k), flows[a][2][0][q]
        return remote(
            spot(a, b, cut, k == 0), spot(a, b, cut), css.at[a, d, k, q], crs.at[a, d, k, q], place.sibling
        )

    def over(a, d, k, q):
        b, cut = block_at(d, k), flows[a][2][0][q]
        return pltpu.make_async_remote_copy(
            src_ref=spot(a, b, cut),
            dst_ref=spot(a, b, cut),
            send_sem=xs.at[a, d, k, q],
            recv_sem=xr.at[a, d, k, q],
            device_id={"dp": 1 - rank},
            device_id_type=MESH,
        )

    def over_across(a, d, k, q):
        b, cut = block_at(d, k), flows[a][2][1][q]
        return remote(spot(a, b, cut, k == 0), spot(a, b, cut), xcs.at[a, d, k, q], xcr.at[a, d, k, q], place.sibling)

    def take(a, b, cut, own=False):
        local = flows[a][3]
        if local is not None:
            at = pl.ds(pl.multiple_of(b * shard, 16), shard)
            pltpu.make_async_copy(spot(a, b, cut, own), local.at[at, pl.ds(*cut)], load_sem.at[0]).start()

    def first(a):
        parts, others = flows[a][2]
        for q in range(PARTS):
            begin(along(a, 0, 1, q))
            begin(along(a, 1, 1, q))
            begin(across(a, 0, 0, q))
            take(a, me, parts[q], True)
            if q in others:
                begin(over_across(a, 0, 0, q))
                take(a, me, others[q], True)

    def arrive(a, d, k, q):
        parts, others = flows[a][2]
        along(a, d, k, q).wait_recv()
        if k < half and goes(d, k + 1, q, half, PARTS):
            begin(along(a, d, k + 1, q))
        if q in others:
            begin(over(a, d, k, q))
        begin(across(a, d, k, q))
        take(a, block_at(d, k), parts[q])

    def places(k):
        return [
            (d, q)
            for q in range(PARTS)
            for d in (0, 1)
            if (k == 0 and d == 0) or (k > 0 and goes(d, k, q, half, PARTS))
        ]

    def aside(a, k):
        parts, others = flows[a][2]
        for d, q in places(k) if k > 0 else ():
            if q in others:
                b = block_at(d, k)
                piece = spot(a, b, others[q])
                remote(piece, piece, xs.at[a, d, k, q], xr.at[a, d, k, q], place.sibling).wait_recv()
                begin(over_across(a, d, k, q))
                take(a, b, others[q])
        for d, q in places(k):
            b = sibling_of(block_at(d, k))
            piece = spot(a, b, parts[q])
            remote(piece, piece, css.at[a, d, k, q], crs.at[a, d, k, q], place.sibling).wait_recv()
            take(a, b, parts[q])

    def aside_over(a, k):
        others = flows[a][2][1]
        for d, q in places(k):
            if q in others:
                b = sibling_of(block_at(d, k))
                piece = spot(a, b, others[q])
                remote(piece, piece, xcs.at[a, d, k, q], xcr.at[a, d, k, q], place.sibling).wait_recv()
                take(a, b, others[q])

    events, ends = [functools.partial(first, 0)], []
    for a in range(len(flows)):
        for k in range(1, half + 1):
            events += [functools.partial(arrive, a, d, k, q) for d, q in places(k)]
            if k == half - 1 and a + 1 < len(flows):
                events.append(functools.partial(first, a + 1))
            events.append(functools.partial(aside, a, k - 1))
            if k >= 2:
                events.append(functools.partial(aside_over, a, k - 2))
        events.append(functools.partial(aside, a, half))
        events += [functools.partial(aside_over, a, k) for k in (half - 1, half)]
        ends.append(len(events))
    done = [0]

    def pump(last):
        while done[0] < last:
            events[done[0]]()
            done[0] += 1

    own = [
        pltpu.make_async_copy(x_ref, o_ref.at[me], own_sem.at[i])
        for i, (x_ref, o_ref) in enumerate(((wall_ref, wallg_ref), (dout_ref, doutg_ref)))
    ]
    alive = lax.broadcasted_iota(jnp.int32, (rows, width), 0) < lengths_ref[0]
    dout_ref[...] = jnp.where(alive, cotangent_ref[...].astype(f32), 0.0).astype(bf16)
    pump(1)
    for copy in own:
        copy.start()
    pump(ends[0])
    pltpu.make_async_copy(weights, weights, load_sem.at[0]).wait()

    lane = lax.broadcasted_iota(jnp.int32, (rows, 128), 1)
    turned = jnp.transpose(weights[:, pl.ds(qkv_width, 128)].astype(f32))
    gains_ref[...] = jnp.concatenate([turned[n : n + 1], turned[n + 1 : n + 2], jnp.zeros((6, width), f32)], axis=0)
    inputs = tokens_ref[...].astype(f32)
    inv = lax.rsqrt(jnp.mean(inputs * inputs, axis=1, keepdims=True) + EPSILON)
    normed = (inputs * inv * gains_ref[0:1]).astype(bf16)
    proj[...] = mul(normed, weights[:, pl.ds(0, qkv_width)], 1, 0)
    normed_t_ref[...] = jnp.transpose(normed)
    cosine, sine = cos_ref[...], sin_ref[...]
    sine_on = jnp.where(lane % HD < HD // 2, -sine, sine)

    def turn(at):
        block = proj[:, at]
        return (block * cosine + swap_halves(block, lane) * sine_on).astype(bf16)

    for b in range(q_width // 128):
        q_ref[:, pl.ds(128 * b, 128)] = turn(pl.ds(128 * b, 128))
    for b in range(kv_width // 256):
        k_ref[:, pl.ds(128 * b, 128)] = turn(pl.ds(q_width + 128 * b, 128))
    v_ref[...] = proj[:, pl.ds(q_width + kv_width // 2, kv_width // 2)].astype(bf16)
    t_at = lax.broadcasted_iota(jnp.int32, (rows, rows), 0)
    u_at = lax.broadcasted_iota(jnp.int32, (rows, rows), 1)
    causal = t_at >= u_at
    kv_count = k_ref.shape[1] // HD
    per_group = q_width // HD // kv_count
    kept = None
    for g in range(kv_count):
        pair = pl.ds(128 * (g // 2), 128)
        k_parts = head_halves(k_ref[:, pair].astype(f32), lane, g % 2)
        v_parts = head_halves(v_ref[:, pair].astype(f32), lane, g % 2)
        for h in range(per_group * g, per_group * (g + 1)):
            at = pl.ds(128 * (h // 2), 128)
            probs = softmax_rows(q_ref[:, at], k_parts[h % 2], causal).astype(bf16)
            kept_new = mul(probs, v_parts[h % 2], 1, 0)
            if h % 2 == 0:
                kept = kept_new
            else:
                attended[:, at] = (kept + kept_new).astype(bf16)
        pump(ends[0] + 4 * (g + 1) // kv_count)
    attended_t_ref[...] = jnp.transpose(attended[...])
    middle_ref[...] = tokens_ref[...].astype(f32) + mul(attended[...], weights[:, pl.ds(near, width)], 1, 0)
    pump(ends[0] + 6)
    tile = 32

    @pl.loop(0, rows // tile)
    def _(r):
        at = pl.ds(pl.multiple_of(r * tile, tile), tile)
        middle = middle_ref[at]
        scale = lax.rsqrt(jnp.mean(middle * middle, axis=1, keepdims=True) + EPSILON)
        mixed_ref[at] = (middle * scale * gains_ref[1:2]).astype(bf16)

    pump(ends[0] + 8)
    logits = mul(mixed_ref[...], weights[:, pl.ds(qkv_width, 128)], 1, 0)
    chosen = lane == routes_ref[:, 0:1]
    for choice in range(1, routes_ref.shape[1]):
        chosen = jnp.logical_or(chosen, lane == routes_ref[:, choice : choice + 1])
    logits = jnp.where(chosen, logits, -1e30)
    e = jnp.where(chosen, jnp.exp(logits - jnp.max(logits, axis=1, keepdims=True)), 0.0)
    gates = e / jnp.sum(e, axis=1, keepdims=True)
    gates_ref[...] = gates
    across_gates = jnp.transpose(gates)
    for e in range(n):
        gate_rows_ref[e] = jnp.broadcast_to(across_gates[e : e + 1], (8, rows))
    pump(ends[1])
    for copy in own:
        copy.wait()
    for copy in started:
        copy.wait_send()


def forward(n, dp, w_query, w_kv, w_extra, w_out, lengths, cotangent, tokens, routes, turns, collective_id):
    half = n // 4
    rows, width = tokens.shape
    shard, q_width = w_query.shape
    kv_width = w_kv.shape[1]
    full_width = q_width + kv_width + 128 + width
    shape = jax.ShapeDtypeStruct
    return pl.pallas_call(
        functools.partial(forward_kernel, n, dp),
        out_shape=[
            shape((n, shard, full_width), bf16),
            shape((n, rows, width), bf16),
            shape((rows, width), bf16),
            shape((rows, q_width), bf16),
            shape((rows, kv_width // 2), bf16),
            shape((rows, kv_width // 2), bf16),
            shape((width, rows), bf16),
            shape((q_width, rows), bf16),
            shape((rows, width), f32),
            shape((rows, width), bf16),
            shape((rows, 128), f32),
            shape((n, 8, rows), f32),
            shape((8, width), f32),
        ],
        in_specs=[ANY] * 4 + [pl.BlockSpec(memory_space=pltpu.SMEM)] + [VMEM] * 5,
        out_specs=[ANY] * 2 + [VMEM] * 11,
        scratch_shapes=[
            pltpu.VMEM((shard, full_width), bf16),
            pltpu.VMEM((width, full_width), bf16),
            pltpu.VMEM((rows, q_width + kv_width), f32),
            pltpu.VMEM((rows, q_width), bf16),
            DMA((2,)),
            DMA((4,)),
            DMA((1,)),
            DMA((2, 2, half, PARTS)),
            DMA((2, 2, half, PARTS)),
            DMA((2, 2, half + 1, PARTS)),
            DMA((2, 2, half + 1, PARTS)),
        ]
        + [DMA((1, 2, half + 1, PARTS)) for _ in range(4)],
        compiler_params=pltpu.CompilerParams(
            collective_id=collective_id, has_side_effects=True, vmem_limit_bytes=56 * MB
        ),
    )(w_query, w_kv, w_extra, w_out, lengths, cotangent, tokens, routes, *turns)


SLOTS = 4


def ring_work(half, parts):
    work = []
    for k in range(half, 0, -1):
        for q in range(parts):
            for d in (0, 1):
                if goes(d, k, q, half, parts):
                    work.append((d, k, q))
    return work + [(None, 0, q) for q in range(parts)]


def goes(d, k, q, half, parts):
    return k < half or ((q < parts // 2) == (d == 0))


def widest(width, parts):
    return max(w for _, w in column_cuts(width, parts))


def reduce_scratch(rows, width, half, parts):
    return [
        pltpu.VMEM((2, half, rows, width), bf16),
        pltpu.VMEM((SLOTS, rows, widest(width, parts)), bf16),
        pltpu.VMEM((SLOTS, rows, widest(width, parts)), bf16),
        DMA((SLOTS,)),
        DMA((SLOTS,)),
        DMA((SLOTS,)),
        DMA((2, half, parts)),
    ]


def ring_reduce(place, own_at, other_at, other_wait, width, write, scratch, first=0):
    arrived, mine, theirs, mine_sem, theirs_sem, send_sem, recv_sem = scratch
    half = place.half
    parts = recv_sem.shape[2]
    cuts = column_cuts(width, parts)
    rows = arrived.shape[2]
    tile = 16
    work = ring_work(half, parts)

    def chip_of(d, k):
        return place.chip_at(k if d != 1 else -k)

    def loads(i):
        d, k, q = work[i]
        slot, chip, (start, size) = i % SLOTS, chip_of(d, k), cuts[q]
        return (
            pltpu.make_async_copy(
                own_at(chip).at[:, pl.ds(start, size)], mine.at[slot, :, pl.ds(0, size)], mine_sem.at[slot]
            ),
            pltpu.make_async_copy(
                other_at(chip).at[:, pl.ds(start, size)], theirs.at[slot, :, pl.ds(0, size)], theirs_sem.at[slot]
            ),
        )

    def send(i):
        d, k, q = work[i]
        start, size = cuts[q]
        return remote(
            mine.at[i % SLOTS, :, pl.ds(0, size)],
            arrived.at[d, k - 1, :, pl.ds(start, size)],
            send_sem.at[i % SLOTS],
            recv_sem.at[d, k - 1, q],
            place.right if d == 0 else place.left,
        )

    waited = set()
    fetched = [0]

    def fetch(last):
        while fetched[0] <= min(last, len(work) - 1):
            fetch_one(fetched[0])
            fetched[0] += 1

    def fetch_one(i):
        d, k, q = work[i]
        if i >= SLOTS:
            send(i - SLOTS).wait_send()
        key = (0 if k in (0, half) else d, k)
        if key not in waited:
            waited.add(key)
            other_wait(chip_of(d, k))
        for copy in loads(i):
            copy.start()

    ahead = SLOTS // 2
    for i, (d, k, q) in enumerate(work):
        fetch(i + ahead if i >= first else min(i + ahead, first - 1))
        for copy in loads(i):
            copy.wait()
        start, size = cuts[q]
        slot = i % SLOTS
        come = []
        for dd in (0, 1) if d is None else (d,):
            if k + 1 <= half and goes(dd, k + 1, q, half, parts):
                piece = arrived.at[dd, k, :, pl.ds(start, size)]
                remote(piece, piece, send_sem.at[slot], recv_sem.at[dd, k, q], place.sibling).wait_recv()
                come.append(dd)

        @pl.loop(0, rows // tile)
        def _(r):
            at = pl.ds(pl.multiple_of(r * tile, tile), tile)
            total = mine[slot, at, pl.ds(0, size)].astype(f32) + theirs[slot, at, pl.ds(0, size)].astype(f32)
            for dd in come:
                total += arrived[dd, k, at, pl.ds(start, size)].astype(f32)
            if d is None:
                write(at, pl.ds(start, size), total)
            else:
                mine[slot, at, pl.ds(0, size)] = total.astype(bf16)

        if d is not None:
            send(i).start()
        yield
    sends = len(work) - parts
    for i in range(max(0, len(work) - SLOTS), sends):
        send(i).wait_send()


DENSE_PARTS = 4


def swap_halves(values, lane):
    width = values.shape[1]
    return jnp.where(lane % HD < HD // 2, pltpu.roll(values, width - HD // 2, 1), pltpu.roll(values, HD // 2, 1))


def head_halves(block, lane, low):
    turned = pltpu.roll(block, HD, 1)
    lower, upper = (block, turned) if low == 0 else (turned, block)
    zero = jnp.zeros_like(block)
    return jnp.where(lane < HD, lower, zero).astype(bf16), jnp.where(lane < HD, zero, upper).astype(bf16)


def softmax_rows(q, k, causal):
    scores = jnp.where(causal, mul(q, k, 1, 1) * HD**-0.5, -1e30)
    e = jnp.exp(scores - jnp.max(scores, axis=1, keepdims=True))
    return e * (1.0 / jnp.sum(e, axis=1, keepdims=True))


def backward_entry(n, dp, count, *refs):
    direct, operands = refs[:5], refs[5 : 5 + count]
    results = refs[5 + count : 12 + count]
    held, operand_sem, scratch = refs[12 + count : 12 + 2 * count], refs[12 + 2 * count], refs[13 + 2 * count :]
    copies = [pltpu.make_async_copy(a, b, operand_sem.at[i]) for i, (a, b) in enumerate(zip(operands, held))]
    for copy in copies:
        copy.start()
    backward_kernel(n, dp, copies, *direct, *held, *results, *scratch)


def backward_kernel(
    n,
    dp,
    operand_copies,
    od_ref,
    sd_ref,
    wall_ref,
    ggu_ref,
    gd_ref,
    dmix_ref,
    dgate_ref,
    gates_ref,
    middle_ref,
    mixed_ref,
    dout_ref,
    tokens_ref,
    normed_t_ref,
    attended_t_ref,
    q_ref,
    k_ref,
    v_ref,
    cos_ref,
    sin_ref,
    gains_ref,
    output_ref,
    input_grad_ref,
    dense_ref,
    ggu_sum,
    gd_sum,
    ggu_in,
    gd_in,
    weights,
    extra_w,
    d_middle,
    d_middle_low,
    d_att,
    d_qkv,
    d_normed,
    extra,
    logits_low,
    own_f,
    stage_f,
    other_f,
    come_f,
    copies_f,
    weight_sem,
    stage_sem,
    other_sem,
    send_f,
    recv_f,
    copy_s,
    copy_r,
    expert_s,
    expert_r,
    tile_in,
    tile_out,
    *scratch_d,
):
    place = Place(n)
    half, ring = place.half, place.ring
    rank = lax.axis_index("dp")
    rows, width = middle_ref.shape
    q_width, kv_width = q_ref.shape[1], 2 * k_ref.shape[1]
    qkv_width = q_width + kv_width
    shard = own_f.shape[1]
    full_width = own_f.shape[2]
    barrier = pltpu.get_barrier_semaphore()
    for target in (place.right, place.left, place.sibling):
        pl.semaphore_signal(barrier, inc=1, device_id={"expert": target}, device_id_type=MESH)
    for turn in range(1, dp):
        pl.semaphore_signal(barrier, inc=1, device_id={"dp": lax.rem(rank + turn, dp)}, device_id_type=MESH)
    out_w = pltpu.make_async_copy(
        wall_ref.at[:, pl.ds(qkv_width + 128, width)], weights.at[:, pl.ds(0, width)], weight_sem.at[0]
    )
    extra_copy = pltpu.make_async_copy(wall_ref.at[:, pl.ds(qkv_width, 128)], extra_w, weight_sem.at[1])
    qkv_w = pltpu.make_async_copy(wall_ref.at[:, pl.ds(0, qkv_width)], weights, weight_sem.at[2])
    out_w.start()
    extra_copy.start()
    pl.semaphore_wait(barrier, 3 + dp - 1)

    hidden_width = ggu_ref.shape[1] // 2
    tiles = [(ggu_ref, ggu_in, r) for r in range(0, ggu_ref.shape[0], rows)]
    tiles += [(gd_ref, gd_in, r) for r in range(0, gd_ref.shape[0], rows)]

    def spread_tile(turn, t):
        own, come, r = tiles[t]
        return pltpu.make_async_remote_copy(
            src_ref=own.at[pl.ds(r, rows)],
            dst_ref=come.at[rank, pl.ds(r, rows)],
            send_sem=expert_s.at[turn, t],
            recv_sem=expert_r.at[turn, t],
            device_id={"dp": lax.rem(rank + turn, dp)},
            device_id_type=MESH,
        )

    for t in range(len(tiles)):
        for turn in range(1, dp):
            spread_tile(turn, t).start()

    def write_output(at, columns, total):
        output_ref[at, columns] = (middle_ref[at, columns] + total).astype(bf16)

    background = ring_reduce(
        place, lambda chip: od_ref.at[chip], lambda chip: sd_ref.at[chip], lambda chip: None, width, write_output, scratch_d
    )
    items = len(ring_work(half, scratch_d[6].shape[2]))
    done = [0]

    def pump(share):
        while done[0] < min(items, int(items * share + 0.5)):
            next(background)
            done[0] += 1

    pump(0.06)
    for copy in operand_copies:
        copy.wait()
    d_rows = jnp.concatenate([dgate_ref[:, 0, :], jnp.zeros((128 - n, rows), f32)], axis=0)
    d_gates = jnp.transpose(d_rows)
    gates = gates_ref[...]
    d_sel = gates * (d_gates - jnp.sum(gates * d_gates, axis=1, keepdims=True))
    logits_low[...] = d_sel.astype(bf16)
    extra_copy.wait()
    d_normed[...] = mul(logits_low[...], extra_w[...], 1, 1)
    gain_one, gain_two = gains_ref[0:1], gains_ref[1:2]
    tile = 32

    @pl.loop(0, rows // tile)
    def _(r):
        at = pl.ds(pl.multiple_of(r * tile, tile), tile)
        middle = middle_ref[at]
        d_mixed = dmix_ref[at] + d_normed[at]
        inv = lax.rsqrt(jnp.mean(middle * middle, axis=1, keepdims=True) + EPSILON)
        scaled = d_mixed * gain_two
        back = jnp.mean(scaled * middle, axis=1, keepdims=True)
        total = dout_ref[at].astype(f32) + inv * scaled - middle * (inv * inv * inv * back)
        d_middle[at] = total
        d_middle_low[at] = total.astype(bf16)
        d_att[at] = (d_mixed * middle * inv).astype(bf16)

    lane = lax.broadcasted_iota(jnp.int32, (rows, 128), 1)
    extra[...] = mul(mixed_ref[...], logits_low[...], 0, 0) + mul(
        d_att[...], (lane == n + 1).astype(bf16), 0, 0
    )
    pump(0.12)
    out_w.wait()
    d_att[...] = mul(d_middle_low[...], weights[:, pl.ds(0, width)], 1, 1).astype(bf16)
    qkv_w.start()
    pump(0.18)

    t_at = lax.broadcasted_iota(jnp.int32, (rows, rows), 0)
    u_at = lax.broadcasted_iota(jnp.int32, (rows, rows), 1)
    causal = t_at >= u_at
    cosine, sine = cos_ref[...], sin_ref[...]
    sine_back = jnp.where(lane % HD < HD // 2, sine, -sine)
    kv_count = k_ref.shape[1] // HD
    per_group = q_width // HD // kv_count
    d_normed[...] = jnp.zeros_like(d_normed)
    pair_k, pair_v = None, None
    for g in range(kv_count):
        pair = pl.ds(128 * (g // 2), 128)
        k_parts = head_halves(k_ref[:, pair].astype(f32), lane, g % 2)
        v_parts = head_halves(v_ref[:, pair].astype(f32), lane, g % 2)
        d_k, d_v = [None, None], [None, None]
        for h in range(per_group * g, per_group * (g + 1)):
            at = pl.ds(128 * (h // 2), 128)
            low = h % 2
            query, d_a = q_ref[:, at], d_att[:, at]
            probs = softmax_rows(query, k_parts[low], causal)
            probs_low = probs.astype(bf16)
            d_probs = mul(d_a, v_parts[low], 1, 1)
            weighted = probs * d_probs
            d_scores = (weighted - probs * jnp.sum(weighted, axis=1, keepdims=True)).astype(bf16)
            d_normed[:, at] += mul(d_scores, k_parts[low], 1, 0)
            step_k, step_v = mul(d_scores, query, 0, 0), mul(probs_low, d_a, 0, 0)
            d_k[low] = step_k if d_k[low] is None else d_k[low] + step_k
            d_v[low] = step_v if d_v[low] is None else d_v[low] + step_v

        def gathered(parts):
            stay, turn = parts[g % 2], parts[1 - g % 2]
            return stay if turn is None else (pltpu.roll(turn, HD, 1) if stay is None else stay + pltpu.roll(turn, HD, 1))

        if g % 2 == 0:
            pair_k, pair_v = gathered(d_k), gathered(d_v)
        if g % 2 == 1 or g + 1 == kv_count:
            total_k = jnp.where(lane < HD, pair_k, gathered(d_k)) * HD**-0.5
            total_v = jnp.where(lane < HD, pair_v, gathered(d_v))
            turned = total_k * cosine + swap_halves(total_k, lane) * sine_back
            d_qkv[:, pl.ds(q_width + 128 * (g // 2), 128)] = turned.astype(bf16)
            d_qkv[:, pl.ds(q_width + kv_width // 2 + 128 * (g // 2), 128)] = total_v.astype(bf16)
        pump(0.18 + 0.3 * (g + 1) / kv_count)
    for b in range(q_width // 128):
        at = pl.ds(128 * b, 128)
        total = d_normed[:, at] * HD**-0.5
        d_qkv[:, at] = (total * cosine + swap_halves(total, lane) * sine_back).astype(bf16)
    pump(0.53)
    qkv_w.wait()
    d_normed[...] = mul(d_qkv[...], weights[...], 1, 1)

    @pl.loop(0, rows // tile)
    def _(r):
        at = pl.ds(pl.multiple_of(r * tile, tile), tile)
        inputs = tokens_ref[at].astype(f32)
        d = d_normed[at]
        inv = lax.rsqrt(jnp.mean(inputs * inputs, axis=1, keepdims=True) + EPSILON)
        scaled = d * gain_one
        back = jnp.mean(scaled * inputs, axis=1, keepdims=True)
        total = d_middle[at] + inv * scaled - inputs * (inv * inv * inv * back)
        input_grad_ref[at] = total.astype(bf16)
        d_att[at] = (d * inputs * inv).astype(bf16)

    extra[...] += mul(d_att[...], (lane == n).astype(bf16), 0, 0)
    pump(0.66)

    def cross(chip, slot):
        return remote(stage_f.at[slot], other_f.at[chip], stage_sem.at[slot], other_sem.at[chip], place.sibling)

    def fill(ref, device):
        at = pl.ds(pl.multiple_of(device * shard, 16), shard)
        ref[:, pl.ds(0, qkv_width)] = mul(normed_t_ref[at], d_qkv[...], 1, 0).astype(bf16)
        ref[:, pl.ds(qkv_width, 128)] = extra[at].astype(bf16)
        ref[:, pl.ds(qkv_width + 128, width)] = mul(attended_t_ref[at], d_middle_low[...], 1, 0).astype(bf16)

    for k in range(half, -1, -1):
        @pl.loop(max(0, 2 * (half - k) - 1), min(ring, 2 * (half - k) + 1))
        def _(i):
            away = half - lax.div(i + 1, 2)
            chip = place.chip_at(jnp.where(lax.rem(i, 2) == 0, away, -away))
            slot = lax.rem(i, 2)

            @pl.when(i >= 2)
            def _():
                cross(chip, slot).wait_send()

            fill(stage_f.at[slot], chip * 2 + 1 - place.core)
            cross(chip, slot).start()
            fill(own_f.at[chip], chip * 2 + place.core)

        pump(1.0 - 0.34 * k / (half + 1))

    for _ in background:
        pass
    for slot in range(2):
        cross(place.chip, slot).wait_send()
    cuts = column_cuts(full_width, DENSE_PARTS)
    work = ring_work(half, DENSE_PARTS)

    def send(d, k, q):
        chip = place.chip_at(k if d == 0 else -k)
        at = pl.ds(*cuts[q])
        return remote(
            own_f.at[chip, :, at],
            come_f.at[d, k - 1, :, at],
            send_f.at[d, k - 1, q],
            recv_f.at[d, k - 1, q],
            place.right if d == 0 else place.left,
        )

    def spread(turn, q):
        at = pl.ds(*cuts[q])
        return pltpu.make_async_remote_copy(
            src_ref=copies_f.at[rank, :, at],
            dst_ref=copies_f.at[rank, :, at],
            send_sem=copy_s.at[turn, q],
            recv_sem=copy_r.at[turn, q],
            device_id={"dp": lax.rem(rank + turn, dp)},
            device_id_type=MESH,
        )

    lanes = 2 if 2 * dp <= weights.shape[0] // rows else 1

    def tile_loads(t):
        own, come, r = tiles[t]
        size = own.shape[1]
        for source in range(dp):
            band = weights.at[pl.ds(((t % lanes) * dp + source) * rows, rows), pl.ds(0, size)]

            @pl.when(rank == source)
            def _():
                pltpu.make_async_copy(own.at[pl.ds(r, rows)], band, tile_in.at[t % lanes, source]).start()

            @pl.when(rank != source)
            def _():
                pltpu.make_async_copy(come.at[source, pl.ds(r, rows)], band, tile_in.at[t % lanes, source]).start()

    def tile_put(t):
        own, _, r = tiles[t]
        held = (d_att, d_middle_low)[t % 2].at[:, pl.ds(0, own.shape[1])]
        to = gd_sum if own is gd_ref else ggu_sum
        return pltpu.make_async_copy(held, to.at[pl.ds(r, rows)], tile_out.at[t % 2])

    def tile_here(t):
        for turn in range(1, dp):
            spread_tile(turn, t).wait_recv()
        tile_loads(t)

    def tile_sum(t):
        own, _, r = tiles[t]
        size = own.shape[1]
        held = (d_att, d_middle_low)[t % 2]
        for source in range(dp):
            band = weights.at[pl.ds(((t % lanes) * dp + source) * rows, rows), pl.ds(0, size)]
            pltpu.make_async_copy(band, band, tile_in.at[t % lanes, source]).wait()
        if t >= 2:
            tile_put(t - 2).wait()

        @pl.loop(0, rows // tile)
        def _(i):
            total = None
            for source in range(dp):
                at = pl.ds(pl.multiple_of(((t % lanes) * dp + source) * rows + i * tile, tile), tile)
                value = weights[at, pl.ds(0, size)].astype(f32)
                total = value if total is None else total + value
            held[pl.ds(pl.multiple_of(i * tile, tile), tile), pl.ds(0, size)] = total.astype(bf16)

        tile_put(t).start()

    def tile_step(t):
        if lanes == 2 and t < len(tiles):
            tile_here(t)
        if t >= 1:
            tile_sum(t - 1)
        if lanes == 1 and t < len(tiles):
            tile_here(t)

    moves = len(work) - DENSE_PARTS
    when = {moves * (t + 2) // (len(tiles) + 2): t for t in range(len(tiles) + 1)}
    met = set()
    for index, (d, k, q) in enumerate(work):
        if index in when:
            tile_step(when[index])
        chip = place.chip_at(0 if d is None else (k if d == 0 else -k))
        key = (0 if k in (0, half) else d, k)
        if key not in met:
            met.add(key)
            remote(other_f.at[chip], other_f.at[chip], stage_sem.at[0], other_sem.at[chip], place.sibling).wait_recv()
        at = pl.ds(*cuts[q])
        total = own_f[chip, :, at].astype(f32) + other_f[chip, :, at].astype(f32)
        for dd in (0, 1) if d is None else (d,):
            if k + 1 <= half and goes(dd, k + 1, q, half, DENSE_PARTS):
                piece = come_f.at[dd, k, :, at]
                remote(piece, piece, send_f.at[dd, k, q], recv_f.at[dd, k, q], place.sibling).wait_recv()
                total += piece[...].astype(f32)
        if d is not None:
            own_f[chip, :, at] = total.astype(bf16)
            send(d, k, q).start()
        else:
            copies_f[rank, :, at] = total.astype(bf16)
            for turn in range(1, dp):
                spread(turn, q).start()
    for t in range(len(tiles) - 2, len(tiles)):
        tile_put(t).wait()
    for q in range(DENSE_PARTS):
        for turn in range(1, dp):
            spread(turn, q).wait()
    total = copies_f[0].astype(f32)
    for r in range(1, dp):
        total += copies_f[r].astype(f32)
    dense_ref[...] = total.astype(bf16)
    for t in range(len(tiles)):
        for turn in range(1, dp):
            spread_tile(turn, t).wait_send()
    for d, k, q in work:
        if d is not None:
            send(d, k, q).wait_send()


def backward(n, dp, own_d, other_d, wall, grad_gu, grad_down, others, collective_id):
    half, ring = n // 4, n // 2
    rows, width = own_d.shape[1:]
    full_width = wall.shape[1]
    qkv_width = full_width - width - 128
    shard = wall.shape[0] // n
    q_width = others[9].shape[1]
    return pl.pallas_call(
        functools.partial(backward_entry, n, dp, len(others)),
        out_shape=[
            jax.ShapeDtypeStruct((rows, width), bf16),
            jax.ShapeDtypeStruct((rows, width), bf16),
            jax.ShapeDtypeStruct((shard, full_width), bf16),
            jax.ShapeDtypeStruct(grad_gu.shape, bf16),
            jax.ShapeDtypeStruct(grad_down.shape, bf16),
            jax.ShapeDtypeStruct((dp,) + grad_gu.shape, bf16),
            jax.ShapeDtypeStruct((dp,) + grad_down.shape, bf16),
        ],
        in_specs=[ANY] * (5 + len(others)),
        out_specs=[VMEM] * 3 + [ANY] * 4,
        scratch_shapes=[pltpu.VMEM(value.shape, value.dtype) for value in others]
        + [DMA((len(others),))]
        + [
            pltpu.VMEM((width, qkv_width), bf16),
            pltpu.VMEM((width, 128), bf16),
            pltpu.VMEM((rows, width), f32),
            pltpu.VMEM((rows, width), bf16),
            pltpu.VMEM((rows, q_width), bf16),
            pltpu.VMEM((rows, qkv_width), bf16),
            pltpu.VMEM((rows, width), f32),
            pltpu.VMEM((width, 128), f32),
            pltpu.VMEM((rows, 128), bf16),
            pltpu.VMEM((ring, shard, full_width), bf16),
            pltpu.VMEM((2, shard, full_width), bf16),
            pltpu.VMEM((ring, shard, full_width), bf16),
            pltpu.VMEM((2, half, shard, full_width), bf16),
            pltpu.VMEM((dp, shard, full_width), bf16),
            DMA((3,)),
            DMA((2,)),
            DMA((ring,)),
            DMA((2, half, DENSE_PARTS)),
            DMA((2, half, DENSE_PARTS)),
            DMA((dp, DENSE_PARTS)),
            DMA((dp, DENSE_PARTS)),
            DMA((dp, (width + grad_down.shape[0]) // rows)),
            DMA((dp, (width + grad_down.shape[0]) // rows)),
            DMA((2, dp)),
            DMA((2,)),
        ]
        + reduce_scratch(rows, width, half, 2),
        compiler_params=pltpu.CompilerParams(
            collective_id=collective_id, has_side_effects=True, vmem_limit_bytes=63 * MB
        ),
    )(own_d, other_d, wall, grad_gu, grad_down, *others)[:5]


def finish_kernel(
    experts_n, output_in, grad_in, dense_in, gu_in, down_in, output, grad, q, kv, out, router, one, two, gate, up, down
):
    output[...] = output_in[...]
    grad[...] = grad_in[...]
    hidden_width = gate.shape[1]
    gate[...] = gu_in[:, pl.ds(0, hidden_width)].astype(f32)
    up[...] = gu_in[:, pl.ds(hidden_width, hidden_width)].astype(f32)
    down[...] = down_in[...].astype(f32)

    @pl.when(pl.program_id(0) == 0)
    def _():
        start = 0
        for ref in (q, kv):
            ref[...] = dense_in[:, pl.ds(start, ref.shape[1])].astype(f32)
            start += ref.shape[1]
        extra = dense_in[:, pl.ds(start, 128)].astype(f32)
        router[...] = extra[:, :experts_n]
        turned = jnp.transpose(extra)
        one[...] = turned[experts_n : experts_n + 1]
        two[...] = turned[experts_n + 1 : experts_n + 2]
        out[...] = dense_in[:, pl.ds(start + 128, out.shape[1])].astype(f32)


def finish(output, grad, dense, gu, down, experts_n, q_width, kv_width):
    steps = 4
    rows, width = output.shape
    shard = dense.shape[0]
    hidden_width = gu.shape[1] // 2

    def tiles(a, b):
        return pl.BlockSpec((a // steps, b), lambda i: (i, 0))

    def whole(a, b):
        return pl.BlockSpec((a, b), lambda i: (0, 0))

    shape = jax.ShapeDtypeStruct
    return pl.pallas_call(
        functools.partial(finish_kernel, experts_n),
        grid=(steps,),
        in_specs=[
            tiles(rows, width),
            tiles(rows, width),
            whole(*dense.shape),
            tiles(*gu.shape),
            tiles(*down.shape),
        ],
        out_specs=[
            tiles(rows, width),
            tiles(rows, width),
            whole(shard, q_width),
            whole(shard, kv_width),
            whole(shard, width),
            whole(shard, experts_n),
            whole(1, shard),
            whole(1, shard),
            tiles(gu.shape[0], hidden_width),
            tiles(gu.shape[0], hidden_width),
            tiles(*down.shape),
        ],
        out_shape=[
            shape((rows, width), bf16),
            shape((rows, width), bf16),
            shape((shard, q_width), f32),
            shape((shard, kv_width), f32),
            shape((shard, width), f32),
            shape((shard, experts_n), f32),
            shape((1, shard), f32),
            shape((1, shard), f32),
            shape((gu.shape[0], hidden_width), f32),
            shape((gu.shape[0], hidden_width), f32),
            shape(down.shape, f32),
        ],
        compiler_params=pltpu.CompilerParams(vmem_limit_bytes=63 * MB),
    )(output, grad, dense, gu, down)


QUARTERS = 4


def expert_kernel(
    n,
    x_ref,
    dog_ref,
    gates_ref,
    gate_any,
    up_any,
    wd_any,
    de_ref,
    dgates_ref,
    ggu_out,
    gd_out,
    od_ref,
    sd_ref,
    oe_ref,
    se_ref,
    xg_ref,
    hg_ref,
    wgu_ref,
    wd_ref,
    ggu_ref,
    gd_ref,
    acc_gu,
    acc_d,
    gate_in,
    dgate_out,
    xbuf,
    dobuf,
    pd,
    pe,
    hbuf,
    own_sem,
    weight_sem,
    ring_s,
    ring_r,
    cross_s,
    cross_r,
    load_sem,
    put_sem,
    sib_r,
    gate_s,
    gate_r,
    dgate_s,
    dgate_r,
    *reduce_refs,
):
    place = Place(n)
    half, ring, me = place.half, place.ring, place.me
    rows, width = x_ref.shape
    hidden_width = wd_ref.shape[0]
    piece = rows // QUARTERS
    weight_copies = [
        pltpu.make_async_copy(gate_any, wgu_ref.at[:, pl.ds(0, hidden_width)], weight_sem.at[0]),
        pltpu.make_async_copy(up_any, wgu_ref.at[:, pl.ds(hidden_width, hidden_width)], weight_sem.at[1]),
        pltpu.make_async_copy(wd_any, wd_ref, weight_sem.at[2]),
    ]
    for copy in weight_copies:
        copy.start()
    pltpu.make_async_copy(x_ref, xbuf.at[0], load_sem.at[0, 0]).start()
    pltpu.make_async_copy(dog_ref.at[me], dobuf.at[0], load_sem.at[1, 0]).start()
    meet_all(place)

    own = pltpu.make_async_copy(xbuf.at[0], xg_ref.at[me], own_sem.at[0])

    def at(q):
        return pl.ds(pl.multiple_of(q * piece, piece), piece)

    def block_of(d, k):
        return jnp.where(d == 0, place.device(-k), place.device(k))

    def along(d, k, q, first=False):
        b = me if first else block_of(d, k - 1)
        return remote(
            x_ref.at[at(q)] if first else xg_ref.at[b, at(q)],
            xg_ref.at[b, at(q)],
            ring_s.at[d, k - 1, q],
            ring_r.at[d, k - 1, q],
            jnp.where(d == 0, place.right, place.left),
        )

    def across(d, k, q, first=False):
        b = me if first else block_of(d, k)
        src = x_ref.at[at(q)] if first else xg_ref.at[b, at(q)]
        return remote(src, xg_ref.at[b, at(q)], cross_s.at[d, k, q], cross_r.at[d, k, q], place.sibling)

    def gate_copy(d):
        to = lax.rem(me + d, n)
        return remote(gates_ref.at[to], gate_in.at[me], gate_s.at[d], gate_r.at[d], to)

    for q in range(QUARTERS):
        for d in (0, 1):
            along(d, 1, q, first=True).start()
        across(0, 0, q, first=True).start()

    @pl.loop(1, n)
    def _(d):
        gate_copy(d).start()

    gate_in[me] = gates_ref[me]
    acc_gu[...] = jnp.zeros_like(acc_gu)
    acc_d[...] = jnp.zeros_like(acc_d)

    def step_of(i):
        late = jnp.where(i < n - 4, i, jnp.where(i < n - 2, i + 2, i - 2))
        k = jnp.where(late < 2, 0, lax.div(late + 2, 4))
        j = jnp.where(late < 2, late, lax.rem(late + 2, 4))
        edge = jnp.logical_or(k == 0, k == half)
        d = jnp.where(edge, 0, lax.rem(j, 2))
        other = jnp.where(edge, j, lax.div(j, 2))
        chip = jnp.where(d == 0, place.chip_at(-k), place.chip_at(k))
        core = jnp.where(other == 0, place.core, 1 - place.core)
        return k, j, d, other, chip, chip * 2 + core

    def pump(d, k, q, last=False):
        along(d, k, q).wait_recv()
        if not last:
            near = jnp.where(q < QUARTERS // 2, 0, 1) == d

            @pl.when(jnp.logical_or(k + 1 < half, near))
            def _():
                along(d, k + 1, q).start()

        across(d, k, q).start()

    def load(block, slot):
        return (
            pltpu.make_async_copy(xg_ref.at[block], xbuf.at[slot], load_sem.at[0, slot]),
            pltpu.make_async_copy(dog_ref.at[block], dobuf.at[slot], load_sem.at[1, slot]),
        )

    def put_wait(slot):
        for which, buf in enumerate((pd, pe, hbuf)):
            pltpu.make_async_copy(buf.at[slot], buf.at[slot], put_sem.at[which, slot]).wait()

    def dgate_copy(block):
        d = lax.rem(block - me + n, n)
        return remote(dgate_out.at[block], dgates_ref.at[me], dgate_s.at[d], dgate_r.at[d], block)

    def load_rest(block, slot):
        return (
            pltpu.make_async_copy(xg_ref.at[block], xbuf.at[slot], load_sem.at[0, slot]),
            pltpu.make_async_copy(dog_ref.at[block], dobuf.at[slot], load_sem.at[1, slot]),
            pltpu.make_async_copy(hg_ref.at[block], hbuf.at[slot], load_sem.at[2, slot]),
        )

    for copy in weight_copies:
        copy.wait()

    def work_on(i):
        k, j, d, other, chip, block = step_of(i)
        slot = lax.rem(i, 2)
        for copy in load(block, slot):
            copy.wait()

        @pl.when(i == 0)
        def _():
            own.start()

        @pl.when(i > 0)
        def _():
            away = lax.rem(me - block + n, n)
            remote(gate_in.at[block], gate_in.at[block], gate_s.at[away], gate_r.at[away], place.sibling).wait_recv()

        @pl.when(jnp.logical_and(i >= 2, i < n - 2))
        def _():
            put_wait(slot)

        gate = jnp.transpose(gate_in[block])[:, :1]
        gu = mul(xbuf[slot], wgu_ref[...], 1, 0)
        dh = mul(dobuf[slot], wd_ref[...], 1, 1)
        g, u = gu[:, :hidden_width], gu[:, hidden_width:]
        s = 1.0 / (1.0 + jnp.exp(-g))
        gs = g * s
        hid = gs * u
        dgate = jnp.sum(dh * hid, axis=1, keepdims=True)
        dgate_out[block] = jnp.transpose(jnp.broadcast_to(dgate, (rows, 128)))[:8]
        dh = dh * gate
        hbuf[slot, :, pl.ds(0, hidden_width)] = (dh * u * s * (1.0 + g * (1.0 - s))).astype(bf16)
        hbuf[slot, :, pl.ds(hidden_width, hidden_width)] = (dh * gs).astype(bf16)
        hbuf[slot, :, pl.ds(2 * hidden_width, hidden_width)] = (hid * gate).astype(bf16)
        pltpu.make_async_copy(hbuf.at[slot], hg_ref.at[block], put_sem.at[2, slot]).start()

        @pl.when(i < 2)
        def _():
            for t in range(2):
                for dd in (0, 1):
                    pump(dd, 1, i * 2 + t)

        @pl.when(jnp.logical_and(i >= 2, k + 1 < half))
        def _():
            for dd in (0, 1):
                pump(dd, k + 1, j)

        @pl.when(jnp.logical_and(k + 1 == half, j < 2))
        def _():
            for dd in (0, 1):
                pump(dd, half, j + dd * (QUARTERS // 2), last=True)

        nk, nj, nd, nother, nchip, nblock = step_of(i + 1)

        @pl.when(jnp.logical_and(i + 1 < n, nother == 1))
        def _():
            for q in range(QUARTERS):
                dd = jnp.where(nk == half, 0 if q < QUARTERS // 2 else 1, nd)
                b = nblock
                remote(
                    xg_ref.at[b, at(q)], xg_ref.at[b, at(q)], cross_s.at[dd, nk, q], cross_r.at[dd, nk, q], place.sibling
                ).wait_recv()

        @pl.when(i == 0)
        def _():
            own.wait()

        @pl.when(i + 1 < n)
        def _():
            for copy in load(nblock, 1 - slot):
                copy.start()

        pd[slot] = mul(hbuf[slot, :, pl.ds(2 * hidden_width, hidden_width)], wd_ref[...], 1, 0).astype(bf16)
        pe[slot] = mul(hbuf[slot, :, pl.ds(0, 2 * hidden_width)], wgu_ref[...], 1, 1).astype(bf16)

        @pl.when(i > 0)
        def _():
            dgate_copy(block).start()

        @pl.when(i == 0)
        def _():
            dgates_ref[me] = dgate_out[me]

        @pl.when(other == 0)
        def _():
            pltpu.make_async_copy(pd.at[slot], od_ref.at[chip], put_sem.at[0, slot]).start()
            pltpu.make_async_copy(pe.at[slot], oe_ref.at[chip], put_sem.at[1, slot]).start()

        @pl.when(other == 1)
        def _():
            remote(pd.at[slot], sd_ref.at[chip], put_sem.at[0, slot], sib_r.at[0, chip], place.sibling).start()
            remote(pe.at[slot], se_ref.at[chip], put_sem.at[1, slot], sib_r.at[1, chip], place.sibling).start()

    @pl.loop(0, n - 2)
    def _(i):
        work_on(i)

    put_wait(0)
    put_wait(1)

    def other_wait(chip):
        remote(se_ref.at[chip], se_ref.at[chip], put_sem.at[1, 0], sib_r.at[1, chip], place.sibling).wait_recv()

    def write(at, columns, total):
        de_ref[at, columns] = total

    back = ring_reduce(
        place, lambda chip: oe_ref.at[chip], lambda chip: se_ref.at[chip], other_wait, width, write, reduce_refs, 2
    )
    next(back)
    next(back)

    @pl.loop(n - 2, n)
    def _(i):
        work_on(i)

    put_wait(0)
    put_wait(1)

    for copy in load_rest(0, 0):
        copy.start()

    def gradients(first, last):
        @pl.loop(first, last)
        def _(b):
            slot = lax.rem(b, 2)
            for copy in load_rest(b, slot):
                copy.wait()

            @pl.when(b + 1 < n)
            def _():
                for copy in load_rest(b + 1, 1 - slot):
                    copy.start()

            acc_gu[...] += mul(xbuf[slot], hbuf[slot, :, pl.ds(0, 2 * hidden_width)], 0, 0)
            acc_d[...] += mul(hbuf[slot, :, pl.ds(2 * hidden_width, hidden_width)], dobuf[slot], 0, 0)

    steps = len(ring_work(half, 2)) // 2 - 2
    for step in range(steps):
        next(back)
        next(back)
        gradients(n * step // steps, n * (step + 1) // steps)
    ggu_ref[...] = acc_gu[...].astype(bf16)
    gd_ref[...] = acc_d[...].astype(bf16)
    out_copies = [
        pltpu.make_async_copy(ggu_ref, ggu_out, weight_sem.at[0]),
        pltpu.make_async_copy(gd_ref, gd_out, weight_sem.at[1]),
    ]
    for copy in out_copies:
        copy.start()
    for _ in back:
        pass
    for copy in out_copies:
        copy.wait()

    @pl.loop(0, ring)
    def _(chip):
        remote(sd_ref.at[chip], sd_ref.at[chip], put_sem.at[0, 0], sib_r.at[0, chip], place.sibling).wait_recv()

    @pl.loop(1, n)
    def _(d):
        gate_copy(d).wait_send()
        source = lax.rem(me - d + n, n)
        remote(dgates_ref.at[source], dgates_ref.at[source], dgate_s.at[d], dgate_r.at[d], place.sibling).wait()

    for q in range(QUARTERS):
        across(0, 0, q, first=True).wait_send()
        for d in (0, 1):
            for k in range(1, half + 1):
                if k < half or ((q < QUARTERS // 2) == (d == 0)):
                    along(d, k, q).wait_send()
                    across(d, k, q).wait_send()


def experts(n, mixed_in, d_gathered, gate_rows, gate_w, up_w, wd, collective_id):
    half, ring = n // 4, n // 2
    rows, width = mixed_in.shape
    blocks = jax.ShapeDtypeStruct((ring, rows, width), bf16)
    hidden_width = wd.shape[0]
    both = (width, 2 * hidden_width)
    out = pl.pallas_call(
        functools.partial(expert_kernel, n),
        out_shape=[
            jax.ShapeDtypeStruct((rows, width), f32),
            jax.ShapeDtypeStruct((n, 8, rows), f32),
            jax.ShapeDtypeStruct(both, bf16),
            jax.ShapeDtypeStruct(wd.shape, bf16),
            blocks,
            blocks,
            blocks,
            blocks,
            jax.ShapeDtypeStruct((n, rows, width), bf16),
            jax.ShapeDtypeStruct((n, rows, 3 * hidden_width), bf16),
        ],
        in_specs=[ANY, ANY, VMEM, ANY, ANY, ANY],
        out_specs=[VMEM, VMEM] + [ANY] * 8,
        scratch_shapes=[
            pltpu.VMEM(both, bf16),
            pltpu.VMEM(wd.shape, bf16),
            pltpu.VMEM(both, bf16),
            pltpu.VMEM(wd.shape, bf16),
            pltpu.VMEM(both, f32),
            pltpu.VMEM(wd.shape, f32),
            pltpu.VMEM((n, 8, rows), f32),
            pltpu.VMEM((n, 8, rows), f32),
            pltpu.VMEM((2, rows, width), bf16),
            pltpu.VMEM((2, rows, width), bf16),
            pltpu.VMEM((2, rows, width), bf16),
            pltpu.VMEM((2, rows, width), bf16),
            pltpu.VMEM((2, rows, 3 * hidden_width), bf16),
            DMA((1,)),
            DMA((3,)),
            DMA((2, half, QUARTERS)),
            DMA((2, half, QUARTERS)),
            DMA((2, half + 1, QUARTERS)),
            DMA((2, half + 1, QUARTERS)),
            DMA((3, 2)),
            DMA((3, 2)),
            DMA((2, ring)),
            DMA((n,)),
            DMA((n,)),
            DMA((n,)),
            DMA((n,)),
        ]
        + reduce_scratch(rows, width, half, 2),
        compiler_params=pltpu.CompilerParams(
            collective_id=collective_id, has_side_effects=True, vmem_limit_bytes=62 * MB
        ),
    )(mixed_in, d_gathered, gate_rows, gate_w, up_w, wd)
    return out[:6]


def rope_tables(length):
    inverse = np.float32(10000.0) ** (-np.arange(HD // 2, dtype=np.float32) / np.float32(HD // 2))
    angles = np.arange(length, dtype=np.float32)[:, None] * inverse.astype(np.float32)[None, :]
    return [np.tile(table(angles).astype(np.float32), (1, 4)) for table in (np.cos, np.sin)]


def per_device(
    n,
    dp,
    tokens,
    cotangent,
    lengths,
    routes,
    norm1_gain,
    w_query,
    w_kv,
    w_out,
    norm2_gain,
    w_router,
    expert_gate,
    expert_up,
    expert_down,
):
    tok_rows, model_width = tokens.shape
    expert_count = w_router.shape[1]
    kv_width, q_width = w_kv.shape[1], w_query.shape[1]
    shard = w_query.shape[0]
    extra = jnp.concatenate(
        [
            w_router,
            norm1_gain[:, None],
            norm2_gain[:, None],
            jnp.zeros((shard, 128 - expert_count - 2), bf16),
        ],
        axis=1,
    )
    turns = rope_tables(tok_rows)
    (
        wall,
        d_gathered,
        d_out_low,
        queries,
        keys,
        values,
        normed_t,
        attended_t,
        middle,
        mixed_in,
        gates,
        gate_rows,
        gains,
    ) = forward(n, dp, w_query, w_kv, extra, w_out, lengths, cotangent, tokens, routes, turns, 0)
    wall = wall.reshape(-1, wall.shape[-1])
    d_mixed_experts, d_gate_rows, grad_gu, grad_down, own_d, other_d = experts(
        n, mixed_in, d_gathered, gate_rows, expert_gate[0], expert_up[0], expert_down[0], 1
    )

    sums = backward(
        n,
        dp,
        own_d,
        other_d,
        wall,
        grad_gu,
        grad_down,
        (
            d_mixed_experts,
            d_gate_rows,
            gates,
            middle,
            mixed_in,
            d_out_low,
            tokens,
            normed_t,
            attended_t,
            queries,
            keys,
            values,
            *turns,
            gains,
        ),
        2,
    )
    output, input_grad, grad_q, grad_kv, grad_out, router, gain_one, gain_two, gate, up, down = finish(
        *sums, expert_count, q_width, kv_width
    )
    return (
        output,
        input_grad,
        gain_one.reshape(-1),
        grad_q,
        grad_kv,
        grad_out,
        gain_two.reshape(-1),
        router,
        gate[None],
        up[None],
        down[None],
    )


def solution(mesh):
    rows, own = P(("dp", "expert"), None), P("expert", None)
    expert = P("expert", None, None)
    return jax.shard_map(
        functools.partial(per_device, mesh.shape["expert"], mesh.shape["dp"]),
        mesh=mesh,
        in_specs=(rows, rows, P(("dp", "expert")), rows, P("expert"), own, own, own, P("expert"), own)
        + (expert,) * 3,
        out_specs=(rows, rows, P("expert"), own, own, own, P("expert"), own) + (expert,) * 3,
        check_vma=False,
    )
```

```python
import functools

import jax
import jax.numpy as jnp
import numpy as np
from jax import lax
from jax.experimental import pallas as pl
from jax.experimental.pallas import tpu as pltpu
from jax.sharding import PartitionSpec as P

HD = 64
EPSILON = 1e-05
MESH = pl.DeviceIdType.MESH
ANY = pl.BlockSpec(memory_space=pl.ANY)
VMEM = pl.BlockSpec(memory_space=pltpu.VMEM)
DMA = pltpu.SemaphoreType.DMA
MB = 2**20
f32 = jnp.float32
bf16 = jnp.bfloat16


def mul(a, b, ca, cb):
    return lax.dot_general(a, b, (((ca,), (cb,)), ((), ())), preferred_element_type=f32)


class Place:
    def __init__(self, n):
        self.n, self.mid, self.ring = n, n // 8, n // 2
        self.half = self.ring // 2
        self.me = lax.axis_index("expert")
        self.chip, self.core = lax.div(self.me, 2), lax.rem(self.me, 2)
        outer, inner = lax.div(self.chip, self.mid), lax.rem(self.chip, self.mid)
        row = 3 - outer
        step = jnp.where(lax.rem(row, 2) == 0, inner - 1, self.mid - 1 - inner)
        self.at = jnp.where(inner == 0, outer, 4 + row * (self.mid - 1) + step)
        self.sibling = self.chip * 2 + 1 - self.core
        self.right, self.left = self.device(1), self.device(-1)

    def chip_at(self, distance):
        p = lax.rem(self.at + distance + self.ring, self.ring)
        wide = max(self.mid - 1, 1)
        row, k = lax.div(lax.max(p - 4, 0), wide), lax.rem(lax.max(p - 4, 0), wide)
        inner = jnp.where(lax.rem(row, 2) == 0, 1 + k, self.mid - 1 - k)
        return jnp.where(p < 4, p * self.mid, (3 - row) * self.mid + inner)

    def device(self, distance):
        return self.chip_at(distance) * 2 + self.core


def remote(src, dst, send, recv, device):
    return pltpu.make_async_remote_copy(
        src_ref=src, dst_ref=dst, send_sem=send, recv_sem=recv, device_id={"expert": device}, device_id_type=MESH
    )


def meet(targets):
    barrier = pltpu.get_barrier_semaphore()
    for target in targets:
        pl.semaphore_signal(barrier, inc=1, device_id={"expert": target}, device_id_type=MESH)
    pl.semaphore_wait(barrier, len(targets))


def meet_all(place):
    barrier = pltpu.get_barrier_semaphore()

    @pl.loop(1, place.n)
    def _(d):
        other = lax.rem(place.me + d, place.n)
        pl.semaphore_signal(barrier, inc=1, device_id={"expert": other}, device_id_type=MESH)

    pl.semaphore_wait(barrier, place.n - 1)


def column_cuts(width, parts):
    tiles = width // 128
    edges = [128 * (tiles * i // parts) for i in range(parts + 1)]
    return [(edges[i], edges[i + 1] - edges[i]) for i in range(parts)]


PARTS = 2


def forward_entry(n, dp, count, *refs):
    direct, results = refs[:12], refs[12 : 12 + count]
    held, result_sem, scratch = refs[12 + count : 12 + 2 * count], refs[12 + 2 * count], refs[13 + 2 * count :]
    copies = [pltpu.make_async_copy(a, b, result_sem.at[i]) for i, (a, b) in enumerate(zip(held, results))]
    forward_kernel(n, dp, copies, *direct, *held, *scratch)


def forward_kernel(
    n,
    dp,
    result_copies,
    w_query_ref,
    w_kv_ref,
    w_extra_ref,
    w_out_ref,
    lengths_ref,
    cotangent_ref,
    tokens_ref,
    routes_ref,
    cos_ref,
    sin_ref,
    wallg_ref,
    doutg_ref,
    dout_ref,
    q_ref,
    k_ref,
    v_ref,
    normed_t_ref,
    attended_t_ref,
    middle_ref,
    mixed_ref,
    gates_ref,
    gate_rows_ref,
    gains_ref,
    wall_ref,
    weights,
    proj,
    attended,
    own_sem,
    piece_sem,
    load_sem,
    ss,
    rs,
    css,
    crs,
    xs,
    xr,
    xcs,
    xcr,
):
    place = Place(n)
    half, me = place.half, place.me
    rank = lax.axis_index("dp")
    helping = dp == 2
    rows, width = tokens_ref.shape
    shard = wall_ref.shape[0]
    q_width, kv_width = q_ref.shape[1], 2 * k_ref.shape[1]
    qkv_width = q_width + kv_width
    near = qkv_width + 128
    edges = (0, q_width, qkv_width, near, near + width)
    pieces = [
        pltpu.make_async_copy(ref, wall_ref.at[:, pl.ds(edges[i], edges[i + 1] - edges[i])], piece_sem.at[i])
        for i, ref in enumerate((w_query_ref, w_kv_ref, w_extra_ref, w_out_ref))
    ]
    for copy in pieces:
        copy.start()
    barrier = pltpu.get_barrier_semaphore()
    for target in (place.right, place.left, place.sibling):
        pl.semaphore_signal(barrier, inc=1, device_id={"expert": target}, device_id_type=MESH)
    if helping:
        pl.semaphore_signal(barrier, inc=1, device_id={"dp": 1 - rank}, device_id_type=MESH)
    pl.semaphore_wait(barrier, 4 if helping else 3)
    for copy in pieces:
        copy.wait()
    started = []

    def begin(copy):
        copy.start()
        started.append(copy)

    alone = 128 * (edges[4] // 128 * 10 // 33)
    shared = (2 * alone, edges[4] - 2 * alone)
    if helping:
        cut_weights = (
            [(pl.multiple_of(rank * alone, 128), alone), shared],
            {0: (pl.multiple_of((1 - rank) * alone, 128), alone)},
        )
    else:
        cut_weights = (column_cuts(edges[4], PARTS), {})
    flows = (
        (wall_ref, wallg_ref, cut_weights, weights),
        (dout_ref, doutg_ref, (column_cuts(width, PARTS), {}), None),
    )

    def block_at(d, k):
        return me if k == 0 else (place.device(-k) if d == 0 else place.device(k))

    def sibling_of(b):
        return b + 1 - 2 * lax.rem(b, 2)

    def spot(a, b, cut, own=False):
        x_ref, o_ref = flows[a][:2]
        return (x_ref if own else o_ref.at[b]).at[:, pl.ds(*cut)]

    def along(a, d, k, q):
        b, cut = block_at(d, k - 1), flows[a][2][0][q]
        target = place.right if d == 0 else place.left
        return remote(spot(a, b, cut, k == 1), spot(a, b, cut), ss.at[a, d, k - 1, q], rs.at[a, d, k - 1, q], target)

    def across(a, d, k, q):
        b, cut = block_at(d, k), flows[a][2][0][q]
        return remote(
            spot(a, b, cut, k == 0), spot(a, b, cut), css.at[a, d, k, q], crs.at[a, d, k, q], place.sibling
        )

    def over(a, d, k, q):
        b, cut = block_at(d, k), flows[a][2][0][q]
        return pltpu.make_async_remote_copy(
            src_ref=spot(a, b, cut),
            dst_ref=spot(a, b, cut),
            send_sem=xs.at[a, d, k, q],
            recv_sem=xr.at[a, d, k, q],
            device_id={"dp": 1 - rank},
            device_id_type=MESH,
        )

    def over_across(a, d, k, q):
        b, cut = block_at(d, k), flows[a][2][1][q]
        return remote(spot(a, b, cut, k == 0), spot(a, b, cut), xcs.at[a, d, k, q], xcr.at[a, d, k, q], place.sibling)

    def take(a, b, cut, own=False):
        local = flows[a][3]
        if local is not None:
            at = pl.ds(pl.multiple_of(b * shard, 16), shard)
            pltpu.make_async_copy(spot(a, b, cut, own), local.at[at, pl.ds(*cut)], load_sem.at[0]).start()

    def first(a):
        parts, others = flows[a][2]
        for q in range(PARTS):
            begin(along(a, 0, 1, q))
            begin(along(a, 1, 1, q))
            begin(across(a, 0, 0, q))
            take(a, me, parts[q], True)
            if q in others:
                begin(over_across(a, 0, 0, q))
                take(a, me, others[q], True)

    def arrive(a, d, k, q):
        parts, others = flows[a][2]
        along(a, d, k, q).wait_recv()
        if k < half and goes(d, k + 1, q, half, PARTS):
            begin(along(a, d, k + 1, q))
        if q in others:
            begin(over(a, d, k, q))
        begin(across(a, d, k, q))
        take(a, block_at(d, k), parts[q])

    def places(k):
        return [
            (d, q)
            for q in range(PARTS)
            for d in (0, 1)
            if (k == 0 and d == 0) or (k > 0 and goes(d, k, q, half, PARTS))
        ]

    def aside(a, k):
        parts, others = flows[a][2]
        for d, q in places(k) if k > 0 else ():
            if q in others:
                b = block_at(d, k)
                piece = spot(a, b, others[q])
                remote(piece, piece, xs.at[a, d, k, q], xr.at[a, d, k, q], place.sibling).wait_recv()
                begin(over_across(a, d, k, q))
                take(a, b, others[q])
        for d, q in places(k):
            b = sibling_of(block_at(d, k))
            piece = spot(a, b, parts[q])
            remote(piece, piece, css.at[a, d, k, q], crs.at[a, d, k, q], place.sibling).wait_recv()
            take(a, b, parts[q])

    def aside_over(a, k):
        others = flows[a][2][1]
        for d, q in places(k):
            if q in others:
                b = sibling_of(block_at(d, k))
                piece = spot(a, b, others[q])
                remote(piece, piece, xcs.at[a, d, k, q], xcr.at[a, d, k, q], place.sibling).wait_recv()
                take(a, b, others[q])

    events, ends = [functools.partial(first, 0)], []
    for a in range(len(flows)):
        for k in range(1, half + 1):
            events += [functools.partial(arrive, a, d, k, q) for d, q in places(k)]
            if k == half - 1 and a + 1 < len(flows):
                events.append(functools.partial(first, a + 1))
            events.append(functools.partial(aside, a, k - 1))
            if k >= 2:
                events.append(functools.partial(aside_over, a, k - 2))
        events.append(functools.partial(aside, a, half))
        events += [functools.partial(aside_over, a, k) for k in (half - 1, half)]
        ends.append(len(events))
    done = [0]

    def pump(last):
        while done[0] < last:
            events[done[0]]()
            done[0] += 1

    own = [
        pltpu.make_async_copy(x_ref, o_ref.at[me], own_sem.at[i])
        for i, (x_ref, o_ref) in enumerate(((wall_ref, wallg_ref), (dout_ref, doutg_ref)))
    ]
    alive = lax.broadcasted_iota(jnp.int32, (rows, width), 0) < lengths_ref[0]
    dout_ref[...] = jnp.where(alive, cotangent_ref[...].astype(f32), 0.0).astype(bf16)
    pump(1)
    for copy in own:
        copy.start()
    pump(ends[0])
    pltpu.make_async_copy(weights, weights, load_sem.at[0]).wait()

    lane = lax.broadcasted_iota(jnp.int32, (rows, 128), 1)
    turned = jnp.transpose(weights[:, pl.ds(qkv_width, 128)].astype(f32))
    gains_ref[...] = jnp.concatenate([turned[n : n + 1], turned[n + 1 : n + 2], jnp.zeros((6, width), f32)], axis=0)
    inputs = tokens_ref[...].astype(f32)
    inv = lax.rsqrt(jnp.mean(inputs * inputs, axis=1, keepdims=True) + EPSILON)
    normed = (inputs * inv * gains_ref[0:1]).astype(bf16)
    proj[...] = mul(normed, weights[:, pl.ds(0, qkv_width)], 1, 0)
    normed_t_ref[...] = jnp.transpose(normed)
    cosine, sine = cos_ref[...], sin_ref[...]
    sine_on = jnp.where(lane % HD < HD // 2, -sine, sine)

    def turn(at):
        block = proj[:, at]
        return (block * cosine + swap_halves(block, lane) * sine_on).astype(bf16)

    for b in range(q_width // 128):
        q_ref[:, pl.ds(128 * b, 128)] = turn(pl.ds(128 * b, 128))
    for b in range(kv_width // 256):
        k_ref[:, pl.ds(128 * b, 128)] = turn(pl.ds(q_width + 128 * b, 128))
    v_ref[...] = proj[:, pl.ds(q_width + kv_width // 2, kv_width // 2)].astype(bf16)
    t_at = lax.broadcasted_iota(jnp.int32, (rows, rows), 0)
    u_at = lax.broadcasted_iota(jnp.int32, (rows, rows), 1)
    causal = t_at >= u_at
    kv_count = k_ref.shape[1] // HD
    per_group = q_width // HD // kv_count
    kept = None
    for g in range(kv_count):
        pair = pl.ds(128 * (g // 2), 128)
        k_parts = head_halves(k_ref[:, pair].astype(f32), lane, g % 2)
        v_parts = head_halves(v_ref[:, pair].astype(f32), lane, g % 2)
        for h in range(per_group * g, per_group * (g + 1)):
            at = pl.ds(128 * (h // 2), 128)
            probs = softmax_rows(q_ref[:, at], k_parts[h % 2], causal).astype(bf16)
            kept_new = mul(probs, v_parts[h % 2], 1, 0)
            if h % 2 == 0:
                kept = kept_new
            else:
                attended[:, at] = (kept + kept_new).astype(bf16)
        pump(ends[0] + 4 * (g + 1) // kv_count)
    attended_t_ref[...] = jnp.transpose(attended[...])
    middle_ref[...] = tokens_ref[...].astype(f32) + mul(attended[...], weights[:, pl.ds(near, width)], 1, 0)
    pump(ends[0] + 6)
    tile = 32

    @pl.loop(0, rows // tile)
    def _(r):
        at = pl.ds(pl.multiple_of(r * tile, tile), tile)
        middle = middle_ref[at]
        scale = lax.rsqrt(jnp.mean(middle * middle, axis=1, keepdims=True) + EPSILON)
        mixed_ref[at] = (middle * scale * gains_ref[1:2]).astype(bf16)

    pump(ends[0] + 8)
    logits = mul(mixed_ref[...], weights[:, pl.ds(qkv_width, 128)], 1, 0)
    chosen = lane == routes_ref[:, 0:1]
    for choice in range(1, routes_ref.shape[1]):
        chosen = jnp.logical_or(chosen, lane == routes_ref[:, choice : choice + 1])
    logits = jnp.where(chosen, logits, -1e30)
    e = jnp.where(chosen, jnp.exp(logits - jnp.max(logits, axis=1, keepdims=True)), 0.0)
    gates = e / jnp.sum(e, axis=1, keepdims=True)
    gates_ref[...] = gates
    across_gates = jnp.transpose(gates)
    for e in range(n):
        gate_rows_ref[e] = jnp.broadcast_to(across_gates[e : e + 1], (8, rows))
    for copy in result_copies:
        copy.start()
    pump(ends[1])
    for copy in result_copies:
        copy.wait()
    for copy in own:
        copy.wait()
    for copy in started:
        copy.wait_send()


def forward(n, dp, w_query, w_kv, w_extra, w_out, lengths, cotangent, tokens, routes, turns, collective_id):
    half = n // 4
    rows, width = tokens.shape
    shard, q_width = w_query.shape
    kv_width = w_kv.shape[1]
    full_width = q_width + kv_width + 128 + width
    shape = jax.ShapeDtypeStruct
    made = [
        shape((rows, width), bf16),
        shape((rows, q_width), bf16),
        shape((rows, kv_width // 2), bf16),
        shape((rows, kv_width // 2), bf16),
        shape((width, rows), bf16),
        shape((q_width, rows), bf16),
        shape((rows, width), f32),
        shape((rows, width), bf16),
        shape((rows, 128), f32),
        shape((n, 8, rows), f32),
        shape((8, width), f32),
    ]
    return pl.pallas_call(
        functools.partial(forward_entry, n, dp, len(made)),
        out_shape=[
            shape((n, shard, full_width), bf16),
            shape((n, rows, width), bf16),
            *made,
        ],
        in_specs=[ANY] * 4 + [pl.BlockSpec(memory_space=pltpu.SMEM)] + [VMEM] * 5,
        out_specs=[ANY] * (2 + len(made)),
        scratch_shapes=[pltpu.VMEM(value.shape, value.dtype) for value in made]
        + [DMA((len(made),))]
        + [
            pltpu.VMEM((shard, full_width), bf16),
            pltpu.VMEM((width, full_width), bf16),
            pltpu.VMEM((rows, q_width + kv_width), f32),
            pltpu.VMEM((rows, q_width), bf16),
            DMA((2,)),
            DMA((4,)),
            DMA((1,)),
            DMA((2, 2, half, PARTS)),
            DMA((2, 2, half, PARTS)),
            DMA((2, 2, half + 1, PARTS)),
            DMA((2, 2, half + 1, PARTS)),
        ]
        + [DMA((1, 2, half + 1, PARTS)) for _ in range(4)],
        compiler_params=pltpu.CompilerParams(
            collective_id=collective_id, has_side_effects=True, vmem_limit_bytes=56 * MB
        ),
    )(w_query, w_kv, w_extra, w_out, lengths, cotangent, tokens, routes, *turns)


SLOTS = 4


def ring_work(half, parts):
    work = []
    for k in range(half, 0, -1):
        for q in range(parts):
            for d in (0, 1):
                if goes(d, k, q, half, parts):
                    work.append((d, k, q))
    return work + [(None, 0, q) for q in range(parts)]


def goes(d, k, q, half, parts):
    return k < half or ((q < parts // 2) == (d == 0))


def widest(width, parts):
    return max(w for _, w in column_cuts(width, parts))


def reduce_scratch(rows, width, half, parts):
    return [
        pltpu.VMEM((2, half, rows, width), bf16),
        pltpu.VMEM((SLOTS, rows, widest(width, parts)), bf16),
        pltpu.VMEM((SLOTS, rows, widest(width, parts)), bf16),
        DMA((SLOTS,)),
        DMA((SLOTS,)),
        DMA((SLOTS,)),
        DMA((2, half, parts)),
    ]


def ring_reduce(place, own_at, other_at, other_wait, width, write, scratch, first=0):
    arrived, mine, theirs, mine_sem, theirs_sem, send_sem, recv_sem = scratch
    half = place.half
    parts = recv_sem.shape[2]
    cuts = column_cuts(width, parts)
    rows = arrived.shape[2]
    tile = 16
    work = ring_work(half, parts)

    def chip_of(d, k):
        return place.chip_at(k if d != 1 else -k)

    def loads(i):
        d, k, q = work[i]
        slot, chip, (start, size) = i % SLOTS, chip_of(d, k), cuts[q]
        return (
            pltpu.make_async_copy(
                own_at(chip).at[:, pl.ds(start, size)], mine.at[slot, :, pl.ds(0, size)], mine_sem.at[slot]
            ),
            pltpu.make_async_copy(
                other_at(chip).at[:, pl.ds(start, size)], theirs.at[slot, :, pl.ds(0, size)], theirs_sem.at[slot]
            ),
        )

    def send(i):
        d, k, q = work[i]
        start, size = cuts[q]
        return remote(
            mine.at[i % SLOTS, :, pl.ds(0, size)],
            arrived.at[d, k - 1, :, pl.ds(start, size)],
            send_sem.at[i % SLOTS],
            recv_sem.at[d, k - 1, q],
            place.right if d == 0 else place.left,
        )

    waited = set()
    fetched = [0]

    def fetch(last):
        while fetched[0] <= min(last, len(work) - 1):
            fetch_one(fetched[0])
            fetched[0] += 1

    def fetch_one(i):
        d, k, q = work[i]
        if i >= SLOTS:
            send(i - SLOTS).wait_send()
        key = (0 if k in (0, half) else d, k)
        if key not in waited:
            waited.add(key)
            other_wait(chip_of(d, k))
        for copy in loads(i):
            copy.start()

    ahead = SLOTS // 2
    for i, (d, k, q) in enumerate(work):
        fetch(i + ahead if i >= first else min(i + ahead, first - 1))
        for copy in loads(i):
            copy.wait()
        start, size = cuts[q]
        slot = i % SLOTS
        come = []
        for dd in (0, 1) if d is None else (d,):
            if k + 1 <= half and goes(dd, k + 1, q, half, parts):
                piece = arrived.at[dd, k, :, pl.ds(start, size)]
                remote(piece, piece, send_sem.at[slot], recv_sem.at[dd, k, q], place.sibling).wait_recv()
                come.append(dd)

        @pl.loop(0, rows // tile)
        def _(r):
            at = pl.ds(pl.multiple_of(r * tile, tile), tile)
            total = mine[slot, at, pl.ds(0, size)].astype(f32) + theirs[slot, at, pl.ds(0, size)].astype(f32)
            for dd in come:
                total += arrived[dd, k, at, pl.ds(start, size)].astype(f32)
            if d is None:
                write(at, pl.ds(start, size), total)
            else:
                mine[slot, at, pl.ds(0, size)] = total.astype(bf16)

        if d is not None:
            send(i).start()
        yield
    sends = len(work) - parts
    for i in range(max(0, len(work) - SLOTS), sends):
        send(i).wait_send()


DENSE_PARTS = 4


def swap_halves(values, lane):
    width = values.shape[1]
    return jnp.where(lane % HD < HD // 2, pltpu.roll(values, width - HD // 2, 1), pltpu.roll(values, HD // 2, 1))


def head_halves(block, lane, low):
    turned = pltpu.roll(block, HD, 1)
    lower, upper = (block, turned) if low == 0 else (turned, block)
    zero = jnp.zeros_like(block)
    return jnp.where(lane < HD, lower, zero).astype(bf16), jnp.where(lane < HD, zero, upper).astype(bf16)


def softmax_rows(q, k, causal):
    scores = jnp.where(causal, mul(q, k, 1, 1) * HD**-0.5, -1e30)
    e = jnp.exp(scores - jnp.max(scores, axis=1, keepdims=True))
    return e * (1.0 / jnp.sum(e, axis=1, keepdims=True))


def backward_entry(n, dp, count, *refs):
    direct, operands = refs[:5], refs[5 : 5 + count]
    results = refs[5 + count : 12 + count]
    held, operand_sem, scratch = refs[12 + count : 12 + 2 * count], refs[12 + 2 * count], refs[13 + 2 * count :]
    copies = [pltpu.make_async_copy(a, b, operand_sem.at[i]) for i, (a, b) in enumerate(zip(operands, held))]
    for copy in copies:
        copy.start()
    backward_kernel(n, dp, copies, *direct, *held, *results, *scratch)


def backward_kernel(
    n,
    dp,
    operand_copies,
    od_ref,
    sd_ref,
    wall_ref,
    ggu_ref,
    gd_ref,
    dmix_ref,
    dgate_ref,
    gates_ref,
    middle_ref,
    mixed_ref,
    dout_ref,
    tokens_ref,
    normed_t_ref,
    attended_t_ref,
    q_ref,
    k_ref,
    v_ref,
    cos_ref,
    sin_ref,
    gains_ref,
    output_ref,
    input_grad_ref,
    dense_ref,
    ggu_sum,
    gd_sum,
    ggu_in,
    gd_in,
    weights,
    extra_w,
    d_middle,
    d_middle_low,
    d_att,
    d_qkv,
    d_normed,
    extra,
    logits_low,
    own_f,
    stage_f,
    other_f,
    come_f,
    copies_f,
    weight_sem,
    stage_sem,
    other_sem,
    send_f,
    recv_f,
    copy_s,
    copy_r,
    expert_s,
    expert_r,
    tile_in,
    tile_out,
    *scratch_d,
):
    place = Place(n)
    half, ring = place.half, place.ring
    rank = lax.axis_index("dp")
    rows, width = middle_ref.shape
    q_width, kv_width = q_ref.shape[1], 2 * k_ref.shape[1]
    qkv_width = q_width + kv_width
    shard = own_f.shape[1]
    full_width = own_f.shape[2]
    barrier = pltpu.get_barrier_semaphore()
    for target in (place.right, place.left, place.sibling):
        pl.semaphore_signal(barrier, inc=1, device_id={"expert": target}, device_id_type=MESH)
    for turn in range(1, dp):
        pl.semaphore_signal(barrier, inc=1, device_id={"dp": lax.rem(rank + turn, dp)}, device_id_type=MESH)
    out_w = pltpu.make_async_copy(
        wall_ref.at[:, pl.ds(qkv_width + 128, width)], weights.at[:, pl.ds(0, width)], weight_sem.at[0]
    )
    extra_copy = pltpu.make_async_copy(wall_ref.at[:, pl.ds(qkv_width, 128)], extra_w, weight_sem.at[1])
    qkv_w = pltpu.make_async_copy(wall_ref.at[:, pl.ds(0, qkv_width)], weights, weight_sem.at[2])
    out_w.start()
    extra_copy.start()
    pl.semaphore_wait(barrier, 3 + dp - 1)

    hidden_width = ggu_ref.shape[1] // 2
    tiles = [(ggu_ref, ggu_in, r) for r in range(0, ggu_ref.shape[0], rows)]
    tiles += [(gd_ref, gd_in, r) for r in range(0, gd_ref.shape[0], rows)]

    def spread_tile(turn, t):
        own, come, r = tiles[t]
        return pltpu.make_async_remote_copy(
            src_ref=own.at[pl.ds(r, rows)],
            dst_ref=come.at[rank, pl.ds(r, rows)],
            send_sem=expert_s.at[turn, t],
            recv_sem=expert_r.at[turn, t],
            device_id={"dp": lax.rem(rank + turn, dp)},
            device_id_type=MESH,
        )

    for t in range(len(tiles)):
        for turn in range(1, dp):
            spread_tile(turn, t).start()

    def write_output(at, columns, total):
        output_ref[at, columns] = (middle_ref[at, columns] + total).astype(bf16)

    background = ring_reduce(
        place, lambda chip: od_ref.at[chip], lambda chip: sd_ref.at[chip], lambda chip: None, width, write_output, scratch_d
    )
    items = len(ring_work(half, scratch_d[6].shape[2]))
    done = [0]

    def pump(share):
        while done[0] < min(items, int(items * share + 0.5)):
            next(background)
            done[0] += 1

    pump(0.06)
    for copy in operand_copies:
        copy.wait()
    d_rows = jnp.concatenate([dgate_ref[:, 0, :], jnp.zeros((128 - n, rows), f32)], axis=0)
    d_gates = jnp.transpose(d_rows)
    gates = gates_ref[...]
    d_sel = gates * (d_gates - jnp.sum(gates * d_gates, axis=1, keepdims=True))
    logits_low[...] = d_sel.astype(bf16)
    extra_copy.wait()
    d_normed[...] = mul(logits_low[...], extra_w[...], 1, 1)
    gain_one, gain_two = gains_ref[0:1], gains_ref[1:2]
    tile = 32

    @pl.loop(0, rows // tile)
    def _(r):
        at = pl.ds(pl.multiple_of(r * tile, tile), tile)
        middle = middle_ref[at]
        d_mixed = dmix_ref[at] + d_normed[at]
        inv = lax.rsqrt(jnp.mean(middle * middle, axis=1, keepdims=True) + EPSILON)
        scaled = d_mixed * gain_two
        back = jnp.mean(scaled * middle, axis=1, keepdims=True)
        total = dout_ref[at].astype(f32) + inv * scaled - middle * (inv * inv * inv * back)
        d_middle[at] = total
        d_middle_low[at] = total.astype(bf16)
        d_att[at] = (d_mixed * middle * inv).astype(bf16)

    lane = lax.broadcasted_iota(jnp.int32, (rows, 128), 1)
    extra[...] = mul(mixed_ref[...], logits_low[...], 0, 0) + mul(
        d_att[...], (lane == n + 1).astype(bf16), 0, 0
    )
    pump(0.12)
    out_w.wait()
    d_att[...] = mul(d_middle_low[...], weights[:, pl.ds(0, width)], 1, 1).astype(bf16)
    qkv_w.start()
    pump(0.18)

    t_at = lax.broadcasted_iota(jnp.int32, (rows, rows), 0)
    u_at = lax.broadcasted_iota(jnp.int32, (rows, rows), 1)
    causal = t_at >= u_at
    cosine, sine = cos_ref[...], sin_ref[...]
    sine_back = jnp.where(lane % HD < HD // 2, sine, -sine)
    kv_count = k_ref.shape[1] // HD
    per_group = q_width // HD // kv_count
    d_normed[...] = jnp.zeros_like(d_normed)
    pair_k, pair_v = None, None
    for g in range(kv_count):
        pair = pl.ds(128 * (g // 2), 128)
        k_parts = head_halves(k_ref[:, pair].astype(f32), lane, g % 2)
        v_parts = head_halves(v_ref[:, pair].astype(f32), lane, g % 2)
        d_k, d_v = [None, None], [None, None]
        for h in range(per_group * g, per_group * (g + 1)):
            at = pl.ds(128 * (h // 2), 128)
            low = h % 2
            query, d_a = q_ref[:, at], d_att[:, at]
            probs = softmax_rows(query, k_parts[low], causal)
            probs_low = probs.astype(bf16)
            d_probs = mul(d_a, v_parts[low], 1, 1)
            weighted = probs * d_probs
            d_scores = (weighted - probs * jnp.sum(weighted, axis=1, keepdims=True)).astype(bf16)
            d_normed[:, at] += mul(d_scores, k_parts[low], 1, 0)
            step_k, step_v = mul(d_scores, query, 0, 0), mul(probs_low, d_a, 0, 0)
            d_k[low] = step_k if d_k[low] is None else d_k[low] + step_k
            d_v[low] = step_v if d_v[low] is None else d_v[low] + step_v

        def gathered(parts):
            stay, turn = parts[g % 2], parts[1 - g % 2]
            return stay if turn is None else (pltpu.roll(turn, HD, 1) if stay is None else stay + pltpu.roll(turn, HD, 1))

        if g % 2 == 0:
            pair_k, pair_v = gathered(d_k), gathered(d_v)
        if g % 2 == 1 or g + 1 == kv_count:
            total_k = jnp.where(lane < HD, pair_k, gathered(d_k)) * HD**-0.5
            total_v = jnp.where(lane < HD, pair_v, gathered(d_v))
            turned = total_k * cosine + swap_halves(total_k, lane) * sine_back
            d_qkv[:, pl.ds(q_width + 128 * (g // 2), 128)] = turned.astype(bf16)
            d_qkv[:, pl.ds(q_width + kv_width // 2 + 128 * (g // 2), 128)] = total_v.astype(bf16)
        pump(0.18 + 0.3 * (g + 1) / kv_count)
    for b in range(q_width // 128):
        at = pl.ds(128 * b, 128)
        total = d_normed[:, at] * HD**-0.5
        d_qkv[:, at] = (total * cosine + swap_halves(total, lane) * sine_back).astype(bf16)
    pump(0.53)
    qkv_w.wait()
    d_normed[...] = mul(d_qkv[...], weights[...], 1, 1)

    @pl.loop(0, rows // tile)
    def _(r):
        at = pl.ds(pl.multiple_of(r * tile, tile), tile)
        inputs = tokens_ref[at].astype(f32)
        d = d_normed[at]
        inv = lax.rsqrt(jnp.mean(inputs * inputs, axis=1, keepdims=True) + EPSILON)
        scaled = d * gain_one
        back = jnp.mean(scaled * inputs, axis=1, keepdims=True)
        total = d_middle[at] + inv * scaled - inputs * (inv * inv * inv * back)
        input_grad_ref[at] = total.astype(bf16)
        d_att[at] = (d * inputs * inv).astype(bf16)

    extra[...] += mul(d_att[...], (lane == n).astype(bf16), 0, 0)
    pump(0.66)

    def cross(chip, slot):
        return remote(stage_f.at[slot], other_f.at[chip], stage_sem.at[slot], other_sem.at[chip], place.sibling)

    def fill(ref, device):
        at = pl.ds(pl.multiple_of(device * shard, 16), shard)
        ref[:, pl.ds(0, qkv_width)] = mul(normed_t_ref[at], d_qkv[...], 1, 0).astype(bf16)
        ref[:, pl.ds(qkv_width, 128)] = extra[at].astype(bf16)
        ref[:, pl.ds(qkv_width + 128, width)] = mul(attended_t_ref[at], d_middle_low[...], 1, 0).astype(bf16)

    for k in range(half, -1, -1):
        @pl.loop(max(0, 2 * (half - k) - 1), min(ring, 2 * (half - k) + 1))
        def _(i):
            away = half - lax.div(i + 1, 2)
            chip = place.chip_at(jnp.where(lax.rem(i, 2) == 0, away, -away))
            slot = lax.rem(i, 2)

            @pl.when(i >= 2)
            def _():
                cross(chip, slot).wait_send()

            fill(stage_f.at[slot], chip * 2 + 1 - place.core)
            cross(chip, slot).start()
            fill(own_f.at[chip], chip * 2 + place.core)

        pump(1.0 - 0.34 * k / (half + 1))

    for _ in background:
        pass
    for slot in range(2):
        cross(place.chip, slot).wait_send()
    cuts = column_cuts(full_width, DENSE_PARTS)
    work = ring_work(half, DENSE_PARTS)

    def send(d, k, q):
        chip = place.chip_at(k if d == 0 else -k)
        at = pl.ds(*cuts[q])
        return remote(
            own_f.at[chip, :, at],
            come_f.at[d, k - 1, :, at],
            send_f.at[d, k - 1, q],
            recv_f.at[d, k - 1, q],
            place.right if d == 0 else place.left,
        )

    def spread(turn, q):
        at = pl.ds(*cuts[q])
        return pltpu.make_async_remote_copy(
            src_ref=copies_f.at[rank, :, at],
            dst_ref=copies_f.at[rank, :, at],
            send_sem=copy_s.at[turn, q],
            recv_sem=copy_r.at[turn, q],
            device_id={"dp": lax.rem(rank + turn, dp)},
            device_id_type=MESH,
        )

    lanes = 2 if 2 * dp <= weights.shape[0] // rows else 1

    def tile_loads(t):
        own, come, r = tiles[t]
        size = own.shape[1]
        for source in range(dp):
            band = weights.at[pl.ds(((t % lanes) * dp + source) * rows, rows), pl.ds(0, size)]

            @pl.when(rank == source)
            def _():
                pltpu.make_async_copy(own.at[pl.ds(r, rows)], band, tile_in.at[t % lanes, source]).start()

            @pl.when(rank != source)
            def _():
                pltpu.make_async_copy(come.at[source, pl.ds(r, rows)], band, tile_in.at[t % lanes, source]).start()

    def tile_put(t):
        own, _, r = tiles[t]
        held = (d_att, d_middle_low)[t % 2].at[:, pl.ds(0, own.shape[1])]
        to = gd_sum if own is gd_ref else ggu_sum
        return pltpu.make_async_copy(held, to.at[pl.ds(r, rows)], tile_out.at[t % 2])

    def tile_here(t):
        for turn in range(1, dp):
            spread_tile(turn, t).wait_recv()
        tile_loads(t)

    def tile_sum(t):
        own, _, r = tiles[t]
        size = own.shape[1]
        held = (d_att, d_middle_low)[t % 2]
        for source in range(dp):
            band = weights.at[pl.ds(((t % lanes) * dp + source) * rows, rows), pl.ds(0, size)]
            pltpu.make_async_copy(band, band, tile_in.at[t % lanes, source]).wait()
        if t >= 2:
            tile_put(t - 2).wait()

        @pl.loop(0, rows // tile)
        def _(i):
            total = None
            for source in range(dp):
                at = pl.ds(pl.multiple_of(((t % lanes) * dp + source) * rows + i * tile, tile), tile)
                value = weights[at, pl.ds(0, size)].astype(f32)
                total = value if total is None else total + value
            held[pl.ds(pl.multiple_of(i * tile, tile), tile), pl.ds(0, size)] = total.astype(bf16)

        tile_put(t).start()

    def tile_step(t):
        if lanes == 2 and t < len(tiles):
            tile_here(t)
        if t >= 1:
            tile_sum(t - 1)
        if lanes == 1 and t < len(tiles):
            tile_here(t)

    moves = len(work) - DENSE_PARTS
    when = {moves * (t + 2) // (len(tiles) + 2): t for t in range(len(tiles) + 1)}
    met = set()
    for index, (d, k, q) in enumerate(work):
        if index in when:
            tile_step(when[index])
        chip = place.chip_at(0 if d is None else (k if d == 0 else -k))
        key = (0 if k in (0, half) else d, k)
        if key not in met:
            met.add(key)
            remote(other_f.at[chip], other_f.at[chip], stage_sem.at[0], other_sem.at[chip], place.sibling).wait_recv()
        at = pl.ds(*cuts[q])
        total = own_f[chip, :, at].astype(f32) + other_f[chip, :, at].astype(f32)
        for dd in (0, 1) if d is None else (d,):
            if k + 1 <= half and goes(dd, k + 1, q, half, DENSE_PARTS):
                piece = come_f.at[dd, k, :, at]
                remote(piece, piece, send_f.at[dd, k, q], recv_f.at[dd, k, q], place.sibling).wait_recv()
                total += piece[...].astype(f32)
        if d is not None:
            own_f[chip, :, at] = total.astype(bf16)
            send(d, k, q).start()
        else:
            copies_f[rank, :, at] = total.astype(bf16)
            for turn in range(1, dp):
                spread(turn, q).start()
    for t in range(len(tiles) - 2, len(tiles)):
        tile_put(t).wait()
    for q in range(DENSE_PARTS):
        for turn in range(1, dp):
            spread(turn, q).wait()
    total = copies_f[0].astype(f32)
    for r in range(1, dp):
        total += copies_f[r].astype(f32)
    dense_ref[...] = total.astype(bf16)
    for t in range(len(tiles)):
        for turn in range(1, dp):
            spread_tile(turn, t).wait_send()
    for d, k, q in work:
        if d is not None:
            send(d, k, q).wait_send()


def backward(n, dp, own_d, other_d, wall, grad_gu, grad_down, others, collective_id):
    half, ring = n // 4, n // 2
    rows, width = own_d.shape[1:]
    full_width = wall.shape[1]
    qkv_width = full_width - width - 128
    shard = wall.shape[0] // n
    q_width = others[9].shape[1]
    return pl.pallas_call(
        functools.partial(backward_entry, n, dp, len(others)),
        out_shape=[
            jax.ShapeDtypeStruct((rows, width), bf16),
            jax.ShapeDtypeStruct((rows, width), bf16),
            jax.ShapeDtypeStruct((shard, full_width), bf16),
            jax.ShapeDtypeStruct(grad_gu.shape, bf16),
            jax.ShapeDtypeStruct(grad_down.shape, bf16),
            jax.ShapeDtypeStruct((dp,) + grad_gu.shape, bf16),
            jax.ShapeDtypeStruct((dp,) + grad_down.shape, bf16),
        ],
        in_specs=[ANY] * (5 + len(others)),
        out_specs=[VMEM] * 3 + [ANY] * 4,
        scratch_shapes=[pltpu.VMEM(value.shape, value.dtype) for value in others]
        + [DMA((len(others),))]
        + [
            pltpu.VMEM((width, qkv_width), bf16),
            pltpu.VMEM((width, 128), bf16),
            pltpu.VMEM((rows, width), f32),
            pltpu.VMEM((rows, width), bf16),
            pltpu.VMEM((rows, q_width), bf16),
            pltpu.VMEM((rows, qkv_width), bf16),
            pltpu.VMEM((rows, width), f32),
            pltpu.VMEM((width, 128), f32),
            pltpu.VMEM((rows, 128), bf16),
            pltpu.VMEM((ring, shard, full_width), bf16),
            pltpu.VMEM((2, shard, full_width), bf16),
            pltpu.VMEM((ring, shard, full_width), bf16),
            pltpu.VMEM((2, half, shard, full_width), bf16),
            pltpu.VMEM((dp, shard, full_width), bf16),
            DMA((3,)),
            DMA((2,)),
            DMA((ring,)),
            DMA((2, half, DENSE_PARTS)),
            DMA((2, half, DENSE_PARTS)),
            DMA((dp, DENSE_PARTS)),
            DMA((dp, DENSE_PARTS)),
            DMA((dp, (width + grad_down.shape[0]) // rows)),
            DMA((dp, (width + grad_down.shape[0]) // rows)),
            DMA((2, dp)),
            DMA((2,)),
        ]
        + reduce_scratch(rows, width, half, 2),
        compiler_params=pltpu.CompilerParams(
            collective_id=collective_id, has_side_effects=True, vmem_limit_bytes=63 * MB
        ),
    )(own_d, other_d, wall, grad_gu, grad_down, *others)[:5]


def finish_kernel(
    experts_n, output_in, grad_in, dense_in, gu_in, down_in, output, grad, q, kv, out, router, one, two, gate, up, down
):
    output[...] = output_in[...]
    grad[...] = grad_in[...]
    hidden_width = gate.shape[1]
    gate[...] = gu_in[:, pl.ds(0, hidden_width)].astype(f32)
    up[...] = gu_in[:, pl.ds(hidden_width, hidden_width)].astype(f32)
    down[...] = down_in[...].astype(f32)

    @pl.when(pl.program_id(0) == 0)
    def _():
        start = 0
        for ref in (q, kv):
            ref[...] = dense_in[:, pl.ds(start, ref.shape[1])].astype(f32)
            start += ref.shape[1]
        extra = dense_in[:, pl.ds(start, 128)].astype(f32)
        router[...] = extra[:, :experts_n]
        turned = jnp.transpose(extra)
        one[...] = turned[experts_n : experts_n + 1]
        two[...] = turned[experts_n + 1 : experts_n + 2]
        out[...] = dense_in[:, pl.ds(start + 128, out.shape[1])].astype(f32)


def finish(output, grad, dense, gu, down, experts_n, q_width, kv_width):
    steps = 4
    rows, width = output.shape
    shard = dense.shape[0]
    hidden_width = gu.shape[1] // 2

    def tiles(a, b):
        return pl.BlockSpec((a // steps, b), lambda i: (i, 0))

    def whole(a, b):
        return pl.BlockSpec((a, b), lambda i: (0, 0))

    shape = jax.ShapeDtypeStruct
    return pl.pallas_call(
        functools.partial(finish_kernel, experts_n),
        grid=(steps,),
        in_specs=[
            tiles(rows, width),
            tiles(rows, width),
            whole(*dense.shape),
            tiles(*gu.shape),
            tiles(*down.shape),
        ],
        out_specs=[
            tiles(rows, width),
            tiles(rows, width),
            whole(shard, q_width),
            whole(shard, kv_width),
            whole(shard, width),
            whole(shard, experts_n),
            whole(1, shard),
            whole(1, shard),
            tiles(gu.shape[0], hidden_width),
            tiles(gu.shape[0], hidden_width),
            tiles(*down.shape),
        ],
        out_shape=[
            shape((rows, width), bf16),
            shape((rows, width), bf16),
            shape((shard, q_width), f32),
            shape((shard, kv_width), f32),
            shape((shard, width), f32),
            shape((shard, experts_n), f32),
            shape((1, shard), f32),
            shape((1, shard), f32),
            shape((gu.shape[0], hidden_width), f32),
            shape((gu.shape[0], hidden_width), f32),
            shape(down.shape, f32),
        ],
        compiler_params=pltpu.CompilerParams(vmem_limit_bytes=63 * MB),
    )(output, grad, dense, gu, down)


QUARTERS = 4


def expert_kernel(
    n,
    x_ref,
    dog_ref,
    gates_ref,
    gate_any,
    up_any,
    wd_any,
    de_ref,
    dgates_ref,
    ggu_out,
    gd_out,
    od_ref,
    sd_ref,
    oe_ref,
    se_ref,
    xg_ref,
    hg_ref,
    wgu_ref,
    wd_ref,
    ggu_ref,
    gd_ref,
    acc_gu,
    acc_d,
    gate_in,
    dgate_out,
    xbuf,
    dobuf,
    pd,
    pe,
    hbuf,
    own_sem,
    weight_sem,
    ring_s,
    ring_r,
    cross_s,
    cross_r,
    load_sem,
    put_sem,
    sib_r,
    gate_s,
    gate_r,
    dgate_s,
    dgate_r,
    *reduce_refs,
):
    place = Place(n)
    half, ring, me = place.half, place.ring, place.me
    rows, width = x_ref.shape
    hidden_width = wd_ref.shape[0]
    piece = rows // QUARTERS
    weight_copies = [
        pltpu.make_async_copy(gate_any, wgu_ref.at[:, pl.ds(0, hidden_width)], weight_sem.at[0]),
        pltpu.make_async_copy(up_any, wgu_ref.at[:, pl.ds(hidden_width, hidden_width)], weight_sem.at[1]),
        pltpu.make_async_copy(wd_any, wd_ref, weight_sem.at[2]),
    ]
    for copy in weight_copies:
        copy.start()
    pltpu.make_async_copy(x_ref, xbuf.at[0], load_sem.at[0, 0]).start()
    pltpu.make_async_copy(dog_ref.at[me], dobuf.at[0], load_sem.at[1, 0]).start()
    meet_all(place)

    own = pltpu.make_async_copy(xbuf.at[0], xg_ref.at[me], own_sem.at[0])

    def at(q):
        return pl.ds(pl.multiple_of(q * piece, piece), piece)

    def block_of(d, k):
        return jnp.where(d == 0, place.device(-k), place.device(k))

    def along(d, k, q, first=False):
        b = me if first else block_of(d, k - 1)
        return remote(
            x_ref.at[at(q)] if first else xg_ref.at[b, at(q)],
            xg_ref.at[b, at(q)],
            ring_s.at[d, k - 1, q],
            ring_r.at[d, k - 1, q],
            jnp.where(d == 0, place.right, place.left),
        )

    def across(d, k, q, first=False):
        b = me if first else block_of(d, k)
        src = x_ref.at[at(q)] if first else xg_ref.at[b, at(q)]
        return remote(src, xg_ref.at[b, at(q)], cross_s.at[d, k, q], cross_r.at[d, k, q], place.sibling)

    def gate_copy(d):
        to = lax.rem(me + d, n)
        return remote(gates_ref.at[to], gate_in.at[me], gate_s.at[d], gate_r.at[d], to)

    for q in range(QUARTERS):
        for d in (0, 1):
            along(d, 1, q, first=True).start()
        across(0, 0, q, first=True).start()

    @pl.loop(1, n)
    def _(d):
        gate_copy(d).start()

    gate_in[me] = gates_ref[me]
    acc_gu[...] = jnp.zeros_like(acc_gu)
    acc_d[...] = jnp.zeros_like(acc_d)

    def step_of(i):
        late = jnp.where(i < n - 4, i, jnp.where(i < n - 2, i + 2, i - 2))
        k = jnp.where(late < 2, 0, lax.div(late + 2, 4))
        j = jnp.where(late < 2, late, lax.rem(late + 2, 4))
        edge = jnp.logical_or(k == 0, k == half)
        d = jnp.where(edge, 0, lax.rem(j, 2))
        other = jnp.where(edge, j, lax.div(j, 2))
        chip = jnp.where(d == 0, place.chip_at(-k), place.chip_at(k))
        core = jnp.where(other == 0, place.core, 1 - place.core)
        return k, j, d, other, chip, chip * 2 + core

    def pump(d, k, q, last=False):
        along(d, k, q).wait_recv()
        if not last:
            near = jnp.where(q < QUARTERS // 2, 0, 1) == d

            @pl.when(jnp.logical_or(k + 1 < half, near))
            def _():
                along(d, k + 1, q).start()

        across(d, k, q).start()

    def load(block, slot):
        return (
            pltpu.make_async_copy(xg_ref.at[block], xbuf.at[slot], load_sem.at[0, slot]),
            pltpu.make_async_copy(dog_ref.at[block], dobuf.at[slot], load_sem.at[1, slot]),
        )

    def put_wait(slot):
        for which, buf in enumerate((pd, pe, hbuf)):
            pltpu.make_async_copy(buf.at[slot], buf.at[slot], put_sem.at[which, slot]).wait()

    def dgate_copy(block):
        d = lax.rem(block - me + n, n)
        return remote(dgate_out.at[block], dgates_ref.at[me], dgate_s.at[d], dgate_r.at[d], block)

    def load_rest(block, slot):
        return (
            pltpu.make_async_copy(xg_ref.at[block], xbuf.at[slot], load_sem.at[0, slot]),
            pltpu.make_async_copy(dog_ref.at[block], dobuf.at[slot], load_sem.at[1, slot]),
            pltpu.make_async_copy(hg_ref.at[block], hbuf.at[slot], load_sem.at[2, slot]),
        )

    for copy in weight_copies:
        copy.wait()

    def work_on(i):
        k, j, d, other, chip, block = step_of(i)
        slot = lax.rem(i, 2)
        for copy in load(block, slot):
            copy.wait()

        @pl.when(i == 0)
        def _():
            own.start()

        @pl.when(i > 0)
        def _():
            away = lax.rem(me - block + n, n)
            remote(gate_in.at[block], gate_in.at[block], gate_s.at[away], gate_r.at[away], place.sibling).wait_recv()

        nk, nj, nd, nother, nchip, nblock = step_of(i + 1)

        def fetch_next():
            @pl.when(nother == 1)
            def _():
                for q in range(QUARTERS):
                    dd = jnp.where(nk == half, 0 if q < QUARTERS // 2 else 1, nd)
                    piece = xg_ref.at[nblock, at(q)]
                    remote(piece, piece, cross_s.at[dd, nk, q], cross_r.at[dd, nk, q], place.sibling).wait_recv()

            for copy in load(nblock, 1 - slot):
                copy.start()

        early = jnp.logical_and(jnp.logical_and(i > 0, i + 1 < n), nk == k)

        @pl.when(early)
        def _():
            fetch_next()

        @pl.when(jnp.logical_and(i >= 2, i < n - 2))
        def _():
            put_wait(slot)

        gate = jnp.transpose(gate_in[block])[:, :1]
        gu = mul(xbuf[slot], wgu_ref[...], 1, 0)
        dh = mul(dobuf[slot], wd_ref[...], 1, 1)
        g, u = gu[:, :hidden_width], gu[:, hidden_width:]
        s = 1.0 / (1.0 + jnp.exp(-g))
        gs = g * s
        hid = gs * u
        dgate = jnp.sum(dh * hid, axis=1, keepdims=True)
        dgate_out[block] = jnp.transpose(jnp.broadcast_to(dgate, (rows, 128)))[:8]
        dh = dh * gate
        hbuf[slot, :, pl.ds(0, hidden_width)] = (dh * u * s * (1.0 + g * (1.0 - s))).astype(bf16)
        hbuf[slot, :, pl.ds(hidden_width, hidden_width)] = (dh * gs).astype(bf16)
        hbuf[slot, :, pl.ds(2 * hidden_width, hidden_width)] = (hid * gate).astype(bf16)
        pltpu.make_async_copy(hbuf.at[slot], hg_ref.at[block], put_sem.at[2, slot]).start()

        @pl.when(i < 2)
        def _():
            for t in range(2):
                for dd in (0, 1):
                    pump(dd, 1, i * 2 + t)

        @pl.when(jnp.logical_and(i >= 2, k + 1 < half))
        def _():
            for dd in (0, 1):
                pump(dd, k + 1, j)

        @pl.when(jnp.logical_and(k + 1 == half, j < 2))
        def _():
            for dd in (0, 1):
                pump(dd, half, j + dd * (QUARTERS // 2), last=True)

        @pl.when(i == 0)
        def _():
            own.wait()

        @pl.when(jnp.logical_and(i + 1 < n, jnp.logical_not(early)))
        def _():
            fetch_next()

        pd[slot] = mul(hbuf[slot, :, pl.ds(2 * hidden_width, hidden_width)], wd_ref[...], 1, 0).astype(bf16)
        pe[slot] = mul(hbuf[slot, :, pl.ds(0, 2 * hidden_width)], wgu_ref[...], 1, 1).astype(bf16)

        @pl.when(i > 0)
        def _():
            dgate_copy(block).start()

        @pl.when(i == 0)
        def _():
            dgates_ref[me] = dgate_out[me]

        @pl.when(other == 0)
        def _():
            pltpu.make_async_copy(pd.at[slot], od_ref.at[chip], put_sem.at[0, slot]).start()
            pltpu.make_async_copy(pe.at[slot], oe_ref.at[chip], put_sem.at[1, slot]).start()

        @pl.when(other == 1)
        def _():
            remote(pd.at[slot], sd_ref.at[chip], put_sem.at[0, slot], sib_r.at[0, chip], place.sibling).start()
            remote(pe.at[slot], se_ref.at[chip], put_sem.at[1, slot], sib_r.at[1, chip], place.sibling).start()

    @pl.loop(0, n - 2)
    def _(i):
        work_on(i)

    put_wait(0)
    put_wait(1)

    def other_wait(chip):
        remote(se_ref.at[chip], se_ref.at[chip], put_sem.at[1, 0], sib_r.at[1, chip], place.sibling).wait_recv()

    def write(at, columns, total):
        de_ref[at, columns] = total

    back = ring_reduce(
        place, lambda chip: oe_ref.at[chip], lambda chip: se_ref.at[chip], other_wait, width, write, reduce_refs, 2
    )
    next(back)
    next(back)

    @pl.loop(n - 2, n)
    def _(i):
        work_on(i)

    put_wait(0)
    put_wait(1)

    for copy in load_rest(0, 0):
        copy.start()

    def gradients(first, last):
        @pl.loop(first, last)
        def _(b):
            slot = lax.rem(b, 2)
            for copy in load_rest(b, slot):
                copy.wait()

            @pl.when(b + 1 < n)
            def _():
                for copy in load_rest(b + 1, 1 - slot):
                    copy.start()

            acc_gu[...] += mul(xbuf[slot], hbuf[slot, :, pl.ds(0, 2 * hidden_width)], 0, 0)
            acc_d[...] += mul(hbuf[slot, :, pl.ds(2 * hidden_width, hidden_width)], dobuf[slot], 0, 0)

    steps = len(ring_work(half, 2)) // 2 - 2
    for step in range(steps):
        next(back)
        next(back)
        gradients(n * step // steps, n * (step + 1) // steps)
    ggu_ref[...] = acc_gu[...].astype(bf16)
    gd_ref[...] = acc_d[...].astype(bf16)
    out_copies = [
        pltpu.make_async_copy(ggu_ref, ggu_out, weight_sem.at[0]),
        pltpu.make_async_copy(gd_ref, gd_out, weight_sem.at[1]),
    ]
    for copy in out_copies:
        copy.start()
    for _ in back:
        pass
    for copy in out_copies:
        copy.wait()

    @pl.loop(0, ring)
    def _(chip):
        remote(sd_ref.at[chip], sd_ref.at[chip], put_sem.at[0, 0], sib_r.at[0, chip], place.sibling).wait_recv()

    @pl.loop(1, n)
    def _(d):
        gate_copy(d).wait_send()
        source = lax.rem(me - d + n, n)
        remote(dgates_ref.at[source], dgates_ref.at[source], dgate_s.at[d], dgate_r.at[d], place.sibling).wait()

    for q in range(QUARTERS):
        across(0, 0, q, first=True).wait_send()
        for d in (0, 1):
            for k in range(1, half + 1):
                if k < half or ((q < QUARTERS // 2) == (d == 0)):
                    along(d, k, q).wait_send()
                    across(d, k, q).wait_send()


def experts(n, mixed_in, d_gathered, gate_rows, gate_w, up_w, wd, collective_id):
    half, ring = n // 4, n // 2
    rows, width = mixed_in.shape
    blocks = jax.ShapeDtypeStruct((ring, rows, width), bf16)
    hidden_width = wd.shape[0]
    both = (width, 2 * hidden_width)
    out = pl.pallas_call(
        functools.partial(expert_kernel, n),
        out_shape=[
            jax.ShapeDtypeStruct((rows, width), f32),
            jax.ShapeDtypeStruct((n, 8, rows), f32),
            jax.ShapeDtypeStruct(both, bf16),
            jax.ShapeDtypeStruct(wd.shape, bf16),
            blocks,
            blocks,
            blocks,
            blocks,
            jax.ShapeDtypeStruct((n, rows, width), bf16),
            jax.ShapeDtypeStruct((n, rows, 3 * hidden_width), bf16),
        ],
        in_specs=[ANY, ANY, VMEM, ANY, ANY, ANY],
        out_specs=[VMEM, VMEM] + [ANY] * 8,
        scratch_shapes=[
            pltpu.VMEM(both, bf16),
            pltpu.VMEM(wd.shape, bf16),
            pltpu.VMEM(both, bf16),
            pltpu.VMEM(wd.shape, bf16),
            pltpu.VMEM(both, f32),
            pltpu.VMEM(wd.shape, f32),
            pltpu.VMEM((n, 8, rows), f32),
            pltpu.VMEM((n, 8, rows), f32),
            pltpu.VMEM((2, rows, width), bf16),
            pltpu.VMEM((2, rows, width), bf16),
            pltpu.VMEM((2, rows, width), bf16),
            pltpu.VMEM((2, rows, width), bf16),
            pltpu.VMEM((2, rows, 3 * hidden_width), bf16),
            DMA((1,)),
            DMA((3,)),
            DMA((2, half, QUARTERS)),
            DMA((2, half, QUARTERS)),
            DMA((2, half + 1, QUARTERS)),
            DMA((2, half + 1, QUARTERS)),
            DMA((3, 2)),
            DMA((3, 2)),
            DMA((2, ring)),
            DMA((n,)),
            DMA((n,)),
            DMA((n,)),
            DMA((n,)),
        ]
        + reduce_scratch(rows, width, half, 2),
        compiler_params=pltpu.CompilerParams(
            collective_id=collective_id, has_side_effects=True, vmem_limit_bytes=62 * MB
        ),
    )(mixed_in, d_gathered, gate_rows, gate_w, up_w, wd)
    return out[:6]


def rope_tables(length):
    inverse = np.float32(10000.0) ** (-np.arange(HD // 2, dtype=np.float32) / np.float32(HD // 2))
    angles = np.arange(length, dtype=np.float32)[:, None] * inverse.astype(np.float32)[None, :]
    return [np.tile(table(angles).astype(np.float32), (1, 4)) for table in (np.cos, np.sin)]


def per_device(
    n,
    dp,
    tokens,
    cotangent,
    lengths,
    routes,
    norm1_gain,
    w_query,
    w_kv,
    w_out,
    norm2_gain,
    w_router,
    expert_gate,
    expert_up,
    expert_down,
):
    tok_rows, model_width = tokens.shape
    expert_count = w_router.shape[1]
    kv_width, q_width = w_kv.shape[1], w_query.shape[1]
    shard = w_query.shape[0]
    extra = jnp.concatenate(
        [
            w_router,
            norm1_gain[:, None],
            norm2_gain[:, None],
            jnp.zeros((shard, 128 - expert_count - 2), bf16),
        ],
        axis=1,
    )
    turns = rope_tables(tok_rows)
    (
        wall,
        d_gathered,
        d_out_low,
        queries,
        keys,
        values,
        normed_t,
        attended_t,
        middle,
        mixed_in,
        gates,
        gate_rows,
        gains,
    ) = forward(n, dp, w_query, w_kv, extra, w_out, lengths, cotangent, tokens, routes, turns, 0)
    wall = wall.reshape(-1, wall.shape[-1])
    d_mixed_experts, d_gate_rows, grad_gu, grad_down, own_d, other_d = experts(
        n, mixed_in, d_gathered, gate_rows, expert_gate[0], expert_up[0], expert_down[0], 1
    )

    sums = backward(
        n,
        dp,
        own_d,
        other_d,
        wall,
        grad_gu,
        grad_down,
        (
            d_mixed_experts,
            d_gate_rows,
            gates,
            middle,
            mixed_in,
            d_out_low,
            tokens,
            normed_t,
            attended_t,
            queries,
            keys,
            values,
            *turns,
            gains,
        ),
        2,
    )
    output, input_grad, grad_q, grad_kv, grad_out, router, gain_one, gain_two, gate, up, down = finish(
        *sums, expert_count, q_width, kv_width
    )
    return (
        output,
        input_grad,
        gain_one.reshape(-1),
        grad_q,
        grad_kv,
        grad_out,
        gain_two.reshape(-1),
        router,
        gate[None],
        up[None],
        down[None],
    )


def solution(mesh):
    rows, own = P(("dp", "expert"), None), P("expert", None)
    expert = P("expert", None, None)
    return jax.shard_map(
        functools.partial(per_device, mesh.shape["expert"], mesh.shape["dp"]),
        mesh=mesh,
        in_specs=(rows, rows, P(("dp", "expert")), rows, P("expert"), own, own, own, P("expert"), own)
        + (expert,) * 3,
        out_specs=(rows, rows, P("expert"), own, own, own, P("expert"), own) + (expert,) * 3,
        check_vma=False,
    )
```
